256 devices in a mesh: rows: 16 (over z_lo, x, core), cols: 16 (over z_hi, y).
Axes of the slice: x: 4, y: 4, z: 8 (z_hi: 4, z_lo: 2; z = z_hi * 2 + z_lo), core: 2. Of those that a mesh axis runs over, the one named last changes fastest.
Arguments:
- tensor: float32 [192, 512, 512], P('rows', 'cols'), may hold values from 0 to 1
- first_factor: float32 [192, 256], P('rows', 'cols'), may hold values from -2.5 to 2.5
- second_factor: float32 [512, 256], P('cols', 'rows'), may hold values from -2.5 to 2.5
- third_factor: float32 [512, 256], P(('rows', 'cols')), may hold values from -2.5 to 2.5
Outputs:
- first_new: float32 [192, 256], P('rows', 'cols')
- second_new: float32 [512, 256], P('cols', 'rows')
- third_new: float32 [512, 256], P(('rows', 'cols'))
The draws below stay inside these ranges and needn't reach their ends.
All inputs are finite; a program needn't handle non-finite values.
Results may differ from the reference program's by a relative error of at most 0.0003.
Values sent between devices are 32-bit elements; how exact they have to be, the bound alone decides.
No kernel may reach another device: no remote copies, remote signals or barrier semaphores. Data moves between devices by JAX's collectives and lax.ppermute only.
A program may use at most 64 MiB of HBM per device.

```python
import jax
import jax.numpy as jnp
from jax import lax

RANK = 256
K = 512
I_DEV = 12
J_DEV = 32
STEPS = 2
I = 192
J = 512
N_ROWS = 16
N_COLS = 16


def shard_levels(own_key, shape, shards, least, high):
    def one(position, parts):
        draws = jax.random.uniform(jax.random.fold_in(jax.random.fold_in(own_key, 6), position), (parts,), jnp.float32, least / len(shards), high / len(shards))
        return jnp.repeat(jnp.exp(draws), shape[position] // parts).reshape((-1,) + (1,) * (len(shape) - position - 1))

    level = one(*shards[0])
    for cut in shards[1:]:
        level = level * one(*cut)
    return level


def noise(key, extent, deviation, limit, shards=(), kind=jnp.bfloat16):
    values = deviation * jax.random.normal(key, extent, jnp.float32)
    if shards:
        values = values * shard_levels(key, extent, shards, -0.22, 0.18)
    return jnp.clip(values, -limit, limit).astype(kind)


def setup_inputs(seed: int = 0) -> dict:
    splits = jax.random.split(jax.random.key(seed), 5)
    return {
        "tensor": jnp.clip(1.0 * jax.random.uniform(splits[0], (I, J, K), jnp.float32) ** shard_levels(splits[0], (I, J, K), ((0, 16), (1, 16)), -0.2, 0.2), 0.0, 1.0),
        "first_factor": noise(splits[1], (I, RANK), 0.4, 2.5, ((0, 16), (1, 16)), jnp.float32),
        "second_factor": noise(splits[2], (J, RANK), 0.4, 2.5, ((0, 16), (1, 16)), jnp.float32),
        "third_factor": noise(splits[3], (K, RANK), 0.4, 2.5, ((0, 256),), jnp.float32),
    }


def reference(tensor, first_factor, second_factor, third_factor):
    high = lax.Precision.HIGHEST
    size_i = I_DEV * N_ROWS
    size_j = J_DEV * N_COLS
    blocks = tensor.reshape(N_ROWS, I_DEV, size_j, K)
    factor_a, factor_b, factor_c = (first_factor, second_factor, third_factor)
    for step_index in range(STEPS):

        def one_block(carry, inputs):
            grad_b, grad_c = carry
            tile, rows_a = inputs
            khatri = (rows_a[:, None, :] * factor_b[None, :, :]).reshape(-1, RANK)
            model_tile = jnp.dot(khatri, factor_c.T, precision=high, preferred_element_type=jnp.float32)
            deriv = jax.nn.sigmoid(model_tile) - tile.reshape(-1, K)
            deriv_c = jnp.dot(deriv, factor_c, precision=high, preferred_element_type=jnp.float32).reshape(I_DEV, size_j, RANK)
            grad_a = jnp.einsum('ijr,jr->ir', deriv_c, factor_b, precision=high)
            grad_b = grad_b + jnp.einsum('ijr,ir->jr', deriv_c, rows_a, precision=high)
            grad_c = grad_c + lax.dot_general(deriv, khatri, (((0,), (0,)), ((), ())), precision=high, preferred_element_type=jnp.float32)
            return ((grad_b, grad_c), grad_a)
        start = (jnp.zeros((size_j, RANK), jnp.float32), jnp.zeros((K, RANK), jnp.float32))
        (grad_b, grad_c), grad_a = lax.scan(one_block, start, (blocks, factor_a.reshape(N_ROWS, I_DEV, RANK)))
        grad_a = grad_a.reshape(size_i, RANK)
        factor_a = factor_a - 4.0 / jnp.sqrt(jnp.float32(size_j * K)) * grad_a
        factor_b = factor_b - 4.0 / jnp.sqrt(jnp.float32(size_i * K)) * grad_b
        factor_c = factor_c - 4.0 / jnp.sqrt(jnp.float32(size_i * size_j)) * grad_c
    return (factor_a, factor_b, factor_c)
```

```python
import jax
import jax.numpy as jnp
from jax import lax
from jax.sharding import PartitionSpec as P

STEPS = 2


def exchange(parts, axis):
    return lax.all_to_all(parts, axis, 0, 0, tiled=True)


def per_device(tensor, first_factor, second_factor, third_factor):
    high = lax.Precision.HIGHEST
    n_rows, n_cols = lax.axis_size("rows"), lax.axis_size("cols")
    rows_dev, cols_dev, depth = tensor.shape
    size_i = rows_dev * n_rows
    size_j = cols_dev * n_cols
    rate_a = 4.0 / jnp.sqrt(jnp.float32(size_j * depth))
    rate_b = 4.0 / jnp.sqrt(jnp.float32(size_i * depth))
    rate_c = 4.0 / jnp.sqrt(jnp.float32(size_i * size_j))
    flat_target = tensor.reshape(-1, depth)
    shard_a, shard_b, shard_c = first_factor, second_factor, third_factor
    words_a, words_b = shard_a.size, shard_b.size
    rank = shard_c.shape[1]
    c_words = shard_c.size
    for _ in range(STEPS):
        mine = jnp.concatenate([shard_c.reshape(-1), shard_a.reshape(-1)])
        got = exchange(jnp.broadcast_to(mine[None], (n_cols, mine.size)), "cols")
        piece_c = got[:, :c_words].reshape(-1)
        whole_a = (
            got[:, c_words:].reshape(n_cols, rows_dev, -1).transpose(1, 0, 2).reshape(rows_dev, rank)
        )
        mine = jnp.concatenate([piece_c, shard_b.reshape(-1)])
        got = exchange(jnp.broadcast_to(mine[None], (n_rows, mine.size)), "rows")
        whole_c = got[:, : piece_c.size].reshape(depth, rank)
        whole_b = (
            got[:, piece_c.size :]
            .reshape(n_rows, cols_dev, -1)
            .transpose(1, 0, 2)
            .reshape(cols_dev, rank)
        )
        khatri = (whole_a[:, None, :] * whole_b[None, :, :]).reshape(-1, rank)
        model_tile = jnp.dot(khatri, whole_c.T, precision=high, preferred_element_type=jnp.float32)
        deriv = jax.nn.sigmoid(model_tile) - flat_target
        deriv_c = jnp.dot(
            deriv, whole_c, precision=high, preferred_element_type=jnp.float32
        ).reshape(rows_dev, cols_dev, -1)
        term_a = jnp.einsum("ijr,jr->ir", deriv_c, whole_b, precision=high)
        term_b = jnp.einsum("ijr,ir->jr", deriv_c, whole_a, precision=high)
        term_c = lax.dot_general(
            deriv,
            khatri,
            (((0,), (0,)), ((), ())),
            precision=high,
            preferred_element_type=jnp.float32,
        )
        send = jnp.concatenate(
            [
                term_c.reshape(n_rows, -1),
                term_b.reshape(cols_dev, n_rows, -1).transpose(1, 0, 2).reshape(n_rows, -1),
            ],
            axis=1,
        )
        got = exchange(send, "rows").sum(axis=0)
        part_c = got[: n_cols * c_words]
        shard_b = shard_b - rate_b * got[n_cols * c_words :].reshape(shard_b.shape)
        send = jnp.concatenate(
            [
                part_c.reshape(n_cols, -1),
                term_a.reshape(rows_dev, n_cols, -1).transpose(1, 0, 2).reshape(n_cols, -1),
            ],
            axis=1,
        )
        got = exchange(send, "cols").sum(axis=0)
        shard_c = shard_c - rate_c * got[:c_words].reshape(shard_c.shape)
        shard_a = shard_a - rate_a * got[c_words:].reshape(shard_a.shape)
    return (shard_a, shard_b, shard_c)


def solution(mesh):
    in_specs = (
        P("rows", "cols", None),
        P("rows", "cols"),
        P("cols", "rows"),
        P(("rows", "cols"), None),
    )
    out_specs = (P("rows", "cols"), P("cols", "rows"), P(("rows", "cols"), None))
    return jax.shard_map(
        per_device, mesh=mesh, in_specs=in_specs, out_specs=out_specs, check_vma=False
    )
```

```python
import jax
import jax.numpy as jnp
import numpy as np
from jax import lax
from jax.sharding import Mesh, PartitionSpec as P

STEPS = 2
XY = ("x", "y")
Z = ("zl", "zh")
HIGH = lax.Precision.HIGHEST


def exchange(parts, axis):
    return lax.all_to_all(parts, axis, 0, 0, tiled=True)


def swap(value):
    return lax.ppermute(value, "core", [(0, 1), (1, 0)])


def spread(block, count):
    return jnp.broadcast_to(block[None], (count,) + block.shape)


def fold(ab):
    return ab.reshape(4, 16, 64).transpose(1, 0, 2).reshape(16, 256)


def unfold(folded):
    lead = folded.shape[:-2]
    n = len(lead)
    split = folded.reshape(lead + (16, 4, 64))
    return split.transpose(tuple(range(n)) + (n + 1, n, n + 2)).reshape(lead + (64, 64))


def join_ab(a_t, b_t):
    return jnp.concatenate([a_t, jnp.zeros((a_t.shape[0], 8), jnp.float32), b_t], axis=1)


def per_device(tensor, first_factor, second_factor, third_factor):
    zl, x, core, zh, y = (lax.axis_index(n) for n in ("zl", "x", "core", "zh", "y"))
    n_i, n_j, depth = tensor.shape
    rank = third_factor.shape[1]
    size_i, size_j = n_i * 16, n_j * 16
    rate_a = 4.0 / jnp.sqrt(jnp.float32(size_j * depth))
    rate_b = 4.0 / jnp.sqrt(jnp.float32(size_i * depth))
    rate_c = 4.0 / jnp.sqrt(jnp.float32(size_i * size_j))

    flat = tensor.reshape(-1, depth)
    spot = lax.broadcasted_iota(jnp.int32, (depth, depth), 1)
    half = (spot // 256) ^ core
    xs, ys, zls, zhs, us = (
        (spot // 64) % 4,
        (spot // 16) % 4,
        (spot // 8) % 2,
        (spot // 2) % 4,
        spot % 2,
    )
    source = zls * 256 + xs * 64 + half * 32 + zhs * 8 + ys * 2 + us
    pick = (lax.broadcasted_iota(jnp.int32, (depth, depth), 0) == source).astype(jnp.float32)
    kept = jnp.dot(flat, pick[:, :256], precision=HIGH)
    sent = jnp.dot(flat, pick[:, 256:], precision=HIGH)
    target = jnp.concatenate([kept, swap(sent)], axis=0)

    a_t, b_t = first_factor.T, second_factor.T
    other = swap(jnp.concatenate([a_t, b_t], axis=1))
    a24 = jnp.concatenate([a_t, other[:, :n_i]], axis=1)
    b_other = other[:, n_i:]
    b32 = jnp.where(core == 0, jnp.concatenate([b_t, b_other]), jnp.concatenate([b_other, b_t]))
    ab = join_ab(jnp.concatenate([a24, a24]), b32)
    ab = ab.reshape(2, 16, 64).transpose(1, 0, 2).reshape(8, 256)
    c_pad = jnp.concatenate([third_factor, jnp.zeros((6, rank), jnp.float32)])
    got = exchange(spread(jnp.concatenate([c_pad, ab]), 8).reshape(-1, rank), Z)
    got = got.reshape(2, 4, 16, rank)
    block_c = got[:, :, :2].reshape(16, rank)
    ab = got[:, :, 8:].reshape(2, 4, 16, 2, 64).transpose(0, 1, 3, 2, 4).reshape(2, 4, 32, 64)
    block_a = lax.dynamic_index_in_dim(ab, zl, 0, False)[:, :16, :24].reshape(64, 24)
    block_b = lax.dynamic_index_in_dim(ab, zh, 1, False)[:, :, 32:].reshape(64, n_j)

    for step_index in range(STEPS):
        mine = jnp.concatenate([block_c, fold(join_ab(block_a, block_b))])
        got = exchange(spread(mine, 16).reshape(-1, rank), XY).reshape(4, 4, 32, rank)
        c = got[:, :, :16].reshape(256, rank)
        ab = unfold(got[:, :, 16:])
        a_all = lax.dynamic_index_in_dim(ab, x, 0, False)[:, :, :24]
        a_all = a_all.reshape(4, 4, 16, 24).transpose(1, 0, 2, 3).reshape(rank, 24).T
        b_all = lax.dynamic_index_in_dim(ab, y, 1, False)[:, :, 32:]
        b_all = b_all.reshape(4, 2, 32, n_j).transpose(1, 0, 2, 3).reshape(rank, n_j).T
        khatri = (a_all[:, None, :] * b_all[None, :, :]).reshape(-1, rank)
        model = jnp.dot(khatri, c.T, precision=HIGH, preferred_element_type=jnp.float32)
        deriv = jax.nn.sigmoid(model) - target
        deriv_c = jnp.dot(deriv, c, precision=HIGH, preferred_element_type=jnp.float32)
        deriv_c = deriv_c.reshape(24, n_j, rank)
        grad_a = jnp.sum(deriv_c * b_all[None], axis=1)
        grad_b = jnp.sum(deriv_c * a_all[:, None], axis=0)
        grad_c = lax.dot_general(
            deriv,
            khatri,
            (((0,), (0,)), ((), ())),
            precision=HIGH,
            preferred_element_type=jnp.float32,
        )
        send_a = grad_a.T.reshape(4, 4, 16, 24).transpose(1, 0, 2, 3).reshape(1, 4, 64, 24)
        send_b = grad_b.T.reshape(2, 4, 32, n_j).transpose(1, 0, 2, 3).reshape(4, 1, 64, n_j)
        send = jnp.concatenate(
            [
                jnp.broadcast_to(send_a, (4, 4, 64, 24)),
                jnp.zeros((4, 4, 64, 8), jnp.float32),
                jnp.broadcast_to(send_b, (4, 4, 64, n_j)),
            ],
            axis=3,
        )
        send = send.reshape(4, 4, 4, 16, 64).transpose(0, 1, 3, 2, 4).reshape(4, 4, 16, rank)
        send = jnp.concatenate([grad_c.reshape(4, 4, 16, rank), send], axis=2)
        got = exchange(send.reshape(-1, rank), XY).reshape(4, 4, 32, rank)
        part_c = got[:, :, :16].sum(axis=(0, 1))
        ab = unfold(got[:, :, 16:])
        part_a = lax.dynamic_index_in_dim(ab, x, 0, False)[:, :, :24].sum(axis=0)
        part_b = lax.dynamic_index_in_dim(ab, y, 1, False)[:, :, 32:].sum(axis=0)
        if step_index < STEPS - 1:
            mine = jnp.concatenate([part_c, fold(join_ab(part_a, part_b))])
            got = exchange(spread(mine, 8).reshape(-1, rank), Z).reshape(2, 4, 32, rank)
            block_c = block_c - rate_c * got[:, :, :16].sum(axis=(0, 1))
            ab = unfold(got[:, :, 16:])
            part_a = lax.dynamic_index_in_dim(ab, zl, 0, False)[:, :, :24].sum(axis=0)
            part_b = lax.dynamic_index_in_dim(ab, zh, 1, False)[:, :, 32:].sum(axis=0)
            other = swap(join_ab(part_a, part_b))
            other_a = jnp.concatenate([other[:, 12:24], other[:, :12]], axis=1)
            block_a = block_a - rate_a * (part_a + other_a)
            block_b = block_b - rate_b * (part_b + other[:, 32:])

    send_a = part_a.reshape(1, 4, 16, 24)
    send_b = part_b.reshape(2, 1, 32, n_j)
    send = jnp.concatenate(
        [
            jnp.broadcast_to(jnp.concatenate([send_a, send_a], axis=2), (2, 4, 32, 24)),
            jnp.zeros((2, 4, 32, 8), jnp.float32),
            jnp.broadcast_to(send_b, (2, 4, 32, n_j)),
        ],
        axis=3,
    )
    send = send.reshape(2, 4, 2, 16, 64).transpose(0, 1, 3, 2, 4).reshape(2, 4, 8, rank)
    send_c = jnp.concatenate(
        [part_c.reshape(2, 4, 2, rank), jnp.zeros((2, 4, 6, rank), jnp.float32)], axis=2
    )
    send = jnp.concatenate([send_c, send], axis=2)
    got = exchange(send.reshape(-1, rank), Z).reshape(2, 4, 16, rank)
    grad_c = got[:, :, :2].sum(axis=(0, 1))
    ab = got[:, :, 8:].reshape(2, 4, 16, 2, 64).transpose(0, 1, 3, 2, 4).reshape(2, 4, 32, 64)
    part_a = lax.dynamic_index_in_dim(ab, zl, 0, False)[:, :16, :24].sum(axis=0)
    part_b = lax.dynamic_index_in_dim(ab, zh, 1, False)[:, :, 32:].sum(axis=0)
    part_b = part_b.reshape(2, 16, n_j)
    own_b = lax.dynamic_index_in_dim(part_b, core, 0, False)
    away_b = lax.dynamic_index_in_dim(part_b, 1 - core, 0, False)
    other = swap(jnp.concatenate([part_a[:, 12:], away_b], axis=1))
    old_a = lax.dynamic_index_in_dim(block_a.reshape(4, 16, 24), zh, 0, False)[:, :n_i]
    old_b = lax.dynamic_index_in_dim(block_b.reshape(4, 16, n_j), zl * 2 + core, 0, False)
    old_c = lax.dynamic_index_in_dim(block_c.reshape(8, 2, rank), zl * 4 + zh, 0, False)
    new_a = old_a - rate_a * (part_a[:, :n_i] + other[:, :n_i])
    new_b = old_b - rate_b * (own_b + other[:, n_i:])
    new_c = old_c - rate_c * grad_c
    return (new_a.T, new_b.T, new_c)


def solution(mesh):
    fine = Mesh(mesh.devices.reshape(2, 4, 2, 4, 4), ("zl", "x", "core", "zh", "y"))
    rows, cols = ("zl", "x", "core"), ("zh", "y")
    in_specs = (P(rows, cols, None), P(rows, cols), P(cols, rows), P(rows + cols, None))
    out_specs = (P(rows, cols), P(cols, rows), P(rows + cols, None))
    return jax.shard_map(
        per_device, mesh=fine, in_specs=in_specs, out_specs=out_specs, check_vma=False
    )
```

```python
import functools

import jax
import jax.numpy as jnp
from jax import lax
from jax.experimental import pallas as pl
from jax.experimental.pallas import tpu as pltpu
from jax.sharding import Mesh, PartitionSpec as P

XY = ("x", "y")
Z = ("zl", "zh")
HIGH = lax.Precision.HIGHEST
F32 = jnp.float32


def exchange(parts, axis):
    shape = parts.shape
    got = lax.all_to_all(parts.reshape(-1, shape[2]), axis, 0, 0, tiled=True)
    return got.reshape(shape)


def swap(value):
    return lax.ppermute(value, "core", [(0, 1), (1, 0)])


def call(body, outs, scratch, index, *operands):
    vmem = pl.BlockSpec(memory_space=pltpu.VMEM)
    return pl.pallas_call(
        body,
        out_shape=[jax.ShapeDtypeStruct(s, F32) for s in outs],
        in_specs=[pl.BlockSpec(memory_space=pltpu.SMEM)] + [vmem] * len(operands),
        out_specs=[vmem] * len(outs),
        scratch_shapes=[pltpu.VMEM(s, F32) for s in scratch],
        compiler_params=pltpu.CompilerParams(vmem_limit_bytes=40 * 1024 * 1024),
    )(index, *operands)


def lanes(rows=16):
    return lax.broadcasted_iota(jnp.int32, (rows, 128), 1)


def split(value):
    top = value.astype(jnp.bfloat16)
    return top, (value - top.astype(F32)).astype(jnp.bfloat16)


def product(left, right, dims):
    (lt, lb), (rt, rb) = left, right
    dot = functools.partial(
        lax.dot_general, dimension_numbers=(dims, ((), ())), preferred_element_type=F32
    )
    return dot(lt, rt) + (dot(lt, rb) + dot(lb, rt))


def slip_of(block, place, zl, zh):
    a = block[16:32, 0:128]
    b = block[16:32, 128:256]
    if zh:
        a = pltpu.roll(a, 128 - 32 * zh, 1)
    if not zl:
        b = pltpu.roll(b, 32, 1)
    at = lanes()
    second = (at // 32) % 2 == 1
    ab = jnp.where(at < 32, a, jnp.where(second, b, 0.0))
    c = block[2 * place : 2 * place + 2, :]
    return c, ab


def first_slip(index, a_ref, bt_ref, c_ref, out_ref, pad):
    core = index[2]
    pad[...] = jnp.zeros((128, 128), F32)
    pad[0:12, 0:16] = a_ref[...]
    at = pad[...].T[0:16, :]
    pad[32:48, 0:32] = bt_ref[...]
    b = pad[32:48, :]
    a = jnp.where(core == 0, at, pltpu.roll(at, 12, 1))
    b = jnp.where(core == 0, pltpu.roll(b, 32, 1), pltpu.roll(b, 96, 1))
    out_ref[0:8, :] = jnp.zeros((8, 128), F32)
    out_ref[0:2, :] = c_ref[:, 0:128]
    out_ref[2:4, :] = c_ref[:, 128:256]
    out_ref[8:24, :] = a + b


def first_pack(index, own_ref, other_ref, out_ref):
    ab = own_ref[8:24, :] + other_ref[8:24, :]
    c = own_ref[0:8, :]
    for p in range(8):
        out_ref[p, 0:8, :] = c
        out_ref[p, 8:24, :] = ab


def block_from_slips(index, got_ref, block_ref, out_ref):
    zl, zh = index[0], index[3]
    for p in range(8):
        block_ref[2 * p : 2 * p + 2, 0:128] = got_ref[p, 0:2, :]
        block_ref[2 * p : 2 * p + 2, 128:256] = got_ref[p, 2:4, :]
    at = lanes()
    a = jnp.zeros((16, 128), F32)
    for q in range(4):
        v = jnp.where(at < 32, got_ref[zl * 4 + q, 8:24, :], 0.0)
        a = a + (pltpu.roll(v, 32 * q, 1) if q else v)
    second = (at // 32) % 2 == 1
    low = jnp.where(second, got_ref[zh, 8:24, :], 0.0)
    high = jnp.where(second, got_ref[4 + zh, 8:24, :], 0.0)
    block_ref[16:32, 0:128] = a
    block_ref[16:32, 128:256] = pltpu.roll(low, 96, 1) + high
    block = block_ref[...]
    for p in range(16):
        out_ref[p] = block


def gradients(index, got_ref, target_ref, out_ref, turn, khatri, terms):
    x, y = index[1], index[4]
    for q in range(4):
        v = got_ref[x * 4 + q, 16:32, 0:128]
        turn[16 * q : 16 * q + 16, :] = v
        turn[64 + 16 * q : 80 + 16 * q, :] = pltpu.roll(v, 96, 1)
    turned = turn[...].T
    a = jnp.concatenate([turned[0:24], turned[64:88]], axis=1)
    for q in range(4):
        v = got_ref[q * 4 + y, 16:32, 128:256]
        turn[32 * q : 32 * q + 16, :] = v
        turn[32 * q + 16 : 32 * q + 32, :] = pltpu.roll(v, 64, 1)
    turned = turn[...].T
    b = jnp.concatenate([turned[0:32], turned[32:64]], axis=1)
    for i in range(24):
        khatri[32 * i : 32 * i + 32, :] = a[i : i + 1, :] * b
    c = split(got_ref[:, 0:16, :].reshape(256, 256))
    parts = split(khatri[...])
    model = product(parts, c, ((1,), (1,)))
    deriv = split(jax.nn.sigmoid(model) - target_ref[...])
    terms[...] = product(deriv, c, ((1,), (0,)))
    grad_c = product(deriv, parts, ((0,), (0,)))
    grad_b = jnp.zeros((32, 256), F32)
    turn[...] = jnp.zeros((128, 128), F32)
    for i in range(24):
        term = terms[32 * i : 32 * i + 32, :]
        grad_b = grad_b + term * a[i : i + 1, :]
        row = jnp.sum(term * b, axis=0, keepdims=True)
        turn[i : i + 1, :] = row[:, 0:128]
        turn[64 + i : 65 + i, :] = row[:, 128:256]
    turned = turn[...].T
    pieces_a = [
        turned[16 * q : 16 * q + 16] + pltpu.roll(turned[64 + 16 * q : 80 + 16 * q], 32, 1)
        for q in range(4)
    ]
    turn[...] = jnp.zeros((128, 128), F32)
    turn[0:32, :] = grad_b[:, 0:128]
    turn[32:64, :] = grad_b[:, 128:256]
    turned = turn[...].T
    pieces_b = [
        turned[32 * q : 32 * q + 16] + pltpu.roll(turned[32 * q + 16 : 32 * q + 32], 64, 1)
        for q in range(4)
    ]
    out_ref[:, 0:16, :] = grad_c.reshape(16, 16, 256)
    for p in range(16):
        out_ref[p, 16:32, 0:128] = pieces_a[p % 4]
        out_ref[p, 16:32, 128:256] = pieces_b[p // 4]


def sum_xy(index, got_ref):
    x, y = index[1], index[4]
    c = jnp.sum(got_ref[:, 0:16, :], axis=0)
    a = got_ref[x * 4, 16:32, 0:128]
    b = got_ref[y, 16:32, 128:256]
    for q in range(1, 4):
        a = a + got_ref[x * 4 + q, 16:32, 0:128]
        b = b + got_ref[q * 4 + y, 16:32, 128:256]
    return c, a, b


def middle_pack(index, got_ref, out_ref):
    c, a, b = sum_xy(index, got_ref)
    for p in range(8):
        out_ref[p, 0:16, :] = c
        out_ref[p, 16:32, 0:128] = a
        out_ref[p, 16:32, 128:256] = b


def middle_sum(index, got_ref, c_ref, ab_ref):
    zl, zh = index[0], index[3]
    c_ref[...] = jnp.sum(got_ref[:, 0:16, :], axis=0)
    a = got_ref[zl * 4, 16:32, 0:128]
    for q in range(1, 4):
        a = a + got_ref[zl * 4 + q, 16:32, 0:128]
    ab_ref[:, 0:128] = a
    ab_ref[:, 128:256] = got_ref[zh, 16:32, 128:256] + got_ref[4 + zh, 16:32, 128:256]


def middle_update(rates, index, block_ref, c_ref, ab_ref, other_ref, slip_ref, out_ref, new):
    rate_a, rate_b, rate_c = rates
    ab = ab_ref[...] + other_ref[...]
    new[0:16, :] = block_ref[0:16, :] - rate_c * c_ref[...]
    new[16:32, 0:128] = block_ref[16:32, 0:128] - rate_a * ab[:, 0:128]
    new[16:32, 128:256] = block_ref[16:32, 128:256] - rate_b * ab[:, 128:256]
    block = new[...]
    for p in range(16):
        out_ref[p] = block
    own = index[0] * 4 + index[3]
    c = jnp.zeros((2, 256), F32)
    ab = jnp.zeros((16, 128), F32)
    for p in range(8):
        c_p, ab_p = slip_of(block, p, p // 4, p % 4)
        c = jnp.where(own == p, c_p, c)
        ab = jnp.where(own == p, ab_p, ab)
    slip_ref[0:8, :] = jnp.zeros((8, 128), F32)
    slip_ref[0:2, :] = c[:, 0:128]
    slip_ref[2:4, :] = c[:, 128:256]
    slip_ref[8:24, :] = ab


def last_pack(index, got_ref, out_ref, new):
    c, a, b = sum_xy(index, got_ref)
    new[0:16, :] = c
    new[16:32, 0:128] = a
    new[16:32, 128:256] = b
    block = new[...]
    for p in range(8):
        c_p, ab_p = slip_of(block, p, p // 4, p % 4)
        out_ref[p, 0:8, :] = jnp.zeros((8, 128), F32)
        out_ref[p, 0:2, :] = c_p[:, 0:128]
        out_ref[p, 2:4, :] = c_p[:, 128:256]
        out_ref[p, 8:24, :] = ab_p


def last_sum(index, got_ref, slip_ref):
    zl, zh = index[0], index[3]
    c = got_ref[0, 0:8, :]
    for p in range(1, 8):
        c = c + got_ref[p, 0:8, :]
    a = got_ref[zl * 4, 8:24, :]
    for q in range(1, 4):
        a = a + got_ref[zl * 4 + q, 8:24, :]
    b = got_ref[zh, 8:24, :] + got_ref[4 + zh, 8:24, :]
    slip_ref[0:8, :] = c
    slip_ref[8:24, :] = jnp.where(lanes() < 32, a, b)


def last_update(rates, index, old_ref, grad_ref, other_ref, a_ref, bt_ref, c_ref, pad):
    rate_a, rate_b, rate_c = rates
    core = index[2]
    c = old_ref[0:8, :] - rate_c * grad_ref[0:8, :]
    c_ref[:, 0:128] = c[0:2, :]
    c_ref[:, 128:256] = c[2:4, :]
    rate = jnp.where(lanes() < 32, rate_a, rate_b)
    ab = old_ref[8:24, :] - rate * (grad_ref[8:24, :] + other_ref[8:24, :])
    b = jnp.where(core == 0, pltpu.roll(ab, 96, 1), pltpu.roll(ab, 32, 1))
    bt_ref[...] = b[:, 0:32]
    pad[...] = jnp.zeros((128, 128), F32)
    pad[0:16, :] = jnp.where(core == 0, ab, pltpu.roll(ab, 116, 1))
    turned = pad[...].T
    a_ref[...] = turned[0:12, 0:16]


def arrange_target(tensor, core):
    depth = tensor.shape[2]
    flat = tensor.reshape(-1, depth)
    spot = lax.broadcasted_iota(jnp.int32, (depth, depth), 1)
    half = (spot // 256) ^ core
    xs, ys = (spot // 64) % 4, (spot // 16) % 4
    zls, zhs, us = (spot // 8) % 2, (spot // 2) % 4, spot % 2
    source = zls * 256 + xs * 64 + half * 32 + zhs * 8 + ys * 2 + us
    pick = (lax.broadcasted_iota(jnp.int32, (depth, depth), 0) == source).astype(F32)
    kept = jnp.dot(flat, pick[:, :256], precision=HIGH)
    came = swap(jnp.dot(flat, pick[:, 256:], precision=HIGH))
    return jnp.concatenate(
        [jnp.where(core == 0, kept, came), jnp.where(core == 0, came, kept)], axis=0
    )


def per_device(tensor, first_factor, second_factor, third_factor):
    index = jnp.stack([lax.axis_index(n) for n in ("zl", "x", "core", "zh", "y")])
    n_i, n_j, depth = tensor.shape
    size_i, size_j = n_i * 16, n_j * 16
    rates = tuple(4.0 / float(n) ** 0.5 for n in (size_j * depth, size_i * depth, size_i * size_j))
    wide = (16, 32, 256)
    square = (128, 128)

    (slip,) = call(first_slip, [(24, 128)], [square], index, first_factor, second_factor.T, third_factor)
    (send,) = call(first_pack, [(8, 24, 128)], [], index, slip, swap(slip))
    got = exchange(send, Z)
    target = arrange_target(tensor, index[2])
    block, send = call(block_from_slips, [(32, 256), wide], [], index, got)
    grads_scratch = [square, (768, 256), (768, 256)]

    (send,) = call(gradients, [wide], grads_scratch, index, exchange(send, XY), target)
    (send,) = call(middle_pack, [(8, 32, 256)], [], index, exchange(send, XY))
    grad_c, grad_ab = call(middle_sum, [(16, 256), (16, 256)], [], index, exchange(send, Z))
    slip, send = call(
        functools.partial(middle_update, rates),
        [(24, 128), wide],
        [(32, 256)],
        index,
        block,
        grad_c,
        grad_ab,
        swap(grad_ab),
    )
    (send,) = call(gradients, [wide], grads_scratch, index, exchange(send, XY), target)
    (send,) = call(last_pack, [(8, 24, 128)], [(32, 256)], index, exchange(send, XY))
    (grad,) = call(last_sum, [(24, 128)], [], index, exchange(send, Z))
    new_a, new_bt, new_c = call(
        functools.partial(last_update, rates),
        [(n_i, 16), (16, n_j), third_factor.shape],
        [square],
        index,
        slip,
        grad,
        swap(grad),
    )
    return (new_a, new_bt.T, new_c)


def solution(mesh):
    fine = Mesh(mesh.devices.reshape(2, 4, 2, 4, 4), ("zl", "x", "core", "zh", "y"))
    rows, cols = ("zl", "x", "core"), ("zh", "y")
    in_specs = (P(rows, cols, None), P(rows, cols), P(cols, rows), P(rows + cols, None))
    out_specs = (P(rows, cols), P(cols, rows), P(rows + cols, None))
    return jax.shard_map(
        per_device, mesh=fine, in_specs=in_specs, out_specs=out_specs, check_vma=False
    )
```

```python
import functools

import jax
import jax.numpy as jnp
from jax import lax
from jax.experimental import pallas as pl
from jax.experimental.pallas import tpu as pltpu
from jax.sharding import Mesh, PartitionSpec as P

XY = ("x", "y")
Z = ("zl", "zh")
HIGH = lax.Precision.HIGHEST
F32 = jnp.float32


def exchange(parts, axis):
    shape = parts.shape
    got = lax.all_to_all(parts.reshape(-1, shape[2]), axis, 0, 0, tiled=True)
    return got.reshape(shape)


def swap(value):
    return lax.ppermute(value, "core", [(0, 1), (1, 0)])


def call(body, outs, scratch, index, *operands):
    vmem = pl.BlockSpec(memory_space=pltpu.VMEM)
    return pl.pallas_call(
        body,
        out_shape=[jax.ShapeDtypeStruct(s, F32) for s in outs],
        in_specs=[pl.BlockSpec(memory_space=pltpu.SMEM)] + [vmem] * len(operands),
        out_specs=[vmem] * len(outs),
        scratch_shapes=[pltpu.VMEM(s, F32) for s in scratch],
        compiler_params=pltpu.CompilerParams(vmem_limit_bytes=40 * 1024 * 1024),
    )(index, *operands)


def lanes(rows=16):
    return lax.broadcasted_iota(jnp.int32, (rows, 128), 1)


def split(value):
    top = value.astype(jnp.bfloat16)
    return top, (value - top.astype(F32)).astype(jnp.bfloat16)


def product(left, right, dims):
    (lt, lb), (rt, rb) = left, right
    dot = functools.partial(
        lax.dot_general, dimension_numbers=(dims, ((), ())), preferred_element_type=F32
    )
    return dot(lt, rt) + (dot(lt, rb) + dot(lb, rt))


def fill_slot(ref, p, value):
    ref[p, 16:24, 0:128] = value[0:8]
    ref[p, 16:24, 128:256] = value[8:16]


def slot(ref, p):
    v = ref[p, 16:24, :]
    return jnp.concatenate([v[:, 0:128], v[:, 128:256]], axis=0)


def send_block(block, out_ref, x):
    for p in range(16):
        out_ref[p, 0:16, :] = block[0:16]
        fill_slot(out_ref, p, jnp.where(x == p // 4, block[16:32, 0:128], block[16:32, 128:256]))


def slip_of(block, place, zl, zh):
    a = block[16:32, 0:128]
    b = block[16:32, 128:256]
    if zh:
        a = pltpu.roll(a, 128 - 32 * zh, 1)
    if not zl:
        b = pltpu.roll(b, 32, 1)
    at = lanes()
    second = (at // 32) % 2 == 1
    ab = jnp.where(at < 32, a, jnp.where(second, b, 0.0))
    c = block[2 * place : 2 * place + 2, :]
    return c, ab


def first_slip(index, a_ref, bt_ref, c_ref, out_ref, pad):
    core = index[2]
    pad[...] = jnp.zeros((128, 128), F32)
    pad[0:12, 0:16] = a_ref[...]
    at = pad[...].T[0:16, :]
    pad[32:48, 0:32] = bt_ref[...]
    b = pad[32:48, :]
    a = jnp.where(core == 0, at, pltpu.roll(at, 12, 1))
    b = jnp.where(core == 0, pltpu.roll(b, 32, 1), pltpu.roll(b, 96, 1))
    out_ref[0:8, :] = jnp.zeros((8, 128), F32)
    out_ref[0:2, :] = c_ref[:, 0:128]
    out_ref[2:4, :] = c_ref[:, 128:256]
    out_ref[8:24, :] = a + b


def first_pack(index, own_ref, other_ref, out_ref):
    ab = own_ref[8:24, :] + other_ref[8:24, :]
    c = own_ref[0:8, :]
    for p in range(8):
        out_ref[p, 0:8, :] = c
        out_ref[p, 8:24, :] = ab


def block_from_slips(index, got_ref, block_ref, out_ref, core_ref):
    zl, zh = index[0], index[3]
    core_ref[...] = jnp.full((8, 128), index[2], jnp.int32).astype(F32)
    for p in range(8):
        block_ref[2 * p : 2 * p + 2, 0:128] = got_ref[p, 0:2, :]
        block_ref[2 * p : 2 * p + 2, 128:256] = got_ref[p, 2:4, :]
    at = lanes()
    a = jnp.zeros((16, 128), F32)
    for q in range(4):
        v = jnp.where(at < 32, got_ref[zl * 4 + q, 8:24, :], 0.0)
        a = a + (pltpu.roll(v, 32 * q, 1) if q else v)
    second = (at // 32) % 2 == 1
    low = jnp.where(second, got_ref[zh, 8:24, :], 0.0)
    high = jnp.where(second, got_ref[4 + zh, 8:24, :], 0.0)
    block_ref[16:32, 0:128] = a
    block_ref[16:32, 128:256] = pltpu.roll(low, 96, 1) + high
    send_block(block_ref[...], out_ref, index[1])


def gradients(
    index, got_ref, block_ref, kept_ref, came_ref, out_ref, own_ref, turn, khatri, terms, first
):
    x, core, y = index[1], index[2], index[4]
    order = [i + 12 * core if i < 12 else i - 12 * core for i in range(24)]
    for q in range(4):
        v = jnp.where(y == q, block_ref[16:32, 0:128], slot(got_ref, x * 4 + q))
        turn[16 * q : 16 * q + 16, :] = v
        turn[64 + 16 * q : 80 + 16 * q, :] = pltpu.roll(v, 96, 1)
    turned = turn[...].T
    first[:, 0:128] = turned[0:24]
    first[:, 128:256] = turned[64:88]
    a = [first[pl.ds(i, 1), :] for i in order]
    for q in range(4):
        v = jnp.where(x == q, block_ref[16:32, 128:256], slot(got_ref, q * 4 + y))
        turn[32 * q : 32 * q + 16, :] = v
        turn[32 * q + 16 : 32 * q + 32, :] = pltpu.roll(v, 64, 1)
    turned = turn[...].T
    b = jnp.concatenate([turned[0:32], turned[32:64]], axis=1)
    for i in range(24):
        khatri[32 * i : 32 * i + 32, :] = a[i] * b
    c = split(got_ref[:, 0:16, :].reshape(256, 256))
    parts = split(khatri[...])
    model = product(parts, c, ((1,), (1,)))
    target = jnp.concatenate([kept_ref[...], came_ref[...]], axis=0)
    deriv = split(jax.nn.sigmoid(model) - target)
    terms[...] = product(deriv, c, ((1,), (0,)))
    grad_c = product(deriv, parts, ((0,), (0,)))
    grad_b = jnp.zeros((32, 256), F32)
    turn[...] = jnp.zeros((128, 128), F32)
    for i in range(24):
        term = terms[32 * i : 32 * i + 32, :]
        grad_b = grad_b + term * a[i]
        row = jnp.sum(term * b, axis=0, keepdims=True)
        turn[pl.ds(order[i], 1), :] = row[:, 0:128]
        turn[pl.ds(order[i] + 64, 1), :] = row[:, 128:256]
    turned = turn[...].T
    pieces_a = [
        turned[16 * q : 16 * q + 16] + pltpu.roll(turned[64 + 16 * q : 80 + 16 * q], 32, 1)
        for q in range(4)
    ]
    turn[...] = jnp.zeros((128, 128), F32)
    turn[0:32, :] = grad_b[:, 0:128]
    turn[32:64, :] = grad_b[:, 128:256]
    turned = turn[...].T
    pieces_b = [
        turned[32 * q : 32 * q + 16] + pltpu.roll(turned[32 * q + 16 : 32 * q + 32], 64, 1)
        for q in range(4)
    ]
    out_ref[:, 0:16, :] = grad_c.reshape(16, 16, 256)
    for p in range(16):
        fill_slot(out_ref, p, jnp.where(x == p // 4, pieces_a[p % 4], pieces_b[p // 4]))
    own_a, own_b = pieces_a[0], pieces_b[0]
    for q in range(1, 4):
        own_a = jnp.where(y == q, pieces_a[q], own_a)
        own_b = jnp.where(x == q, pieces_b[q], own_b)
    own_ref[:, 0:128] = own_a
    own_ref[:, 128:256] = own_b


def sum_xy(index, got_ref, own_ref):
    x, y = index[1], index[4]
    c = jnp.sum(got_ref[:, 0:16, :], axis=0)
    a, b = own_ref[:, 0:128], own_ref[:, 128:256]
    for q in range(4):
        a = a + jnp.where(y == q, 0.0, slot(got_ref, x * 4 + q))
        b = b + jnp.where(x == q, 0.0, slot(got_ref, q * 4 + y))
    return c, a, b


def middle_pack(index, got_ref, own_ref, out_ref, sum_ref):
    c, a, b = sum_xy(index, got_ref, own_ref)
    for p in range(8):
        out_ref[p, 0:16, :] = c
        fill_slot(out_ref, p, jnp.where(index[0] == p // 4, a, b))
    sum_ref[:, 0:128] = a
    sum_ref[:, 128:256] = b


def middle_sum(index, got_ref, own_ref, c_ref, ab_ref):
    zl, zh = index[0], index[3]
    c_ref[...] = jnp.sum(got_ref[:, 0:16, :], axis=0)
    a = own_ref[:, 0:128]
    for q in range(4):
        a = a + jnp.where(zh == q, 0.0, slot(got_ref, zl * 4 + q))
    ab_ref[:, 0:128] = a
    ab_ref[:, 128:256] = own_ref[:, 128:256] + slot(got_ref, (1 - zl) * 4 + zh)


def middle_update(rates, index, block_ref, c_ref, ab_ref, other_ref, slip_ref, block_out, out_ref, new):
    rate_a, rate_b, rate_c = rates
    ab = ab_ref[...] + other_ref[...]
    new[0:16, :] = block_ref[0:16, :] - rate_c * c_ref[...]
    new[16:32, 0:128] = block_ref[16:32, 0:128] - rate_a * ab[:, 0:128]
    new[16:32, 128:256] = block_ref[16:32, 128:256] - rate_b * ab[:, 128:256]
    block = new[...]
    block_out[...] = block
    send_block(block, out_ref, index[1])
    own = index[0] * 4 + index[3]
    c = jnp.zeros((2, 256), F32)
    ab = jnp.zeros((16, 128), F32)
    for p in range(8):
        c_p, ab_p = slip_of(block, p, p // 4, p % 4)
        c = jnp.where(own == p, c_p, c)
        ab = jnp.where(own == p, ab_p, ab)
    slip_ref[0:8, :] = jnp.zeros((8, 128), F32)
    slip_ref[0:2, :] = c[:, 0:128]
    slip_ref[2:4, :] = c[:, 128:256]
    slip_ref[8:24, :] = ab


def last_pack(index, got_ref, own_ref, out_ref, new):
    c, a, b = sum_xy(index, got_ref, own_ref)
    new[0:16, :] = c
    new[16:32, 0:128] = a
    new[16:32, 128:256] = b
    block = new[...]
    for p in range(8):
        c_p, ab_p = slip_of(block, p, p // 4, p % 4)
        out_ref[p, 0:8, :] = jnp.zeros((8, 128), F32)
        out_ref[p, 0:2, :] = c_p[:, 0:128]
        out_ref[p, 2:4, :] = c_p[:, 128:256]
        out_ref[p, 8:24, :] = ab_p


def last_sum(index, got_ref, slip_ref):
    zl, zh = index[0], index[3]
    c = got_ref[0, 0:8, :]
    for p in range(1, 8):
        c = c + got_ref[p, 0:8, :]
    a = got_ref[zl * 4, 8:24, :]
    for q in range(1, 4):
        a = a + got_ref[zl * 4 + q, 8:24, :]
    b = got_ref[zh, 8:24, :] + got_ref[4 + zh, 8:24, :]
    slip_ref[0:8, :] = c
    slip_ref[8:24, :] = jnp.where(lanes() < 32, a, b)


def last_update(rates, index, old_ref, grad_ref, other_ref, a_ref, bt_ref, c_ref, pad):
    rate_a, rate_b, rate_c = rates
    core = index[2]
    c = old_ref[0:8, :] - rate_c * grad_ref[0:8, :]
    c_ref[:, 0:128] = c[0:2, :]
    c_ref[:, 128:256] = c[2:4, :]
    rate = jnp.where(lanes() < 32, rate_a, rate_b)
    ab = old_ref[8:24, :] - rate * (grad_ref[8:24, :] + other_ref[8:24, :])
    b = jnp.where(core == 0, pltpu.roll(ab, 96, 1), pltpu.roll(ab, 32, 1))
    bt_ref[...] = b[:, 0:32]
    pad[...] = jnp.zeros((128, 128), F32)
    pad[0:16, :] = jnp.where(core == 0, ab, pltpu.roll(ab, 116, 1))
    turned = pad[...].T
    a_ref[...] = turned[0:12, 0:16]


def arrange(flats, core):
    depth = flats[0].shape[1]
    spot = lax.broadcasted_iota(jnp.int32, (depth, depth // 2), 1)
    half = jnp.where(core == 0.0, 0, 32)
    xs, ys = spot // 64, (spot // 16) % 4
    zls, zhs, us = (spot // 8) % 2, (spot // 2) % 4, spot % 2
    source = zls * 256 + xs * 64 + half + zhs * 8 + ys * 2 + us
    here = lax.broadcasted_iota(jnp.int32, (depth, depth // 2), 0)
    pick = (here == source).astype(F32)
    return [jnp.dot(flat, pick, precision=HIGH) for flat in flats]


def per_device(tensor, first_factor, second_factor, third_factor):
    index = jnp.stack([lax.axis_index(n) for n in ("zl", "x", "core", "zh", "y")])
    n_i, n_j, depth = tensor.shape
    size_i, size_j = n_i * 16, n_j * 16
    rates = tuple(4.0 / float(n) ** 0.5 for n in (size_j * depth, size_i * depth, size_i * size_j))
    wide = (16, 24, 256)
    square, pair = (128, 128), (16, 256)

    flat = tensor.reshape(-1, depth)
    flat_other = swap(flat)
    (slip,) = call(first_slip, [(24, 128)], [square], index, first_factor, second_factor.T, third_factor)
    (send,) = call(first_pack, [(8, 24, 128)], [], index, slip, swap(slip))
    block, send, core = call(
        block_from_slips, [(32, 256), wide, (8, 128)], [], index, exchange(send, Z)
    )
    targets = arrange((flat, flat_other), core[0, 0])
    step = functools.partial(
        call, gradients, [wide, pair], [square, (768, 256), (768, 256), (24, 256)], index
    )

    send, own = step(exchange(send, XY), block, *targets)
    send, own = call(middle_pack, [(8, 24, 256), pair], [], index, exchange(send, XY), own)
    grad_c, grad_ab = call(middle_sum, [pair, pair], [], index, exchange(send, Z), own)
    slip, block, send = call(
        functools.partial(middle_update, rates),
        [(24, 128), (32, 256), wide],
        [(32, 256)],
        index,
        block,
        grad_c,
        grad_ab,
        swap(grad_ab),
    )
    send, own = step(exchange(send, XY), block, *targets)
    (send,) = call(last_pack, [(8, 24, 128)], [(32, 256)], index, exchange(send, XY), own)
    (grad,) = call(last_sum, [(24, 128)], [], index, exchange(send, Z))
    new_a, new_bt, new_c = call(
        functools.partial(last_update, rates),
        [(n_i, 16), (16, n_j), third_factor.shape],
        [square],
        index,
        slip,
        grad,
        swap(grad),
    )
    return (new_a, new_bt.T, new_c)


def solution(mesh):
    fine = Mesh(mesh.devices.reshape(2, 4, 2, 4, 4), ("zl", "x", "core", "zh", "y"))
    rows, cols = ("zl", "x", "core"), ("zh", "y")
    in_specs = (P(rows, cols, None), P(rows, cols), P(cols, rows), P(rows + cols, None))
    out_specs = (P(rows, cols), P(cols, rows), P(rows + cols, None))
    return jax.shard_map(
        per_device, mesh=fine, in_specs=in_specs, out_specs=out_specs, check_vma=False
    )
```

```python
import functools

import jax
import jax.numpy as jnp
from jax import lax
from jax.experimental import pallas as pl
from jax.experimental.pallas import tpu as pltpu
from jax.sharding import Mesh, PartitionSpec as P

XY = ("x", "y")
Z = ("zl", "zh")
HIGH = lax.Precision.HIGHEST
F32 = jnp.float32


def exchange(parts, axis):
    shape = parts.shape
    got = lax.all_to_all(parts.reshape(-1, shape[2]), axis, 0, 0, tiled=True)
    return got.reshape(shape)


def swap(value):
    return lax.ppermute(value, "core", [(0, 1), (1, 0)])


def call(body, outs, scratch, index, *operands):
    vmem = pl.BlockSpec(memory_space=pltpu.VMEM)
    return pl.pallas_call(
        body,
        out_shape=[jax.ShapeDtypeStruct(s, F32) for s in outs],
        in_specs=[pl.BlockSpec(memory_space=pltpu.SMEM)] + [vmem] * len(operands),
        out_specs=[vmem] * len(outs),
        scratch_shapes=[pltpu.VMEM(s, F32) for s in scratch],
        compiler_params=pltpu.CompilerParams(vmem_limit_bytes=40 * 1024 * 1024),
    )(index, *operands)


def lanes(rows=16):
    return lax.broadcasted_iota(jnp.int32, (rows, 128), 1)


def split(value):
    top = value.astype(jnp.bfloat16)
    return top, (value - top.astype(F32)).astype(jnp.bfloat16)


def product(left, right, dims):
    (lt, lb), (rt, rb) = left, right
    dot = functools.partial(
        lax.dot_general, dimension_numbers=(dims, ((), ())), preferred_element_type=F32
    )
    return dot(lt, rt) + (dot(lt, rb) + dot(lb, rt))


def fill_slot(ref, p, value):
    ref[p, 16:24, 0:128] = value[0:8]
    ref[p, 16:24, 128:256] = value[8:16]


def slot(ref, p):
    v = ref[p, 16:24, :]
    return jnp.concatenate([v[:, 0:128], v[:, 128:256]], axis=0)


def send_block(block, out_ref, x):
    for p in range(16):
        out_ref[p, 0:16, :] = block[0:16]
        fill_slot(out_ref, p, jnp.where(x == p // 4, block[16:32, 0:128], block[16:32, 128:256]))


def slip_of(block, place, zl, zh):
    a = block[16:32, 0:128]
    b = block[16:32, 128:256]
    if zh:
        a = pltpu.roll(a, 128 - 32 * zh, 1)
    if not zl:
        b = pltpu.roll(b, 32, 1)
    at = lanes()
    second = (at // 32) % 2 == 1
    ab = jnp.where(at < 32, a, jnp.where(second, b, 0.0))
    c = block[2 * place : 2 * place + 2, :]
    return c, ab


def placed(a, bt, core, pad):
    pad[...] = jnp.zeros((128, 128), F32)
    pad[0:12, 0:16] = a
    at = pad[...].T[0:16, :]
    pad[32:48, 0:32] = bt
    b = pad[32:48, :]
    even = core == 0
    at = jnp.where(even, at, pltpu.roll(at, 16, 1))
    return at + jnp.where(even, pltpu.roll(b, 32, 1), pltpu.roll(b, 96, 1))


def first_slip(index, a_ref, bt_ref, c_ref, out_ref, pad):
    out_ref[0:8, :] = jnp.zeros((8, 128), F32)
    out_ref[0:2, :] = c_ref[:, 0:128]
    out_ref[2:4, :] = c_ref[:, 128:256]
    out_ref[8:24, :] = placed(a_ref[...], bt_ref[...], index[2], pad)


def first_pack(index, own_ref, other_ref, out_ref):
    ab = own_ref[8:24, :] + other_ref[8:24, :]
    c = own_ref[0:8, :]
    for p in range(8):
        out_ref[p, 0:8, :] = c
        out_ref[p, 8:24, :] = ab


def block_from_slips(index, got_ref, block_ref, out_ref):
    zl, zh = index[0], index[3]
    for p in range(8):
        block_ref[2 * p : 2 * p + 2, 0:128] = got_ref[p, 0:2, :]
        block_ref[2 * p : 2 * p + 2, 128:256] = got_ref[p, 2:4, :]
    at = lanes()
    a = jnp.zeros((16, 128), F32)
    for q in range(4):
        v = jnp.where(at < 32, got_ref[zl * 4 + q, 8:24, :], 0.0)
        a = a + (pltpu.roll(v, 32 * q, 1) if q else v)
    second = (at // 32) % 2 == 1
    low = jnp.where(second, got_ref[zh, 8:24, :], 0.0)
    high = jnp.where(second, got_ref[4 + zh, 8:24, :], 0.0)
    block_ref[16:32, 0:128] = a
    block_ref[16:32, 128:256] = pltpu.roll(low, 96, 1) + high
    send_block(block_ref[...], out_ref, index[1])


def gradients(
    index, got_ref, block_ref, kept_ref, came_ref, out_ref, own_ref, turn, khatri, terms, first
):
    x, core, y = index[1], index[2], index[4]
    order = [i + 16 * core if i < 12 else i + 4 - 16 * core for i in range(24)]
    for q in range(4):
        v = jnp.where(y == q, block_ref[16:32, 0:128], slot(got_ref, x * 4 + q))
        turn[16 * q : 16 * q + 16, :] = v
        turn[64 + 16 * q : 80 + 16 * q, :] = pltpu.roll(v, 96, 1)
    turned = turn[...].T
    first[:, 0:128] = turned[0:32]
    first[:, 128:256] = turned[64:96]
    a = [first[pl.ds(i, 1), :] for i in order]
    for q in range(4):
        v = jnp.where(x == q, block_ref[16:32, 128:256], slot(got_ref, q * 4 + y))
        turn[32 * q : 32 * q + 16, :] = v
        turn[32 * q + 16 : 32 * q + 32, :] = pltpu.roll(v, 64, 1)
    turned = turn[...].T
    b = jnp.concatenate([turned[0:32], turned[32:64]], axis=1)
    for i in range(24):
        khatri[32 * i : 32 * i + 32, :] = a[i] * b
    c = split(got_ref[:, 0:16, :].reshape(256, 256))
    parts = split(khatri[...])
    model = product(parts, c, ((1,), (1,)))
    target = jnp.concatenate([kept_ref[...], came_ref[...]], axis=0)
    deriv = split(jax.nn.sigmoid(model) - target)
    terms[...] = product(deriv, c, ((1,), (0,)))
    grad_c = product(deriv, parts, ((0,), (0,)))
    grad_b = jnp.zeros((32, 256), F32)
    turn[...] = jnp.zeros((128, 128), F32)
    for i in range(24):
        term = terms[32 * i : 32 * i + 32, :]
        grad_b = grad_b + term * a[i]
        row = jnp.sum(term * b, axis=0, keepdims=True)
        turn[pl.ds(order[i], 1), :] = row[:, 0:128]
        turn[pl.ds(order[i] + 64, 1), :] = row[:, 128:256]
    turned = turn[...].T
    pieces_a = [
        turned[16 * q : 16 * q + 16] + pltpu.roll(turned[64 + 16 * q : 80 + 16 * q], 32, 1)
        for q in range(4)
    ]
    turn[...] = jnp.zeros((128, 128), F32)
    turn[0:32, :] = grad_b[:, 0:128]
    turn[32:64, :] = grad_b[:, 128:256]
    turned = turn[...].T
    pieces_b = [
        turned[32 * q : 32 * q + 16] + pltpu.roll(turned[32 * q + 16 : 32 * q + 32], 64, 1)
        for q in range(4)
    ]
    out_ref[:, 0:16, :] = grad_c.reshape(16, 16, 256)
    for p in range(16):
        fill_slot(out_ref, p, jnp.where(x == p // 4, pieces_a[p % 4], pieces_b[p // 4]))
    own_a, own_b = pieces_a[0], pieces_b[0]
    for q in range(1, 4):
        own_a = jnp.where(y == q, pieces_a[q], own_a)
        own_b = jnp.where(x == q, pieces_b[q], own_b)
    own_ref[:, 0:128] = own_a
    own_ref[:, 128:256] = own_b


def sum_xy(index, got_ref, own_ref):
    x, y = index[1], index[4]
    c = jnp.sum(got_ref[:, 0:16, :], axis=0)
    a, b = own_ref[:, 0:128], own_ref[:, 128:256]
    for q in range(4):
        a = a + jnp.where(y == q, 0.0, slot(got_ref, x * 4 + q))
        b = b + jnp.where(x == q, 0.0, slot(got_ref, q * 4 + y))
    return c, a, b


def middle_pack(index, got_ref, own_ref, out_ref, sum_ref):
    c, a, b = sum_xy(index, got_ref, own_ref)
    for p in range(8):
        out_ref[p, 0:16, :] = c
        fill_slot(out_ref, p, jnp.where(index[0] == p // 4, a, b))
    sum_ref[:, 0:128] = a
    sum_ref[:, 128:256] = b


def middle_sum(index, got_ref, own_ref, c_ref, ab_ref):
    zl, zh = index[0], index[3]
    c_ref[...] = jnp.sum(got_ref[:, 0:16, :], axis=0)
    a = own_ref[:, 0:128]
    for q in range(4):
        a = a + jnp.where(zh == q, 0.0, slot(got_ref, zl * 4 + q))
    ab_ref[:, 0:128] = a
    ab_ref[:, 128:256] = own_ref[:, 128:256] + slot(got_ref, (1 - zl) * 4 + zh)


def middle_update(rates, index, block_ref, c_ref, ab_ref, other_ref, slip_ref, block_out, out_ref, new):
    rate_a, rate_b, rate_c = rates
    ab = ab_ref[...] + other_ref[...]
    new[0:16, :] = block_ref[0:16, :] - rate_c * c_ref[...]
    new[16:32, 0:128] = block_ref[16:32, 0:128] - rate_a * ab[:, 0:128]
    new[16:32, 128:256] = block_ref[16:32, 128:256] - rate_b * ab[:, 128:256]
    block = new[...]
    block_out[...] = block
    send_block(block, out_ref, index[1])
    own = index[0] * 4 + index[3]
    c = jnp.zeros((2, 256), F32)
    ab = jnp.zeros((16, 128), F32)
    for p in range(8):
        c_p, ab_p = slip_of(block, p, p // 4, p % 4)
        c = jnp.where(own == p, c_p, c)
        ab = jnp.where(own == p, ab_p, ab)
    slip_ref[0:8, :] = jnp.zeros((8, 128), F32)
    slip_ref[0:2, :] = c[:, 0:128]
    slip_ref[2:4, :] = c[:, 128:256]
    slip_ref[8:24, :] = ab


def last_pack(index, got_ref, own_ref, out_ref, new):
    c, a, b = sum_xy(index, got_ref, own_ref)
    new[0:16, :] = c
    new[16:32, 0:128] = a
    new[16:32, 128:256] = b
    block = new[...]
    for p in range(8):
        c_p, ab_p = slip_of(block, p, p // 4, p % 4)
        out_ref[p, 0:8, :] = jnp.zeros((8, 128), F32)
        out_ref[p, 0:2, :] = c_p[:, 0:128]
        out_ref[p, 2:4, :] = c_p[:, 128:256]
        out_ref[p, 8:24, :] = ab_p


def last_sum(index, got_ref, slip_ref):
    zl, zh = index[0], index[3]
    c = got_ref[0, 0:8, :]
    for p in range(1, 8):
        c = c + got_ref[p, 0:8, :]
    a = got_ref[zl * 4, 8:24, :]
    for q in range(1, 4):
        a = a + got_ref[zl * 4 + q, 8:24, :]
    b = got_ref[zh, 8:24, :] + got_ref[4 + zh, 8:24, :]
    slip_ref[0:8, :] = c
    slip_ref[8:24, :] = jnp.where(lanes() < 32, a, b)


def last_update(rates, index, old_ref, grad_ref, other_ref, a_ref, bt_ref, c_ref, pad):
    rate_a, rate_b, rate_c = rates
    core = index[2]
    c = old_ref[0:8, :] - rate_c * grad_ref[0:8, :]
    c_ref[:, 0:128] = c[0:2, :]
    c_ref[:, 128:256] = c[2:4, :]
    rate = jnp.where(lanes() < 32, rate_a, rate_b)
    ab = old_ref[8:24, :] - rate * (grad_ref[8:24, :] + other_ref[8:24, :])
    b = jnp.where(core == 0, pltpu.roll(ab, 96, 1), pltpu.roll(ab, 32, 1))
    bt_ref[...] = b[:, 0:32]
    pad[...] = jnp.zeros((128, 128), F32)
    pad[0:16, :] = jnp.where(core == 0, ab, pltpu.roll(ab, 112, 1))
    turned = pad[...].T
    a_ref[...] = turned[0:12, 0:16]


def arrange(index, after_ref, own_ref, other_ref, kept_ref, came_ref):
    del after_ref
    spot = lax.broadcasted_iota(jnp.int32, (512, 256), 1)
    xs, ys = spot // 64, (spot // 16) % 4
    zls, zhs, us = (spot // 8) % 2, (spot // 2) % 4, spot % 2
    source = zls * 256 + xs * 64 + index[2] * 32 + zhs * 8 + ys * 2 + us
    here = lax.broadcasted_iota(jnp.int32, (512, 256), 0)
    pick = jnp.where(here == source, 1.0, 0.0).astype(jnp.bfloat16)
    for from_ref, to_ref in ((own_ref, kept_ref), (other_ref, came_ref)):
        rest = from_ref[...]
        total = jnp.zeros((384, 256), F32)
        for _ in range(3):
            part = rest.astype(jnp.bfloat16)
            rest = rest - part.astype(F32)
            total = total + jnp.dot(part, pick, preferred_element_type=F32)
        to_ref[...] = total


def per_device(tensor, first_factor, second_factor, third_factor):
    index = jnp.stack([lax.axis_index(n) for n in ("zl", "x", "core", "zh", "y")])
    n_i, n_j, depth = tensor.shape
    size_i, size_j = n_i * 16, n_j * 16
    rates = tuple(4.0 / float(n) ** 0.5 for n in (size_j * depth, size_i * depth, size_i * size_j))
    wide = (16, 24, 256)
    square, pair = (128, 128), (16, 256)

    flat = tensor.reshape(-1, depth)
    b_t = second_factor.T
    flat_other = swap(flat)
    (slip,) = call(first_slip, [(24, 128)], [square], index, first_factor, b_t, third_factor)
    (send,) = call(first_pack, [(8, 24, 128)], [], index, slip, swap(slip))
    block, send = call(block_from_slips, [(32, 256), wide], [], index, exchange(send, Z))
    targets = call(arrange, [(384, 256), (384, 256)], [], index, block, flat, flat_other)
    step = functools.partial(
        call, gradients, [wide, pair], [square, (768, 256), (768, 256), (32, 256)], index
    )

    send, own = step(exchange(send, XY), block, *targets)
    send, own = call(middle_pack, [(8, 24, 256), pair], [], index, exchange(send, XY), own)
    grad_c, grad_ab = call(middle_sum, [pair, pair], [], index, exchange(send, Z), own)
    slip, block, send = call(
        functools.partial(middle_update, rates),
        [(24, 128), (32, 256), wide],
        [(32, 256)],
        index,
        block,
        grad_c,
        grad_ab,
        swap(grad_ab),
    )
    send, own = step(exchange(send, XY), block, *targets)
    (send,) = call(last_pack, [(8, 24, 128)], [(32, 256)], index, exchange(send, XY), own)
    (grad,) = call(last_sum, [(24, 128)], [], index, exchange(send, Z))
    new_a, new_bt, new_c = call(
        functools.partial(last_update, rates),
        [(n_i, 16), (16, n_j), third_factor.shape],
        [square],
        index,
        slip,
        grad,
        swap(grad),
    )
    return (new_a, new_bt.T, new_c)


def solution(mesh):
    fine = Mesh(mesh.devices.reshape(2, 4, 2, 4, 4), ("zl", "x", "core", "zh", "y"))
    rows, cols = ("zl", "x", "core"), ("zh", "y")
    in_specs = (P(rows, cols, None), P(rows, cols), P(cols, rows), P(rows + cols, None))
    out_specs = (P(rows, cols), P(cols, rows), P(rows + cols, None))
    return jax.shard_map(
        per_device, mesh=fine, in_specs=in_specs, out_specs=out_specs, check_vma=False
    )
```

```python
import functools

import jax
import jax.numpy as jnp
from jax import lax
from jax.experimental import pallas as pl
from jax.experimental.pallas import tpu as pltpu
from jax.sharding import Mesh, PartitionSpec as P

XY = ("x", "y")
Z = ("zl", "zh")
HIGH = lax.Precision.HIGHEST
F32 = jnp.float32


def exchange(parts, axis):
    shape = parts.shape
    got = lax.all_to_all(parts.reshape(-1, shape[2]), axis, 0, 0, tiled=True)
    return got.reshape(shape)


def swap(value):
    return lax.ppermute(value, "core", [(0, 1), (1, 0)])


def call(body, outs, scratch, index, *operands):
    vmem = pl.BlockSpec(memory_space=pltpu.VMEM)
    return pl.pallas_call(
        body,
        out_shape=[jax.ShapeDtypeStruct(s, F32) for s in outs],
        in_specs=[pl.BlockSpec(memory_space=pltpu.SMEM)] + [vmem] * len(operands),
        out_specs=[vmem] * len(outs),
        scratch_shapes=[pltpu.VMEM(s, F32) for s in scratch],
        compiler_params=pltpu.CompilerParams(vmem_limit_bytes=40 * 1024 * 1024),
    )(index, *operands)


def lanes(rows=16):
    return lax.broadcasted_iota(jnp.int32, (rows, 128), 1)


def split(value):
    top = value.astype(jnp.bfloat16)
    return top, (value - top.astype(F32)).astype(jnp.bfloat16)


def product(left, right, dims):
    (lt, lb), (rt, rb) = left, right
    dot = functools.partial(
        lax.dot_general, dimension_numbers=(dims, ((), ())), preferred_element_type=F32
    )
    return dot(lt, rt) + (dot(lt, rb) + dot(lb, rt))


def fill_slot(ref, p, value):
    ref[p, 16:24, 0:128] = value[0:8]
    ref[p, 16:24, 128:256] = value[8:16]


def slot(ref, p):
    v = ref[p, 16:24, :]
    return jnp.concatenate([v[:, 0:128], v[:, 128:256]], axis=0)


def send_block(block, out_ref, x):
    for p in range(16):
        out_ref[p, 0:16, :] = block[0:16]
        fill_slot(out_ref, p, jnp.where(x == p // 4, block[16:32, 0:128], block[16:32, 128:256]))


def slip_of(block, place, zl, zh):
    a = block[16:32, 0:128]
    b = block[16:32, 128:256]
    if zh:
        a = pltpu.roll(a, 128 - 32 * zh, 1)
    if not zl:
        b = pltpu.roll(b, 32, 1)
    at = lanes()
    second = (at // 32) % 2 == 1
    ab = jnp.where(at < 32, a, jnp.where(second, b, 0.0))
    c = block[2 * place : 2 * place + 2, :]
    return c, ab


def first_pack(index, own_ref, other_ref, out_ref, pad):
    even = index[2] == 0
    own, other = own_ref[0:32, 0:128], other_ref[0:32, 0:128]
    low, high = jnp.where(even, own, other), jnp.where(even, other, own)
    pad[...] = jnp.zeros((128, 128), F32)
    pad[0:16, :] = low[0:16]
    pad[16:32, :] = high[0:16]
    ab = pad[...].T[0:16, :] + pltpu.roll(low[16:32], 32, 1) + pltpu.roll(high[16:32], 96, 1)
    for p in range(8):
        out_ref[p, 0:8, :] = jnp.zeros((8, 128), F32)
        out_ref[p, 0:2, :] = own_ref[32:34, 0:128]
        out_ref[p, 2:4, :] = own_ref[32:34, 128:256]
        out_ref[p, 8:24, :] = ab


def block_from_slips(index, got_ref, block_ref, out_ref):
    zl, zh = index[0], index[3]
    for p in range(8):
        block_ref[2 * p : 2 * p + 2, 0:128] = got_ref[p, 0:2, :]
        block_ref[2 * p : 2 * p + 2, 128:256] = got_ref[p, 2:4, :]
    at = lanes()
    a = jnp.zeros((16, 128), F32)
    for q in range(4):
        v = jnp.where(at < 32, got_ref[zl * 4 + q, 8:24, :], 0.0)
        a = a + (pltpu.roll(v, 32 * q, 1) if q else v)
    second = (at // 32) % 2 == 1
    low = jnp.where(second, got_ref[zh, 8:24, :], 0.0)
    high = jnp.where(second, got_ref[4 + zh, 8:24, :], 0.0)
    block_ref[16:32, 0:128] = a
    block_ref[16:32, 128:256] = pltpu.roll(low, 96, 1) + high
    send_block(block_ref[...], out_ref, index[1])


def gradients(
    index, got_ref, block_ref, kept_ref, came_ref, out_ref, own_ref, turn, khatri, terms, first
):
    x, core, y = index[1], index[2], index[4]
    order = [i + 16 * core if i < 12 else i + 4 - 16 * core for i in range(24)]
    for q in range(4):
        v = jnp.where(y == q, block_ref[16:32, 0:128], slot(got_ref, x * 4 + q))
        turn[16 * q : 16 * q + 16, :] = v
        turn[64 + 16 * q : 80 + 16 * q, :] = pltpu.roll(v, 96, 1)
    turned = turn[...].T
    first[:, 0:128] = turned[0:32]
    first[:, 128:256] = turned[64:96]
    a = [first[pl.ds(i, 1), :] for i in order]
    for q in range(4):
        v = jnp.where(x == q, block_ref[16:32, 128:256], slot(got_ref, q * 4 + y))
        turn[32 * q : 32 * q + 16, :] = v
        turn[32 * q + 16 : 32 * q + 32, :] = pltpu.roll(v, 64, 1)
    turned = turn[...].T
    b = jnp.concatenate([turned[0:32], turned[32:64]], axis=1)
    for i in range(24):
        khatri[32 * i : 32 * i + 32, :] = a[i] * b
    c = split(got_ref[:, 0:16, :].reshape(256, 256))
    parts = split(khatri[...])
    model = product(parts, c, ((1,), (1,)))
    target = jnp.concatenate([kept_ref[...], came_ref[...]], axis=0)
    deriv = split(jax.nn.sigmoid(model) - target)
    terms[...] = product(deriv, c, ((1,), (0,)))
    grad_c = product(deriv, parts, ((0,), (0,)))
    grad_b = jnp.zeros((32, 256), F32)
    turn[...] = jnp.zeros((128, 128), F32)
    for i in range(24):
        term = terms[32 * i : 32 * i + 32, :]
        grad_b = grad_b + term * a[i]
        row = jnp.sum(term * b, axis=0, keepdims=True)
        turn[pl.ds(order[i], 1), :] = row[:, 0:128]
        turn[pl.ds(order[i] + 64, 1), :] = row[:, 128:256]
    turned = turn[...].T
    pieces_a = [
        turned[16 * q : 16 * q + 16] + pltpu.roll(turned[64 + 16 * q : 80 + 16 * q], 32, 1)
        for q in range(4)
    ]
    turn[...] = jnp.zeros((128, 128), F32)
    turn[0:32, :] = grad_b[:, 0:128]
    turn[32:64, :] = grad_b[:, 128:256]
    turned = turn[...].T
    pieces_b = [
        turned[32 * q : 32 * q + 16] + pltpu.roll(turned[32 * q + 16 : 32 * q + 32], 64, 1)
        for q in range(4)
    ]
    out_ref[:, 0:16, :] = grad_c.reshape(16, 16, 256)
    for p in range(16):
        fill_slot(out_ref, p, jnp.where(x == p // 4, pieces_a[p % 4], pieces_b[p // 4]))
    own_a, own_b = pieces_a[0], pieces_b[0]
    for q in range(1, 4):
        own_a = jnp.where(y == q, pieces_a[q], own_a)
        own_b = jnp.where(x == q, pieces_b[q], own_b)
    own_ref[:, 0:128] = own_a
    own_ref[:, 128:256] = own_b


def sum_xy(index, got_ref, own_ref):
    x, y = index[1], index[4]
    c = jnp.sum(got_ref[:, 0:16, :], axis=0)
    a, b = own_ref[:, 0:128], own_ref[:, 128:256]
    for q in range(4):
        a = a + jnp.where(y == q, 0.0, slot(got_ref, x * 4 + q))
        b = b + jnp.where(x == q, 0.0, slot(got_ref, q * 4 + y))
    return c, a, b


def middle_pack(index, got_ref, own_ref, out_ref, sum_ref):
    c, a, b = sum_xy(index, got_ref, own_ref)
    for p in range(8):
        out_ref[p, 0:16, :] = c
        fill_slot(out_ref, p, jnp.where(index[0] == p // 4, a, b))
    sum_ref[:, 0:128] = a
    sum_ref[:, 128:256] = b


def middle_sum(index, got_ref, own_ref, c_ref, ab_ref):
    zl, zh = index[0], index[3]
    c_ref[...] = jnp.sum(got_ref[:, 0:16, :], axis=0)
    a = own_ref[:, 0:128]
    for q in range(4):
        a = a + jnp.where(zh == q, 0.0, slot(got_ref, zl * 4 + q))
    ab_ref[:, 0:128] = a
    ab_ref[:, 128:256] = own_ref[:, 128:256] + slot(got_ref, (1 - zl) * 4 + zh)


def middle_update(rates, index, block_ref, c_ref, ab_ref, other_ref, slip_ref, block_out, out_ref, new):
    rate_a, rate_b, rate_c = rates
    ab = ab_ref[...] + other_ref[...]
    new[0:16, :] = block_ref[0:16, :] - rate_c * c_ref[...]
    new[16:32, 0:128] = block_ref[16:32, 0:128] - rate_a * ab[:, 0:128]
    new[16:32, 128:256] = block_ref[16:32, 128:256] - rate_b * ab[:, 128:256]
    block = new[...]
    block_out[...] = block
    send_block(block, out_ref, index[1])
    own = index[0] * 4 + index[3]
    c = jnp.zeros((2, 256), F32)
    ab = jnp.zeros((16, 128), F32)
    for p in range(8):
        c_p, ab_p = slip_of(block, p, p // 4, p % 4)
        c = jnp.where(own == p, c_p, c)
        ab = jnp.where(own == p, ab_p, ab)
    slip_ref[0:8, :] = jnp.zeros((8, 128), F32)
    slip_ref[0:2, :] = c[:, 0:128]
    slip_ref[2:4, :] = c[:, 128:256]
    slip_ref[8:24, :] = ab


def last_pack(index, got_ref, own_ref, out_ref, new):
    c, a, b = sum_xy(index, got_ref, own_ref)
    new[0:16, :] = c
    new[16:32, 0:128] = a
    new[16:32, 128:256] = b
    block = new[...]
    for p in range(8):
        c_p, ab_p = slip_of(block, p, p // 4, p % 4)
        out_ref[p, 0:8, :] = jnp.zeros((8, 128), F32)
        out_ref[p, 0:2, :] = c_p[:, 0:128]
        out_ref[p, 2:4, :] = c_p[:, 128:256]
        out_ref[p, 8:24, :] = ab_p


def last_sum(index, got_ref, slip_ref):
    zl, zh = index[0], index[3]
    c = got_ref[0, 0:8, :]
    for p in range(1, 8):
        c = c + got_ref[p, 0:8, :]
    a = got_ref[zl * 4, 8:24, :]
    for q in range(1, 4):
        a = a + got_ref[zl * 4 + q, 8:24, :]
    b = got_ref[zh, 8:24, :] + got_ref[4 + zh, 8:24, :]
    slip_ref[0:8, :] = c
    slip_ref[8:24, :] = jnp.where(lanes() < 32, a, b)


def last_update(rates, index, old_ref, grad_ref, other_ref, a_ref, bt_ref, c_ref, pad):
    rate_a, rate_b, rate_c = rates
    core = index[2]
    c = old_ref[0:8, :] - rate_c * grad_ref[0:8, :]
    c_ref[:, 0:128] = c[0:2, :]
    c_ref[:, 128:256] = c[2:4, :]
    rate = jnp.where(lanes() < 32, rate_a, rate_b)
    ab = old_ref[8:24, :] - rate * (grad_ref[8:24, :] + other_ref[8:24, :])
    b = jnp.where(core == 0, pltpu.roll(ab, 96, 1), pltpu.roll(ab, 32, 1))
    bt_ref[...] = b[:, 0:32]
    pad[...] = jnp.zeros((128, 128), F32)
    pad[0:16, :] = jnp.where(core == 0, ab, pltpu.roll(ab, 112, 1))
    turned = pad[...].T
    a_ref[...] = turned[0:12, 0:16]


def arrange(index, after_ref, own_ref, other_ref, kept_ref, came_ref):
    del after_ref
    spot = lax.broadcasted_iota(jnp.int32, (512, 256), 1)
    xs, ys = spot // 64, (spot // 16) % 4
    zls, zhs, us = (spot // 8) % 2, (spot // 2) % 4, spot % 2
    source = zls * 256 + xs * 64 + index[2] * 32 + zhs * 8 + ys * 2 + us
    here = lax.broadcasted_iota(jnp.int32, (512, 256), 0)
    pick = jnp.where(here == source, 1.0, 0.0).astype(jnp.bfloat16)
    for from_ref, to_ref in ((own_ref, kept_ref), (other_ref, came_ref)):
        rest = from_ref[...]
        total = jnp.zeros((384, 256), F32)
        for _ in range(3):
            part = rest.astype(jnp.bfloat16)
            rest = rest - part.astype(F32)
            total = total + jnp.dot(part, pick, preferred_element_type=F32)
        to_ref[...] = total


def per_device(tensor, first_factor, second_factor, third_factor):
    index = jnp.stack([lax.axis_index(n) for n in ("zl", "x", "core", "zh", "y")])
    n_i, n_j, depth = tensor.shape
    size_i, size_j = n_i * 16, n_j * 16
    rates = tuple(4.0 / float(n) ** 0.5 for n in (size_j * depth, size_i * depth, size_i * size_j))
    wide = (16, 24, 256)
    square, pair = (128, 128), (16, 256)

    flat = tensor.reshape(-1, depth)
    arguments = (first_factor, 16), (second_factor.T, 16), (third_factor, 8)
    shards = jnp.concatenate(
        [jnp.pad(v, ((0, n - v.shape[0]), (0, 256 - v.shape[1]))) for v, n in arguments]
    )
    shards_other = swap(shards)
    flat, shards_other = lax.optimization_barrier((flat, shards_other))
    flat_other = swap(flat)
    (send,) = call(first_pack, [(8, 24, 128)], [square], index, shards, shards_other)
    block, send = call(block_from_slips, [(32, 256), wide], [], index, exchange(send, Z))
    targets = call(arrange, [(384, 256), (384, 256)], [], index, block, flat, flat_other)
    step = functools.partial(
        call, gradients, [wide, pair], [square, (768, 256), (768, 256), (32, 256)], index
    )

    send, own = step(exchange(send, XY), block, *targets)
    send, own = call(middle_pack, [(8, 24, 256), pair], [], index, exchange(send, XY), own)
    grad_c, grad_ab = call(middle_sum, [pair, pair], [], index, exchange(send, Z), own)
    slip, block, send = call(
        functools.partial(middle_update, rates),
        [(24, 128), (32, 256), wide],
        [(32, 256)],
        index,
        block,
        grad_c,
        grad_ab,
        swap(grad_ab),
    )
    send, own = step(exchange(send, XY), block, *targets)
    (send,) = call(last_pack, [(8, 24, 128)], [(32, 256)], index, exchange(send, XY), own)
    (grad,) = call(last_sum, [(24, 128)], [], index, exchange(send, Z))
    new_a, new_bt, new_c = call(
        functools.partial(last_update, rates),
        [(n_i, 16), (16, n_j), third_factor.shape],
        [square],
        index,
        slip,
        grad,
        swap(grad),
    )
    return (new_a, new_bt.T, new_c)


def solution(mesh):
    fine = Mesh(mesh.devices.reshape(2, 4, 2, 4, 4), ("zl", "x", "core", "zh", "y"))
    rows, cols = ("zl", "x", "core"), ("zh", "y")
    in_specs = (P(rows, cols, None), P(rows, cols), P(cols, rows), P(rows + cols, None))
    out_specs = (P(rows, cols), P(cols, rows), P(rows + cols, None))
    return jax.shard_map(
        per_device, mesh=fine, in_specs=in_specs, out_specs=out_specs, check_vma=False
    )
```

```python
import functools

import jax
import jax.numpy as jnp
from jax import lax
from jax.experimental import pallas as pl
from jax.experimental.pallas import tpu as pltpu
from jax.sharding import Mesh, PartitionSpec as P

XY = ("x", "y")
Z = ("zl", "zh")
HIGH = lax.Precision.HIGHEST
F32 = jnp.float32


def exchange(parts, axis):
    shape = parts.shape
    got = lax.all_to_all(parts.reshape(-1, shape[2]), axis, 0, 0, tiled=True)
    return got.reshape(shape)


def swap(value):
    return lax.ppermute(value, "core", [(0, 1), (1, 0)])


def call(body, outs, scratch, index, *operands):
    vmem = pl.BlockSpec(memory_space=pltpu.VMEM)
    return pl.pallas_call(
        body,
        out_shape=[jax.ShapeDtypeStruct(s, F32) for s in outs],
        in_specs=[pl.BlockSpec(memory_space=pltpu.SMEM)] + [vmem] * len(operands),
        out_specs=[vmem] * len(outs),
        scratch_shapes=[pltpu.VMEM(s, F32) for s in scratch],
        compiler_params=pltpu.CompilerParams(vmem_limit_bytes=40 * 1024 * 1024),
    )(index, *operands)


def lanes(rows=16):
    return lax.broadcasted_iota(jnp.int32, (rows, 128), 1)


def split(value):
    top = value.astype(jnp.bfloat16)
    return top, (value - top.astype(F32)).astype(jnp.bfloat16)


def product(left, right, dims):
    (lt, lb), (rt, rb) = left, right
    dot = functools.partial(
        lax.dot_general, dimension_numbers=(dims, ((), ())), preferred_element_type=F32
    )
    return dot(lt, rt) + (dot(lt, rb) + dot(lb, rt))


def fill_slot(ref, p, value):
    ref[p, 16:24, 0:128] = value[0:8]
    ref[p, 16:24, 128:256] = value[8:16]


def slot(ref, p):
    v = ref[p, 16:24, :]
    return jnp.concatenate([v[:, 0:128], v[:, 128:256]], axis=0)


def send_block(block, out_ref, x):
    for p in range(16):
        out_ref[p, 0:16, :] = block[0:16]
        fill_slot(out_ref, p, jnp.where(x == p // 4, block[16:32, 0:128], block[16:32, 128:256]))


def slip_of(block, place, zl, zh):
    a = block[16:32, 0:128]
    b = block[16:32, 128:256]
    if zh:
        a = pltpu.roll(a, 128 - 32 * zh, 1)
    if not zl:
        b = pltpu.roll(b, 32, 1)
    at = lanes()
    second = (at // 32) % 2 == 1
    ab = jnp.where(at < 32, a, jnp.where(second, b, 0.0))
    c = block[2 * place : 2 * place + 2, :]
    return c, ab


def first_pack(index, own_ref, other_ref, out_ref, pad):
    even = index[2] == 0
    own, other = own_ref[0:32, 0:128], other_ref[0:32, 0:128]
    low, high = jnp.where(even, own, other), jnp.where(even, other, own)
    pad[...] = jnp.zeros((128, 128), F32)
    pad[0:16, :] = low[0:16]
    pad[16:32, :] = high[0:16]
    ab = pad[...].T[0:16, :] + pltpu.roll(low[16:32], 32, 1) + pltpu.roll(high[16:32], 96, 1)
    for p in range(8):
        out_ref[p, 0:8, :] = jnp.zeros((8, 128), F32)
        out_ref[p, 0:2, :] = own_ref[32:34, 0:128]
        out_ref[p, 2:4, :] = own_ref[32:34, 128:256]
        out_ref[p, 8:24, :] = ab


def block_from_slips(index, got_ref, block_ref, out_ref):
    zl, zh = index[0], index[3]
    for p in range(8):
        block_ref[2 * p : 2 * p + 2, 0:128] = got_ref[p, 0:2, :]
        block_ref[2 * p : 2 * p + 2, 128:256] = got_ref[p, 2:4, :]
    at = lanes()
    a = jnp.zeros((16, 128), F32)
    for q in range(4):
        v = jnp.where(at < 32, got_ref[zl * 4 + q, 8:24, :], 0.0)
        a = a + (pltpu.roll(v, 32 * q, 1) if q else v)
    second = (at // 32) % 2 == 1
    low = jnp.where(second, got_ref[zh, 8:24, :], 0.0)
    high = jnp.where(second, got_ref[4 + zh, 8:24, :], 0.0)
    block_ref[16:32, 0:128] = a
    block_ref[16:32, 128:256] = pltpu.roll(low, 96, 1) + high
    send_block(block_ref[...], out_ref, index[1])


def gradients(
    index, got_ref, block_ref, kept_ref, came_ref, out_ref, own_ref, turn, khatri, terms, first
):
    x, core, y = index[1], index[2], index[4]
    order = [i + 16 * core if i < 12 else i + 4 - 16 * core for i in range(24)]
    for q in range(4):
        v = jnp.where(y == q, block_ref[16:32, 0:128], slot(got_ref, x * 4 + q))
        turn[16 * q : 16 * q + 16, :] = v
        turn[64 + 16 * q : 80 + 16 * q, :] = pltpu.roll(v, 96, 1)
    turned = turn[...].T
    first[:, 0:128] = turned[0:32]
    first[:, 128:256] = turned[64:96]
    a = [first[pl.ds(i, 1), :] for i in order]
    for q in range(4):
        v = jnp.where(x == q, block_ref[16:32, 128:256], slot(got_ref, q * 4 + y))
        turn[32 * q : 32 * q + 16, :] = v
        turn[32 * q + 16 : 32 * q + 32, :] = pltpu.roll(v, 64, 1)
    turned = turn[...].T
    b = jnp.concatenate([turned[0:32], turned[32:64]], axis=1)
    for i in range(24):
        khatri[32 * i : 32 * i + 32, :] = a[i] * b
    c = got_ref[:, 0:16, :].reshape(256, 256)
    c, turned_c = split(c), split(c.T)
    parts = split(khatri[...])
    model = product(parts, turned_c, ((1,), (0,)))
    target = jnp.concatenate([kept_ref[...], came_ref[...]], axis=0)
    deriv = split(jax.nn.sigmoid(model) - target)
    terms[...] = product(deriv, c, ((1,), (0,)))
    grad_c = product(deriv, parts, ((0,), (0,)))
    grad_b = jnp.zeros((32, 256), F32)
    turn[...] = jnp.zeros((128, 128), F32)
    for i in range(24):
        term = terms[32 * i : 32 * i + 32, :]
        grad_b = grad_b + term * a[i]
        row = jnp.sum(term * b, axis=0, keepdims=True)
        turn[pl.ds(order[i], 1), :] = row[:, 0:128]
        turn[pl.ds(order[i] + 64, 1), :] = row[:, 128:256]
    turned = turn[...].T
    pieces_a = [
        turned[16 * q : 16 * q + 16] + pltpu.roll(turned[64 + 16 * q : 80 + 16 * q], 32, 1)
        for q in range(4)
    ]
    turn[...] = jnp.zeros((128, 128), F32)
    turn[0:32, :] = grad_b[:, 0:128]
    turn[32:64, :] = grad_b[:, 128:256]
    turned = turn[...].T
    pieces_b = [
        turned[32 * q : 32 * q + 16] + pltpu.roll(turned[32 * q + 16 : 32 * q + 32], 64, 1)
        for q in range(4)
    ]
    out_ref[:, 0:16, :] = grad_c.reshape(16, 16, 256)
    for p in range(16):
        fill_slot(out_ref, p, jnp.where(x == p // 4, pieces_a[p % 4], pieces_b[p // 4]))
    own_a, own_b = pieces_a[0], pieces_b[0]
    for q in range(1, 4):
        own_a = jnp.where(y == q, pieces_a[q], own_a)
        own_b = jnp.where(x == q, pieces_b[q], own_b)
    own_ref[:, 0:128] = own_a
    own_ref[:, 128:256] = own_b


def sum_xy(index, got_ref, own_ref):
    x, y = index[1], index[4]
    c = jnp.sum(got_ref[:, 0:16, :], axis=0)
    a, b = own_ref[:, 0:128], own_ref[:, 128:256]
    for q in range(4):
        a = a + jnp.where(y == q, 0.0, slot(got_ref, x * 4 + q))
        b = b + jnp.where(x == q, 0.0, slot(got_ref, q * 4 + y))
    return c, a, b


def middle_pack(index, got_ref, own_ref, out_ref, sum_ref):
    c, a, b = sum_xy(index, got_ref, own_ref)
    for p in range(8):
        out_ref[p, 0:16, :] = c
        fill_slot(out_ref, p, jnp.where(index[0] == p // 4, a, b))
    sum_ref[:, 0:128] = a
    sum_ref[:, 128:256] = b


def middle_sum(index, got_ref, own_ref, c_ref, ab_ref):
    zl, zh = index[0], index[3]
    c_ref[...] = jnp.sum(got_ref[:, 0:16, :], axis=0)
    a = own_ref[:, 0:128]
    for q in range(4):
        a = a + jnp.where(zh == q, 0.0, slot(got_ref, zl * 4 + q))
    ab_ref[:, 0:128] = a
    ab_ref[:, 128:256] = own_ref[:, 128:256] + slot(got_ref, (1 - zl) * 4 + zh)


def middle_update(rates, index, block_ref, c_ref, ab_ref, other_ref, slip_ref, block_out, out_ref, new):
    rate_a, rate_b, rate_c = rates
    ab = ab_ref[...] + other_ref[...]
    new[0:16, :] = block_ref[0:16, :] - rate_c * c_ref[...]
    new[16:32, 0:128] = block_ref[16:32, 0:128] - rate_a * ab[:, 0:128]
    new[16:32, 128:256] = block_ref[16:32, 128:256] - rate_b * ab[:, 128:256]
    block = new[...]
    block_out[...] = block
    send_block(block, out_ref, index[1])
    own = index[0] * 4 + index[3]
    c = jnp.zeros((2, 256), F32)
    ab = jnp.zeros((16, 128), F32)
    for p in range(8):
        c_p, ab_p = slip_of(block, p, p // 4, p % 4)
        c = jnp.where(own == p, c_p, c)
        ab = jnp.where(own == p, ab_p, ab)
    slip_ref[0:8, :] = jnp.zeros((8, 128), F32)
    slip_ref[0:2, :] = c[:, 0:128]
    slip_ref[2:4, :] = c[:, 128:256]
    slip_ref[8:24, :] = ab


def last_pack(index, got_ref, own_ref, out_ref, new):
    c, a, b = sum_xy(index, got_ref, own_ref)
    new[0:16, :] = c
    new[16:32, 0:128] = a
    new[16:32, 128:256] = b
    block = new[...]
    for p in range(8):
        c_p, ab_p = slip_of(block, p, p // 4, p % 4)
        out_ref[p, 0:8, :] = jnp.zeros((8, 128), F32)
        out_ref[p, 0:2, :] = c_p[:, 0:128]
        out_ref[p, 2:4, :] = c_p[:, 128:256]
        out_ref[p, 8:24, :] = ab_p


def last_sum(index, got_ref, slip_ref):
    zl, zh = index[0], index[3]
    c = got_ref[0, 0:8, :]
    for p in range(1, 8):
        c = c + got_ref[p, 0:8, :]
    a = got_ref[zl * 4, 8:24, :]
    for q in range(1, 4):
        a = a + got_ref[zl * 4 + q, 8:24, :]
    b = got_ref[zh, 8:24, :] + got_ref[4 + zh, 8:24, :]
    slip_ref[0:8, :] = c
    slip_ref[8:24, :] = jnp.where(lanes() < 32, a, b)


def last_update(rates, index, old_ref, grad_ref, other_ref, a_ref, bt_ref, c_ref, pad):
    rate_a, rate_b, rate_c = rates
    core = index[2]
    c = old_ref[0:8, :] - rate_c * grad_ref[0:8, :]
    c_ref[:, 0:128] = c[0:2, :]
    c_ref[:, 128:256] = c[2:4, :]
    rate = jnp.where(lanes() < 32, rate_a, rate_b)
    ab = old_ref[8:24, :] - rate * (grad_ref[8:24, :] + other_ref[8:24, :])
    b = jnp.where(core == 0, pltpu.roll(ab, 96, 1), pltpu.roll(ab, 32, 1))
    bt_ref[...] = b[:, 0:32]
    pad[...] = jnp.zeros((128, 128), F32)
    pad[0:16, :] = jnp.where(core == 0, ab, pltpu.roll(ab, 112, 1))
    turned = pad[...].T
    a_ref[...] = turned[0:12, 0:16]


def arrange(index, flat_ref, kept_ref, sent_ref):
    spot = lax.broadcasted_iota(jnp.int32, (512, 256), 1)
    xs, ys = spot // 64, (spot // 16) % 4
    zls, zhs, us = (spot // 8) % 2, (spot // 2) % 4, spot % 2
    source = zls * 256 + xs * 64 + zhs * 8 + ys * 2 + us
    gap = lax.broadcasted_iota(jnp.int32, (512, 256), 0) - source
    own, other = index[2] * 32, 32 - index[2] * 32
    picks = [jnp.where(gap == n, 1.0, 0.0).astype(jnp.bfloat16) for n in (own, other)]
    totals = [jnp.zeros((384, 256), F32)] * 2
    rest = flat_ref[...]
    for _ in range(3):
        part = rest.astype(jnp.bfloat16)
        rest = rest - part.astype(F32)
        totals = [
            t + jnp.dot(part, pick, preferred_element_type=F32) for t, pick in zip(totals, picks)
        ]
    kept_ref[...], sent_ref[...] = totals


def per_device(tensor, first_factor, second_factor, third_factor):
    index = jnp.stack([lax.axis_index(n) for n in ("zl", "x", "core", "zh", "y")])
    n_i, n_j, depth = tensor.shape
    size_i, size_j = n_i * 16, n_j * 16
    rates = tuple(4.0 / float(n) ** 0.5 for n in (size_j * depth, size_i * depth, size_i * size_j))
    wide = (16, 24, 256)
    square, pair = (128, 128), (16, 256)

    flat = tensor.reshape(-1, depth)
    arguments = (first_factor, 16), (second_factor.T, 16), (third_factor, 8)
    shards = jnp.concatenate(
        [jnp.pad(v, ((0, n - v.shape[0]), (0, 256 - v.shape[1]))) for v, n in arguments]
    )
    kept, sent = call(arrange, [(384, 256), (384, 256)], [], index, flat)
    sent, shards_other = lax.optimization_barrier((sent, swap(shards)))
    came = swap(sent)
    (send,) = call(first_pack, [(8, 24, 128)], [square], index, shards, shards_other)
    got, came = lax.optimization_barrier((exchange(send, Z), came))
    block, send = call(block_from_slips, [(32, 256), wide], [], index, got)
    targets = kept, came
    step = functools.partial(
        call, gradients, [wide, pair], [square, (768, 256), (768, 256), (32, 256)], index
    )

    send, own = step(exchange(send, XY), block, *targets)
    send, own = call(middle_pack, [(8, 24, 256), pair], [], index, exchange(send, XY), own)
    grad_c, grad_ab = call(middle_sum, [pair, pair], [], index, exchange(send, Z), own)
    slip, block, send = call(
        functools.partial(middle_update, rates),
        [(24, 128), (32, 256), wide],
        [(32, 256)],
        index,
        block,
        grad_c,
        grad_ab,
        swap(grad_ab),
    )
    send, own = step(exchange(send, XY), block, *targets)
    (send,) = call(last_pack, [(8, 24, 128)], [(32, 256)], index, exchange(send, XY), own)
    (grad,) = call(last_sum, [(24, 128)], [], index, exchange(send, Z))
    new_a, new_bt, new_c = call(
        functools.partial(last_update, rates),
        [(n_i, 16), (16, n_j), third_factor.shape],
        [square],
        index,
        slip,
        grad,
        swap(grad),
    )
    return (new_a, new_bt.T, new_c)


def solution(mesh):
    fine = Mesh(mesh.devices.reshape(2, 4, 2, 4, 4), ("zl", "x", "core", "zh", "y"))
    rows, cols = ("zl", "x", "core"), ("zh", "y")
    in_specs = (P(rows, cols, None), P(rows, cols), P(cols, rows), P(rows + cols, None))
    out_specs = (P(rows, cols), P(cols, rows), P(rows + cols, None))
    return jax.shard_map(
        per_device, mesh=fine, in_specs=in_specs, out_specs=out_specs, check_vma=False
    )
```

```python
import functools

import jax
import jax.numpy as jnp
from jax import lax
from jax.experimental import pallas as pl
from jax.experimental.pallas import tpu as pltpu
from jax.sharding import Mesh, PartitionSpec as P

XY = ("x", "y")
Z = ("zl", "zh")
HIGH = lax.Precision.HIGHEST
F32 = jnp.float32


def exchange(parts, axis):
    shape = parts.shape
    got = lax.all_to_all(parts.reshape(-1, shape[2]), axis, 0, 0, tiled=True)
    return got.reshape(shape)


def swap(value):
    return lax.ppermute(value, "core", [(0, 1), (1, 0)])


def call(body, outs, scratch, index, *operands):
    vmem = pl.BlockSpec(memory_space=pltpu.VMEM)
    return pl.pallas_call(
        body,
        out_shape=[jax.ShapeDtypeStruct(s, F32) for s in outs],
        in_specs=[pl.BlockSpec(memory_space=pltpu.SMEM)] + [vmem] * len(operands),
        out_specs=[vmem] * len(outs),
        scratch_shapes=[pltpu.VMEM(s, F32) for s in scratch],
        compiler_params=pltpu.CompilerParams(vmem_limit_bytes=40 * 1024 * 1024),
    )(index, *operands)


def lanes(rows=16):
    return lax.broadcasted_iota(jnp.int32, (rows, 128), 1)


def split(value):
    top = value.astype(jnp.bfloat16)
    return top, (value - top.astype(F32)).astype(jnp.bfloat16)


def product(left, right, dims):
    (lt, lb), (rt, rb) = left, right
    dot = functools.partial(
        lax.dot_general, dimension_numbers=(dims, ((), ())), preferred_element_type=F32
    )
    return dot(lt, rt) + (dot(lt, rb) + dot(lb, rt))


def fill_slot(ref, p, value):
    ref[p, 16:24, 0:128] = value[0:8]
    ref[p, 16:24, 128:256] = value[8:16]


def slot(ref, p):
    v = ref[p, 16:24, :]
    return jnp.concatenate([v[:, 0:128], v[:, 128:256]], axis=0)


def send_block(block, out_ref, x):
    for p in range(16):
        out_ref[p, 0:16, :] = block[0:16]
        fill_slot(out_ref, p, jnp.where(x == p // 4, block[16:32, 0:128], block[16:32, 128:256]))


def slip_of(block, place, zl, zh):
    a = block[16:32, 0:128]
    b = block[16:32, 128:256]
    if zh:
        a = pltpu.roll(a, 128 - 32 * zh, 1)
    if not zl:
        b = pltpu.roll(b, 32, 1)
    at = lanes()
    second = (at // 32) % 2 == 1
    ab = jnp.where(at < 32, a, jnp.where(second, b, 0.0))
    c = block[2 * place : 2 * place + 2, :]
    return c, ab


def first_pack(index, own_ref, other_ref, out_ref, done_ref, pad):
    even = index[2] == 0
    own, other = own_ref[0:32, 0:128], other_ref[0:32, 0:128]
    low, high = jnp.where(even, own, other), jnp.where(even, other, own)
    pad[...] = jnp.zeros((128, 128), F32)
    pad[0:16, :] = low[0:16]
    pad[16:32, :] = high[0:16]
    ab = pad[...].T[0:16, :] + pltpu.roll(low[16:32], 32, 1) + pltpu.roll(high[16:32], 96, 1)
    for p in range(8):
        out_ref[p, 0:8, :] = jnp.zeros((8, 128), F32)
        out_ref[p, 0:2, :] = own_ref[32:34, 0:128]
        out_ref[p, 2:4, :] = own_ref[32:34, 128:256]
        out_ref[p, 8:24, :] = ab
    done_ref[...] = ab


def block_from_slips(index, got_ref, block_ref, out_ref):
    zl, zh = index[0], index[3]
    for p in range(8):
        block_ref[2 * p : 2 * p + 2, 0:128] = got_ref[p, 0:2, :]
        block_ref[2 * p : 2 * p + 2, 128:256] = got_ref[p, 2:4, :]
    at = lanes()
    a = jnp.zeros((16, 128), F32)
    for q in range(4):
        v = jnp.where(at < 32, got_ref[zl * 4 + q, 8:24, :], 0.0)
        a = a + (pltpu.roll(v, 32 * q, 1) if q else v)
    second = (at // 32) % 2 == 1
    low = jnp.where(second, got_ref[zh, 8:24, :], 0.0)
    high = jnp.where(second, got_ref[4 + zh, 8:24, :], 0.0)
    block_ref[16:32, 0:128] = a
    block_ref[16:32, 128:256] = pltpu.roll(low, 96, 1) + high
    send_block(block_ref[...], out_ref, index[1])


def gradients(
    index, got_ref, block_ref, kept_ref, came_ref, out_ref, own_ref, turn, khatri, terms, first
):
    x, core, y = index[1], index[2], index[4]
    order = [i + 16 * core if i < 12 else i + 4 - 16 * core for i in range(24)]
    for q in range(4):
        v = jnp.where(y == q, block_ref[16:32, 0:128], slot(got_ref, x * 4 + q))
        turn[16 * q : 16 * q + 16, :] = v
        turn[64 + 16 * q : 80 + 16 * q, :] = pltpu.roll(v, 96, 1)
    turned = turn[...].T
    first[:, 0:128] = turned[0:32]
    first[:, 128:256] = turned[64:96]
    a = [first[pl.ds(i, 1), :] for i in order]
    for q in range(4):
        v = jnp.where(x == q, block_ref[16:32, 128:256], slot(got_ref, q * 4 + y))
        turn[32 * q : 32 * q + 16, :] = v
        turn[32 * q + 16 : 32 * q + 32, :] = pltpu.roll(v, 64, 1)
    turned = turn[...].T
    b = jnp.concatenate([turned[0:32], turned[32:64]], axis=1)
    for i in range(24):
        khatri[32 * i : 32 * i + 32, :] = a[i] * b
    c = got_ref[:, 0:16, :].reshape(256, 256)
    c, turned_c = split(c), split(c.T)
    parts = split(khatri[...])
    model = product(parts, turned_c, ((1,), (0,)))
    target = jnp.concatenate([kept_ref[...], came_ref[...]], axis=0)
    deriv = split(jax.nn.sigmoid(model) - target)
    terms[...] = product(deriv, c, ((1,), (0,)))
    grad_c = product(deriv, parts, ((0,), (0,)))
    grad_b = jnp.zeros((32, 256), F32)
    turn[...] = jnp.zeros((128, 128), F32)
    for i in range(24):
        term = terms[32 * i : 32 * i + 32, :]
        grad_b = grad_b + term * a[i]
        row = jnp.sum(term * b, axis=0, keepdims=True)
        turn[pl.ds(order[i], 1), :] = row[:, 0:128]
        turn[pl.ds(order[i] + 64, 1), :] = row[:, 128:256]
    turned = turn[...].T
    pieces_a = [
        turned[16 * q : 16 * q + 16] + pltpu.roll(turned[64 + 16 * q : 80 + 16 * q], 32, 1)
        for q in range(4)
    ]
    turn[...] = jnp.zeros((128, 128), F32)
    turn[0:32, :] = grad_b[:, 0:128]
    turn[32:64, :] = grad_b[:, 128:256]
    turned = turn[...].T
    pieces_b = [
        turned[32 * q : 32 * q + 16] + pltpu.roll(turned[32 * q + 16 : 32 * q + 32], 64, 1)
        for q in range(4)
    ]
    out_ref[:, 0:16, :] = grad_c.reshape(16, 16, 256)
    for p in range(16):
        fill_slot(out_ref, p, jnp.where(x == p // 4, pieces_a[p % 4], pieces_b[p // 4]))
    own_a, own_b = pieces_a[0], pieces_b[0]
    for q in range(1, 4):
        own_a = jnp.where(y == q, pieces_a[q], own_a)
        own_b = jnp.where(x == q, pieces_b[q], own_b)
    own_ref[:, 0:128] = own_a
    own_ref[:, 128:256] = own_b


def sum_xy(index, got_ref, own_ref):
    x, y = index[1], index[4]
    c = jnp.sum(got_ref[:, 0:16, :], axis=0)
    a, b = own_ref[:, 0:128], own_ref[:, 128:256]
    for q in range(4):
        a = a + jnp.where(y == q, 0.0, slot(got_ref, x * 4 + q))
        b = b + jnp.where(x == q, 0.0, slot(got_ref, q * 4 + y))
    return c, a, b


def middle_pack(index, got_ref, own_ref, out_ref, sum_ref):
    c, a, b = sum_xy(index, got_ref, own_ref)
    for p in range(8):
        out_ref[p, 0:16, :] = c
        fill_slot(out_ref, p, jnp.where(index[0] == p // 4, a, b))
    sum_ref[:, 0:128] = a
    sum_ref[:, 128:256] = b


def middle_sum(index, got_ref, own_ref, c_ref, ab_ref):
    zl, zh = index[0], index[3]
    c_ref[...] = jnp.sum(got_ref[:, 0:16, :], axis=0)
    a = own_ref[:, 0:128]
    for q in range(4):
        a = a + jnp.where(zh == q, 0.0, slot(got_ref, zl * 4 + q))
    ab_ref[:, 0:128] = a
    ab_ref[:, 128:256] = own_ref[:, 128:256] + slot(got_ref, (1 - zl) * 4 + zh)


def middle_update(rates, index, block_ref, c_ref, ab_ref, other_ref, slip_ref, block_out, out_ref, new):
    rate_a, rate_b, rate_c = rates
    ab = ab_ref[...] + other_ref[...]
    new[0:16, :] = block_ref[0:16, :] - rate_c * c_ref[...]
    new[16:32, 0:128] = block_ref[16:32, 0:128] - rate_a * ab[:, 0:128]
    new[16:32, 128:256] = block_ref[16:32, 128:256] - rate_b * ab[:, 128:256]
    block = new[...]
    block_out[...] = block
    send_block(block, out_ref, index[1])
    own = index[0] * 4 + index[3]
    c = jnp.zeros((2, 256), F32)
    ab = jnp.zeros((16, 128), F32)
    for p in range(8):
        c_p, ab_p = slip_of(block, p, p // 4, p % 4)
        c = jnp.where(own == p, c_p, c)
        ab = jnp.where(own == p, ab_p, ab)
    slip_ref[0:8, :] = jnp.zeros((8, 128), F32)
    slip_ref[0:2, :] = c[:, 0:128]
    slip_ref[2:4, :] = c[:, 128:256]
    slip_ref[8:24, :] = ab


def last_pack(index, got_ref, own_ref, out_ref, new):
    c, a, b = sum_xy(index, got_ref, own_ref)
    new[0:16, :] = c
    new[16:32, 0:128] = a
    new[16:32, 128:256] = b
    block = new[...]
    for p in range(8):
        c_p, ab_p = slip_of(block, p, p // 4, p % 4)
        out_ref[p, 0:8, :] = jnp.zeros((8, 128), F32)
        out_ref[p, 0:2, :] = c_p[:, 0:128]
        out_ref[p, 2:4, :] = c_p[:, 128:256]
        out_ref[p, 8:24, :] = ab_p


def last_sum(index, got_ref, slip_ref):
    zl, zh = index[0], index[3]
    c = got_ref[0, 0:8, :]
    for p in range(1, 8):
        c = c + got_ref[p, 0:8, :]
    a = got_ref[zl * 4, 8:24, :]
    for q in range(1, 4):
        a = a + got_ref[zl * 4 + q, 8:24, :]
    b = got_ref[zh, 8:24, :] + got_ref[4 + zh, 8:24, :]
    slip_ref[0:8, :] = c
    slip_ref[8:24, :] = jnp.where(lanes() < 32, a, b)


def last_update(rates, index, old_ref, grad_ref, other_ref, a_ref, bt_ref, c_ref, pad):
    rate_a, rate_b, rate_c = rates
    core = index[2]
    c = old_ref[0:8, :] - rate_c * grad_ref[0:8, :]
    c_ref[:, 0:128] = c[0:2, :]
    c_ref[:, 128:256] = c[2:4, :]
    rate = jnp.where(lanes() < 32, rate_a, rate_b)
    ab = old_ref[8:24, :] - rate * (grad_ref[8:24, :] + other_ref[8:24, :])
    b = jnp.where(core == 0, pltpu.roll(ab, 96, 1), pltpu.roll(ab, 32, 1))
    bt_ref[...] = b[:, 0:32]
    pad[...] = jnp.zeros((128, 128), F32)
    pad[0:16, :] = jnp.where(core == 0, ab, pltpu.roll(ab, 112, 1))
    turned = pad[...].T
    a_ref[...] = turned[0:12, 0:16]


def arrange(index, after_ref, own_ref, other_ref, kept_ref, came_ref):
    del after_ref
    spot = lax.broadcasted_iota(jnp.int32, (512, 256), 1)
    xs, ys = spot // 64, (spot // 16) % 4
    zls, zhs, us = (spot // 8) % 2, (spot // 2) % 4, spot % 2
    source = zls * 256 + xs * 64 + index[2] * 32 + zhs * 8 + ys * 2 + us
    here = lax.broadcasted_iota(jnp.int32, (512, 256), 0)
    pick = jnp.where(here == source, 1.0, 0.0).astype(jnp.bfloat16)
    for from_ref, to_ref in ((own_ref, kept_ref), (other_ref, came_ref)):
        rest = from_ref[...]
        total = jnp.zeros((384, 256), F32)
        for _ in range(3):
            part = rest.astype(jnp.bfloat16)
            rest = rest - part.astype(F32)
            total = total + jnp.dot(part, pick, preferred_element_type=F32)
        to_ref[...] = total


def per_device(tensor, first_factor, second_factor, third_factor):
    index = jnp.stack([lax.axis_index(n) for n in ("zl", "x", "core", "zh", "y")])
    n_i, n_j, depth = tensor.shape
    size_i, size_j = n_i * 16, n_j * 16
    rates = tuple(4.0 / float(n) ** 0.5 for n in (size_j * depth, size_i * depth, size_i * size_j))
    wide = (16, 24, 256)
    square, pair = (128, 128), (16, 256)

    flat = tensor.reshape(-1, depth)
    arguments = (first_factor, 16), (second_factor.T, 16), (third_factor, 8)
    shards = jnp.concatenate(
        [jnp.pad(v, ((0, n - v.shape[0]), (0, 256 - v.shape[1]))) for v, n in arguments]
    )
    shards_other = swap(shards)
    flat, shards_other = lax.optimization_barrier((flat, shards_other))
    flat_other = swap(flat)
    send, done = call(
        first_pack, [(8, 24, 128), (16, 128)], [square], index, shards, shards_other
    )
    targets = call(arrange, [(384, 256), (384, 256)], [], index, done, flat, flat_other)
    got, targets = lax.optimization_barrier((exchange(send, Z), targets))
    block, send = call(block_from_slips, [(32, 256), wide], [], index, got)
    step = functools.partial(
        call, gradients, [wide, pair], [square, (768, 256), (768, 256), (32, 256)], index
    )

    send, own = step(exchange(send, XY), block, *targets)
    send, own = call(middle_pack, [(8, 24, 256), pair], [], index, exchange(send, XY), own)
    grad_c, grad_ab = call(middle_sum, [pair, pair], [], index, exchange(send, Z), own)
    slip, block, send = call(
        functools.partial(middle_update, rates),
        [(24, 128), (32, 256), wide],
        [(32, 256)],
        index,
        block,
        grad_c,
        grad_ab,
        swap(grad_ab),
    )
    send, own = step(exchange(send, XY), block, *targets)
    (send,) = call(last_pack, [(8, 24, 128)], [(32, 256)], index, exchange(send, XY), own)
    (grad,) = call(last_sum, [(24, 128)], [], index, exchange(send, Z))
    new_a, new_bt, new_c = call(
        functools.partial(last_update, rates),
        [(n_i, 16), (16, n_j), third_factor.shape],
        [square],
        index,
        slip,
        grad,
        swap(grad),
    )
    return (new_a, new_bt.T, new_c)


def solution(mesh):
    fine = Mesh(mesh.devices.reshape(2, 4, 2, 4, 4), ("zl", "x", "core", "zh", "y"))
    rows, cols = ("zl", "x", "core"), ("zh", "y")
    in_specs = (P(rows, cols, None), P(rows, cols), P(cols, rows), P(rows + cols, None))
    out_specs = (P(rows, cols), P(cols, rows), P(rows + cols, None))
    return jax.shard_map(
        per_device, mesh=fine, in_specs=in_specs, out_specs=out_specs, check_vma=False
    )
```

```python
import functools

import jax
import jax.numpy as jnp
from jax import lax
from jax.experimental import pallas as pl
from jax.experimental.pallas import tpu as pltpu
from jax.sharding import Mesh, PartitionSpec as P

XY = ("x", "y")
Z = ("zl", "zh")
HIGH = lax.Precision.HIGHEST
F32 = jnp.float32


def exchange(parts, axis):
    shape = parts.shape
    got = lax.all_to_all(parts.reshape(-1, shape[2]), axis, 0, 0, tiled=True)
    return got.reshape(shape)


def swap(value):
    return lax.ppermute(value, "core", [(0, 1), (1, 0)])


def call(body, outs, scratch, *operands):
    def kernel(*refs):
        body([lax.axis_index(n) for n in ("zl", "x", "core", "zh", "y")], *refs)

    vmem = pl.BlockSpec(memory_space=pltpu.VMEM)
    return pl.pallas_call(
        kernel,
        out_shape=[jax.ShapeDtypeStruct(s, F32) for s in outs],
        in_specs=[vmem] * len(operands),
        out_specs=[vmem] * len(outs),
        scratch_shapes=[pltpu.VMEM(s, F32) for s in scratch],
        compiler_params=pltpu.CompilerParams(vmem_limit_bytes=40 * 1024 * 1024),
    )(*operands)


def lanes(rows=16):
    return lax.broadcasted_iota(jnp.int32, (rows, 128), 1)


def split(value):
    top = value.astype(jnp.bfloat16)
    return top, (value - top.astype(F32)).astype(jnp.bfloat16)


def product(left, right, dims):
    (lt, lb), (rt, rb) = left, right
    dot = functools.partial(
        lax.dot_general, dimension_numbers=(dims, ((), ())), preferred_element_type=F32
    )
    return dot(lt, rt) + (dot(lt, rb) + dot(lb, rt))


def fill_slot(ref, p, value):
    ref[p, 16:24, 0:128] = value[0:8]
    ref[p, 16:24, 128:256] = value[8:16]


def slot(ref, p):
    v = ref[p, 16:24, :]
    return jnp.concatenate([v[:, 0:128], v[:, 128:256]], axis=0)


def send_block(block, out_ref, x):
    for p in range(16):
        out_ref[p, 0:16, :] = block[0:16]
        fill_slot(out_ref, p, jnp.where(x == p // 4, block[16:32, 0:128], block[16:32, 128:256]))


def slip_of(block, place, zl, zh):
    a = block[16:32, 0:128]
    b = block[16:32, 128:256]
    if zh:
        a = pltpu.roll(a, 128 - 32 * zh, 1)
    if not zl:
        b = pltpu.roll(b, 32, 1)
    at = lanes()
    second = (at // 32) % 2 == 1
    ab = jnp.where(at < 32, a, jnp.where(second, b, 0.0))
    c = block[2 * place : 2 * place + 2, :]
    return c, ab


def first_pack(index, own_ref, other_ref, out_ref, done_ref, pad):
    even = index[2] == 0
    own, other = own_ref[0:32, 0:128], other_ref[0:32, 0:128]
    low, high = jnp.where(even, own, other), jnp.where(even, other, own)
    pad[...] = jnp.zeros((128, 128), F32)
    pad[0:16, :] = low[0:16]
    pad[16:32, :] = high[0:16]
    ab = pad[...].T[0:16, :] + pltpu.roll(low[16:32], 32, 1) + pltpu.roll(high[16:32], 96, 1)
    for p in range(8):
        out_ref[p, 0:8, :] = jnp.zeros((8, 128), F32)
        out_ref[p, 0:2, :] = own_ref[32:34, 0:128]
        out_ref[p, 2:4, :] = own_ref[32:34, 128:256]
        out_ref[p, 8:24, :] = ab
    done_ref[...] = ab


def block_from_slips(index, got_ref, block_ref, out_ref):
    zl, zh = index[0], index[3]
    for p in range(8):
        block_ref[2 * p : 2 * p + 2, 0:128] = got_ref[p, 0:2, :]
        block_ref[2 * p : 2 * p + 2, 128:256] = got_ref[p, 2:4, :]
    at = lanes()
    a = jnp.zeros((16, 128), F32)
    for q in range(4):
        v = jnp.where(at < 32, got_ref[zl * 4 + q, 8:24, :], 0.0)
        a = a + (pltpu.roll(v, 32 * q, 1) if q else v)
    second = (at // 32) % 2 == 1
    low = jnp.where(second, got_ref[zh, 8:24, :], 0.0)
    high = jnp.where(second, got_ref[4 + zh, 8:24, :], 0.0)
    block_ref[16:32, 0:128] = a
    block_ref[16:32, 128:256] = pltpu.roll(low, 96, 1) + high
    send_block(block_ref[...], out_ref, index[1])


def gradients(
    index, got_ref, block_ref, kept_ref, came_ref, out_ref, own_ref, turn, khatri, terms, first
):
    x, core, y = index[1], index[2], index[4]
    order = [i + 16 * core if i < 12 else i + 4 - 16 * core for i in range(24)]
    for q in range(4):
        v = jnp.where(y == q, block_ref[16:32, 0:128], slot(got_ref, x * 4 + q))
        turn[16 * q : 16 * q + 16, :] = v
        turn[64 + 16 * q : 80 + 16 * q, :] = pltpu.roll(v, 96, 1)
    turned = turn[...].T
    first[:, 0:128] = turned[0:32]
    first[:, 128:256] = turned[64:96]
    a = [first[pl.ds(i, 1), :] for i in order]
    for q in range(4):
        v = jnp.where(x == q, block_ref[16:32, 128:256], slot(got_ref, q * 4 + y))
        turn[32 * q : 32 * q + 16, :] = v
        turn[32 * q + 16 : 32 * q + 32, :] = pltpu.roll(v, 64, 1)
    turned = turn[...].T
    b = jnp.concatenate([turned[0:32], turned[32:64]], axis=1)
    for i in range(24):
        khatri[32 * i : 32 * i + 32, :] = a[i] * b
    c = got_ref[:, 0:16, :].reshape(256, 256)
    c, turned_c = split(c), split(c.T)
    parts = split(khatri[...])
    model = product(parts, turned_c, ((1,), (0,)))
    target = jnp.concatenate([kept_ref[...], came_ref[...]], axis=0)
    deriv = split(jax.nn.sigmoid(model) - target)
    terms[...] = product(deriv, c, ((1,), (0,)))
    grad_c = product(deriv, parts, ((0,), (0,)))
    grad_b = jnp.zeros((32, 256), F32)
    turn[...] = jnp.zeros((128, 128), F32)
    for i in range(24):
        term = terms[32 * i : 32 * i + 32, :]
        grad_b = grad_b + term * a[i]
        row = jnp.sum(term * b, axis=0, keepdims=True)
        turn[pl.ds(order[i], 1), :] = row[:, 0:128]
        turn[pl.ds(order[i] + 64, 1), :] = row[:, 128:256]
    turned = turn[...].T
    pieces_a = [
        turned[16 * q : 16 * q + 16] + pltpu.roll(turned[64 + 16 * q : 80 + 16 * q], 32, 1)
        for q in range(4)
    ]
    turn[...] = jnp.zeros((128, 128), F32)
    turn[0:32, :] = grad_b[:, 0:128]
    turn[32:64, :] = grad_b[:, 128:256]
    turned = turn[...].T
    pieces_b = [
        turned[32 * q : 32 * q + 16] + pltpu.roll(turned[32 * q + 16 : 32 * q + 32], 64, 1)
        for q in range(4)
    ]
    out_ref[:, 0:16, :] = grad_c.reshape(16, 16, 256)
    for p in range(16):
        fill_slot(out_ref, p, jnp.where(x == p // 4, pieces_a[p % 4], pieces_b[p // 4]))
    own_a, own_b = pieces_a[0], pieces_b[0]
    for q in range(1, 4):
        own_a = jnp.where(y == q, pieces_a[q], own_a)
        own_b = jnp.where(x == q, pieces_b[q], own_b)
    own_ref[:, 0:128] = own_a
    own_ref[:, 128:256] = own_b


def sum_xy(index, got_ref, own_ref):
    x, y = index[1], index[4]
    c = jnp.sum(got_ref[:, 0:16, :], axis=0)
    a, b = own_ref[:, 0:128], own_ref[:, 128:256]
    for q in range(4):
        a = a + jnp.where(y == q, 0.0, slot(got_ref, x * 4 + q))
        b = b + jnp.where(x == q, 0.0, slot(got_ref, q * 4 + y))
    return c, a, b


def middle_pack(index, got_ref, own_ref, out_ref, sum_ref):
    c, a, b = sum_xy(index, got_ref, own_ref)
    for p in range(8):
        out_ref[p, 0:16, :] = c
        fill_slot(out_ref, p, jnp.where(index[0] == p // 4, a, b))
    sum_ref[:, 0:128] = a
    sum_ref[:, 128:256] = b


def middle_sum(index, got_ref, own_ref, c_ref, ab_ref):
    zl, zh = index[0], index[3]
    c_ref[...] = jnp.sum(got_ref[:, 0:16, :], axis=0)
    a = own_ref[:, 0:128]
    for q in range(4):
        a = a + jnp.where(zh == q, 0.0, slot(got_ref, zl * 4 + q))
    ab_ref[:, 0:128] = a
    ab_ref[:, 128:256] = own_ref[:, 128:256] + slot(got_ref, (1 - zl) * 4 + zh)


def middle_update(rates, index, block_ref, c_ref, ab_ref, other_ref, slip_ref, block_out, out_ref, new):
    rate_a, rate_b, rate_c = rates
    ab = ab_ref[...] + other_ref[...]
    new[0:16, :] = block_ref[0:16, :] - rate_c * c_ref[...]
    new[16:32, 0:128] = block_ref[16:32, 0:128] - rate_a * ab[:, 0:128]
    new[16:32, 128:256] = block_ref[16:32, 128:256] - rate_b * ab[:, 128:256]
    block = new[...]
    block_out[...] = block
    send_block(block, out_ref, index[1])
    own = index[0] * 4 + index[3]
    c = jnp.zeros((2, 256), F32)
    ab = jnp.zeros((16, 128), F32)
    for p in range(8):
        c_p, ab_p = slip_of(block, p, p // 4, p % 4)
        c = jnp.where(own == p, c_p, c)
        ab = jnp.where(own == p, ab_p, ab)
    slip_ref[0:8, :] = jnp.zeros((8, 128), F32)
    slip_ref[0:2, :] = c[:, 0:128]
    slip_ref[2:4, :] = c[:, 128:256]
    slip_ref[8:24, :] = ab


def last_pack(index, got_ref, own_ref, out_ref, new):
    c, a, b = sum_xy(index, got_ref, own_ref)
    new[0:16, :] = c
    new[16:32, 0:128] = a
    new[16:32, 128:256] = b
    block = new[...]
    for p in range(8):
        c_p, ab_p = slip_of(block, p, p // 4, p % 4)
        out_ref[p, 0:8, :] = jnp.zeros((8, 128), F32)
        out_ref[p, 0:2, :] = c_p[:, 0:128]
        out_ref[p, 2:4, :] = c_p[:, 128:256]
        out_ref[p, 8:24, :] = ab_p


def last_sum(index, got_ref, slip_ref):
    zl, zh = index[0], index[3]
    c = got_ref[0, 0:8, :]
    for p in range(1, 8):
        c = c + got_ref[p, 0:8, :]
    a = got_ref[zl * 4, 8:24, :]
    for q in range(1, 4):
        a = a + got_ref[zl * 4 + q, 8:24, :]
    b = got_ref[zh, 8:24, :] + got_ref[4 + zh, 8:24, :]
    slip_ref[0:8, :] = c
    slip_ref[8:24, :] = jnp.where(lanes() < 32, a, b)


def last_update(rates, index, old_ref, grad_ref, other_ref, a_ref, bt_ref, c_ref, pad):
    rate_a, rate_b, rate_c = rates
    core = index[2]
    c = old_ref[0:8, :] - rate_c * grad_ref[0:8, :]
    c_ref[:, 0:128] = c[0:2, :]
    c_ref[:, 128:256] = c[2:4, :]
    rate = jnp.where(lanes() < 32, rate_a, rate_b)
    ab = old_ref[8:24, :] - rate * (grad_ref[8:24, :] + other_ref[8:24, :])
    b = jnp.where(core == 0, pltpu.roll(ab, 96, 1), pltpu.roll(ab, 32, 1))
    bt_ref[...] = b[:, 0:32]
    pad[...] = jnp.zeros((128, 128), F32)
    pad[0:16, :] = jnp.where(core == 0, ab, pltpu.roll(ab, 112, 1))
    turned = pad[...].T
    a_ref[...] = turned[0:12, 0:16]


def arrange(index, after_ref, own_ref, other_ref, kept_ref, came_ref):
    del after_ref
    spot = lax.broadcasted_iota(jnp.int32, (512, 256), 1)
    xs, ys = spot // 64, (spot // 16) % 4
    zls, zhs, us = (spot // 8) % 2, (spot // 2) % 4, spot % 2
    source = zls * 256 + xs * 64 + index[2] * 32 + zhs * 8 + ys * 2 + us
    here = lax.broadcasted_iota(jnp.int32, (512, 256), 0)
    pick = jnp.where(here == source, 1.0, 0.0).astype(jnp.bfloat16)
    for from_ref, to_ref in ((own_ref, kept_ref), (other_ref, came_ref)):
        rest = from_ref[...]
        total = jnp.zeros((384, 256), F32)
        for _ in range(3):
            part = rest.astype(jnp.bfloat16)
            rest = rest - part.astype(F32)
            total = total + jnp.dot(part, pick, preferred_element_type=F32)
        to_ref[...] = total


def per_device(tensor, first_factor, second_factor, third_factor):
    n_i, n_j, depth = tensor.shape
    size_i, size_j = n_i * 16, n_j * 16
    rates = tuple(4.0 / float(n) ** 0.5 for n in (size_j * depth, size_i * depth, size_i * size_j))
    wide = (16, 24, 256)
    square, pair = (128, 128), (16, 256)

    flat = tensor.reshape(-1, depth)
    arguments = (first_factor, 16), (second_factor.T, 16), (third_factor, 8)
    shards = jnp.concatenate(
        [jnp.pad(v, ((0, n - v.shape[0]), (0, 256 - v.shape[1]))) for v, n in arguments]
    )
    shards_other = swap(shards)
    flat, shards_other = lax.optimization_barrier((flat, shards_other))
    flat_other = swap(flat)
    send, done = call(
        first_pack, [(8, 24, 128), (16, 128)], [square], shards, shards_other
    )
    targets = call(arrange, [(384, 256), (384, 256)], [], done, flat, flat_other)
    got, targets = lax.optimization_barrier((exchange(send, Z), targets))
    block, send = call(block_from_slips, [(32, 256), wide], [], got)
    step = functools.partial(
        call, gradients, [wide, pair], [square, (768, 256), (768, 256), (32, 256)]
    )

    send, own = step(exchange(send, XY), block, *targets)
    send, own = call(middle_pack, [(8, 24, 256), pair], [], exchange(send, XY), own)
    grad_c, grad_ab = call(middle_sum, [pair, pair], [], exchange(send, Z), own)
    slip, block, send = call(
        functools.partial(middle_update, rates),
        [(24, 128), (32, 256), wide],
        [(32, 256)],
        block,
        grad_c,
        grad_ab,
        swap(grad_ab),
    )
    send, own = step(exchange(send, XY), block, *targets)
    (send,) = call(last_pack, [(8, 24, 128)], [(32, 256)], exchange(send, XY), own)
    (grad,) = call(last_sum, [(24, 128)], [], exchange(send, Z))
    new_a, new_bt, new_c = call(
        functools.partial(last_update, rates),
        [(n_i, 16), (16, n_j), third_factor.shape],
        [square],
        slip,
        grad,
        swap(grad),
    )
    return (new_a, new_bt.T, new_c)


def solution(mesh):
    fine = Mesh(mesh.devices.reshape(2, 4, 2, 4, 4), ("zl", "x", "core", "zh", "y"))
    rows, cols = ("zl", "x", "core"), ("zh", "y")
    in_specs = (P(rows, cols, None), P(rows, cols), P(cols, rows), P(rows + cols, None))
    out_specs = (P(rows, cols), P(cols, rows), P(rows + cols, None))
    return jax.shard_map(
        per_device, mesh=fine, in_specs=in_specs, out_specs=out_specs, check_vma=False
    )
```

```python
import functools

import jax
import jax.numpy as jnp
from jax import lax
from jax.experimental import pallas as pl
from jax.experimental.pallas import tpu as pltpu
from jax.sharding import Mesh, PartitionSpec as P

XY = ("x", "y")
Z = ("zl", "zh")
HIGH = lax.Precision.HIGHEST
F32 = jnp.float32


def exchange(parts, axis):
    shape = parts.shape
    got = lax.all_to_all(parts.reshape(-1, shape[2]), axis, 0, 0, tiled=True)
    return got.reshape(shape)


def swap(value):
    return lax.ppermute(value, "core", [(0, 1), (1, 0)])


def call(body, outs, scratch, *operands):
    def kernel(*refs):
        body([lax.axis_index(n) for n in ("zl", "x", "core", "zh", "y")], *refs)

    vmem = pl.BlockSpec(memory_space=pltpu.VMEM)
    return pl.pallas_call(
        kernel,
        out_shape=[jax.ShapeDtypeStruct(s, F32) for s in outs],
        in_specs=[vmem] * len(operands),
        out_specs=[vmem] * len(outs),
        scratch_shapes=[pltpu.VMEM(s, F32) for s in scratch],
        compiler_params=pltpu.CompilerParams(vmem_limit_bytes=40 * 1024 * 1024),
    )(*operands)


def lanes(rows=16):
    return lax.broadcasted_iota(jnp.int32, (rows, 128), 1)


def split(value):
    top = value.astype(jnp.bfloat16)
    return top, (value - top.astype(F32)).astype(jnp.bfloat16)


def product(left, right, dims):
    (lt, lb), (rt, rb) = left, right
    dot = functools.partial(
        lax.dot_general, dimension_numbers=(dims, ((), ())), preferred_element_type=F32
    )
    return dot(lt, rt) + (dot(lt, rb) + dot(lb, rt))


def fill_slot(ref, p, value):
    ref[p, 16:24, 0:128] = value[0:8]
    ref[p, 16:24, 128:256] = value[8:16]


def slot(ref, p):
    v = ref[p, 16:24, :]
    return jnp.concatenate([v[:, 0:128], v[:, 128:256]], axis=0)


def send_block(block, out_ref, x):
    for p in range(16):
        out_ref[p, 0:16, :] = block[0:16]
        fill_slot(out_ref, p, jnp.where(x == p // 4, block[16:32, 0:128], block[16:32, 128:256]))


def slip_of(block, place, zl, zh):
    a = block[16:32, 0:128]
    b = block[16:32, 128:256]
    if zh:
        a = pltpu.roll(a, 128 - 32 * zh, 1)
    if not zl:
        b = pltpu.roll(b, 32, 1)
    at = lanes()
    second = (at // 32) % 2 == 1
    ab = jnp.where(at < 32, a, jnp.where(second, b, 0.0))
    c = block[2 * place : 2 * place + 2, :]
    return c, ab


def first_pack(index, own_ref, other_ref, out_ref, done_ref, pad):
    even = index[2] == 0
    own, other = own_ref[0:32, 0:128], other_ref[0:32, 0:128]
    low, high = jnp.where(even, own, other), jnp.where(even, other, own)
    pad[...] = jnp.zeros((128, 128), F32)
    pad[0:16, :] = low[0:16]
    pad[16:32, :] = high[0:16]
    ab = pad[...].T[0:16, :] + pltpu.roll(low[16:32], 32, 1) + pltpu.roll(high[16:32], 96, 1)
    for p in range(8):
        out_ref[p, 0:8, :] = jnp.zeros((8, 128), F32)
        out_ref[p, 0:2, :] = own_ref[32:34, 0:128]
        out_ref[p, 2:4, :] = own_ref[32:34, 128:256]
        out_ref[p, 8:24, :] = ab
    done_ref[...] = ab


def block_from_slips(index, got_ref, block_ref, out_ref):
    zl, zh = index[0], index[3]
    for p in range(8):
        block_ref[2 * p : 2 * p + 2, 0:128] = got_ref[p, 0:2, :]
        block_ref[2 * p : 2 * p + 2, 128:256] = got_ref[p, 2:4, :]
    at = lanes()
    a = jnp.zeros((16, 128), F32)
    for q in range(4):
        v = jnp.where(at < 32, got_ref[zl * 4 + q, 8:24, :], 0.0)
        a = a + (pltpu.roll(v, 32 * q, 1) if q else v)
    second = (at // 32) % 2 == 1
    low = jnp.where(second, got_ref[zh, 8:24, :], 0.0)
    high = jnp.where(second, got_ref[4 + zh, 8:24, :], 0.0)
    block_ref[16:32, 0:128] = a
    block_ref[16:32, 128:256] = pltpu.roll(low, 96, 1) + high
    send_block(block_ref[...], out_ref, index[1])


def gradients(
    index, got_ref, block_ref, kept_ref, came_ref, pieces_ref, deriv_ref, khatri, turn, terms, first
):
    x, core, y = index[1], index[2], index[4]
    order = [i + 16 * core if i < 12 else i + 4 - 16 * core for i in range(24)]
    for q in range(4):
        v = jnp.where(y == q, block_ref[16:32, 0:128], slot(got_ref, x * 4 + q))
        turn[16 * q : 16 * q + 16, :] = v
        turn[64 + 16 * q : 80 + 16 * q, :] = pltpu.roll(v, 96, 1)
    turned = turn[...].T
    first[:, 0:128] = turned[0:32]
    first[:, 128:256] = turned[64:96]
    a = [first[pl.ds(i, 1), :] for i in order]
    for q in range(4):
        v = jnp.where(x == q, block_ref[16:32, 128:256], slot(got_ref, q * 4 + y))
        turn[32 * q : 32 * q + 16, :] = v
        turn[32 * q + 16 : 32 * q + 32, :] = pltpu.roll(v, 64, 1)
    turned = turn[...].T
    b = jnp.concatenate([turned[0:32], turned[32:64]], axis=1)
    for i in range(24):
        khatri[32 * i : 32 * i + 32, :] = a[i] * b
    c = got_ref[:, 0:16, :].reshape(256, 256)
    c, turned_c = split(c), split(c.T)
    parts = split(khatri[...])
    model = product(parts, turned_c, ((1,), (0,)))
    target = jnp.concatenate([kept_ref[...], came_ref[...]], axis=0)
    deriv = jax.nn.sigmoid(model) - target
    deriv_ref[...] = deriv
    deriv = split(deriv)
    terms[...] = product(deriv, c, ((1,), (0,)))
    grad_b = jnp.zeros((32, 256), F32)
    turn[...] = jnp.zeros((128, 128), F32)
    for i in range(24):
        term = terms[32 * i : 32 * i + 32, :]
        grad_b = grad_b + term * a[i]
        row = jnp.sum(term * b, axis=0, keepdims=True)
        turn[pl.ds(order[i], 1), :] = row[:, 0:128]
        turn[pl.ds(order[i] + 64, 1), :] = row[:, 128:256]
    turned = turn[...].T
    for q in range(4):
        pieces_ref[16 * q : 16 * q + 16, 0:128] = turned[16 * q : 16 * q + 16] + pltpu.roll(
            turned[64 + 16 * q : 80 + 16 * q], 32, 1
        )
    turn[...] = jnp.zeros((128, 128), F32)
    turn[0:32, :] = grad_b[:, 0:128]
    turn[32:64, :] = grad_b[:, 128:256]
    turned = turn[...].T
    for q in range(4):
        pieces_ref[16 * q : 16 * q + 16, 128:256] = turned[32 * q : 32 * q + 16] + pltpu.roll(
            turned[32 * q + 16 : 32 * q + 32], 64, 1
        )


def third_gradient(index, deriv_ref, khatri_ref, out_ref):
    del index
    out_ref[...] = product(split(deriv_ref[...]), split(khatri_ref[...]), ((0,), (0,)))


def gradients_pack(index, pieces_ref, other_ref, c_ref, out_ref, own_ref):
    x, y = index[1], index[4]
    pieces = [
        pieces_ref[16 * q : 16 * q + 16, :] + other_ref[16 * q : 16 * q + 16, :] for q in range(4)
    ]
    out_ref[:, 0:16, :] = c_ref[...].reshape(16, 16, 256)
    for p in range(16):
        fill_slot(
            out_ref, p, jnp.where(x == p // 4, pieces[p % 4][:, 0:128], pieces[p // 4][:, 128:256])
        )
    own_a, own_b = pieces[0][:, 0:128], pieces[0][:, 128:256]
    for q in range(1, 4):
        own_a = jnp.where(y == q, pieces[q][:, 0:128], own_a)
        own_b = jnp.where(x == q, pieces[q][:, 128:256], own_b)
    own_ref[:, 0:128] = own_a
    own_ref[:, 128:256] = own_b


def sum_xy(index, got_ref, own_ref):
    x, y = index[1], index[4]
    c = jnp.sum(got_ref[:, 0:16, :], axis=0)
    a, b = own_ref[:, 0:128], own_ref[:, 128:256]
    for q in range(4):
        a = a + jnp.where(y == q, 0.0, slot(got_ref, x * 4 + q))
        b = b + jnp.where(x == q, 0.0, slot(got_ref, q * 4 + y))
    return c, a, b


def middle_pack(index, got_ref, own_ref, out_ref, sum_ref):
    c, a, b = sum_xy(index, got_ref, own_ref)
    for p in range(8):
        out_ref[p, 0:16, :] = c
        fill_slot(out_ref, p, jnp.where(index[0] == p // 4, a, b))
    sum_ref[:, 0:128] = a
    sum_ref[:, 128:256] = b


def middle_update(rates, index, got_ref, own_ref, block_ref, slip_ref, block_out, out_ref, new):
    zl, zh = index[0], index[3]
    rate_a, rate_b, rate_c = rates
    c = jnp.sum(got_ref[:, 0:16, :], axis=0)
    a = own_ref[:, 0:128]
    for q in range(4):
        a = a + jnp.where(zh == q, 0.0, slot(got_ref, zl * 4 + q))
    b = own_ref[:, 128:256] + slot(got_ref, (1 - zl) * 4 + zh)
    new[0:16, :] = block_ref[0:16, :] - rate_c * c
    new[16:32, 0:128] = block_ref[16:32, 0:128] - rate_a * a
    new[16:32, 128:256] = block_ref[16:32, 128:256] - rate_b * b
    block = new[...]
    block_out[...] = block
    send_block(block, out_ref, index[1])
    own = index[0] * 4 + index[3]
    c = jnp.zeros((2, 256), F32)
    ab = jnp.zeros((16, 128), F32)
    for p in range(8):
        c_p, ab_p = slip_of(block, p, p // 4, p % 4)
        c = jnp.where(own == p, c_p, c)
        ab = jnp.where(own == p, ab_p, ab)
    slip_ref[0:8, :] = jnp.zeros((8, 128), F32)
    slip_ref[0:2, :] = c[:, 0:128]
    slip_ref[2:4, :] = c[:, 128:256]
    slip_ref[8:24, :] = ab


def last_pack(index, got_ref, own_ref, out_ref, new):
    c, a, b = sum_xy(index, got_ref, own_ref)
    new[0:16, :] = c
    new[16:32, 0:128] = a
    new[16:32, 128:256] = b
    block = new[...]
    for p in range(8):
        c_p, ab_p = slip_of(block, p, p // 4, p % 4)
        out_ref[p, 0:8, :] = jnp.zeros((8, 128), F32)
        out_ref[p, 0:2, :] = c_p[:, 0:128]
        out_ref[p, 2:4, :] = c_p[:, 128:256]
        out_ref[p, 8:24, :] = ab_p


def last_update(rates, index, old_ref, got_ref, a_ref, bt_ref, c_ref, pad):
    zl, core, zh = index[0], index[2], index[3]
    rate_a, rate_b, rate_c = rates
    c = got_ref[0, 0:8, :]
    for p in range(1, 8):
        c = c + got_ref[p, 0:8, :]
    c = old_ref[0:8, :] - rate_c * c
    c_ref[:, 0:128] = c[0:2, :]
    c_ref[:, 128:256] = c[2:4, :]
    a = got_ref[zl * 4, 8:24, :]
    for q in range(1, 4):
        a = a + got_ref[zl * 4 + q, 8:24, :]
    b = got_ref[zh, 8:24, :] + got_ref[4 + zh, 8:24, :]
    ab = old_ref[8:24, :] - jnp.where(lanes() < 32, rate_a * a, rate_b * b)
    b = jnp.where(core == 0, pltpu.roll(ab, 96, 1), pltpu.roll(ab, 32, 1))
    bt_ref[...] = b[:, 0:32]
    pad[...] = jnp.zeros((128, 128), F32)
    pad[0:16, :] = jnp.where(core == 0, ab, pltpu.roll(ab, 112, 1))
    turned = pad[...].T
    a_ref[...] = turned[0:12, 0:16]


def arrange(index, after_ref, own_ref, other_ref, kept_ref, came_ref):
    del after_ref
    spot = lax.broadcasted_iota(jnp.int32, (512, 256), 1)
    xs, ys = spot // 64, (spot // 16) % 4
    zls, zhs, us = (spot // 8) % 2, (spot // 2) % 4, spot % 2
    source = zls * 256 + xs * 64 + index[2] * 32 + zhs * 8 + ys * 2 + us
    here = lax.broadcasted_iota(jnp.int32, (512, 256), 0)
    pick = jnp.where(here == source, 1.0, 0.0).astype(jnp.bfloat16)
    for from_ref, to_ref in ((own_ref, kept_ref), (other_ref, came_ref)):
        rest = from_ref[...]
        total = jnp.zeros((384, 256), F32)
        for _ in range(3):
            part = rest.astype(jnp.bfloat16)
            rest = rest - part.astype(F32)
            total = total + jnp.dot(part, pick, preferred_element_type=F32)
        to_ref[...] = total


def per_device(tensor, first_factor, second_factor, third_factor):
    n_i, n_j, depth = tensor.shape
    size_i, size_j = n_i * 16, n_j * 16
    rates = tuple(4.0 / float(n) ** 0.5 for n in (size_j * depth, size_i * depth, size_i * size_j))
    wide = (16, 24, 256)
    square, pair = (128, 128), (16, 256)

    flat = tensor.reshape(-1, depth)
    arguments = (first_factor, 16), (second_factor.T, 16), (third_factor, 8)
    shards = jnp.concatenate(
        [jnp.pad(v, ((0, n - v.shape[0]), (0, 256 - v.shape[1]))) for v, n in arguments]
    )
    shards_other = swap(shards)
    flat, shards_other = lax.optimization_barrier((flat, shards_other))
    flat_other = swap(flat)
    send, done = call(
        first_pack, [(8, 24, 128), (16, 128)], [square], shards, shards_other
    )
    targets = call(arrange, [(384, 256), (384, 256)], [], done, flat, flat_other)
    got, targets = lax.optimization_barrier((exchange(send, Z), targets))
    block, send = call(block_from_slips, [(32, 256), wide], [], got)
    tall = (768, 256)

    def step(got, block):
        pieces, deriv, khatri = call(
            gradients, [(64, 256), tall, tall], [square, tall, (32, 256)], got, block, *targets
        )
        (grad_c,) = call(third_gradient, [(256, 256)], [], deriv, khatri)
        return call(gradients_pack, [wide, pair], [], pieces, swap(pieces), grad_c)

    send, own = step(exchange(send, XY), block)
    send, own = call(middle_pack, [(8, 24, 256), pair], [], exchange(send, XY), own)
    slip, block, send = call(
        functools.partial(middle_update, rates),
        [(24, 128), (32, 256), wide],
        [(32, 256)],
        exchange(send, Z),
        own,
        block,
    )
    send, own = step(exchange(send, XY), block)
    (send,) = call(last_pack, [(8, 24, 128)], [(32, 256)], exchange(send, XY), own)
    new_a, new_bt, new_c = call(
        functools.partial(last_update, rates),
        [(n_i, 16), (16, n_j), third_factor.shape],
        [square],
        slip,
        exchange(send, Z),
    )
    return (new_a, new_bt.T, new_c)


def solution(mesh):
    fine = Mesh(mesh.devices.reshape(2, 4, 2, 4, 4), ("zl", "x", "core", "zh", "y"))
    rows, cols = ("zl", "x", "core"), ("zh", "y")
    in_specs = (P(rows, cols, None), P(rows, cols), P(cols, rows), P(rows + cols, None))
    out_specs = (P(rows, cols), P(cols, rows), P(rows + cols, None))
    return jax.shard_map(
        per_device, mesh=fine, in_specs=in_specs, out_specs=out_specs, check_vma=False
    )
```

```python
import functools

import jax
import jax.numpy as jnp
from jax import lax
from jax.experimental import pallas as pl
from jax.experimental.pallas import tpu as pltpu
from jax.sharding import Mesh, PartitionSpec as P

XY = ("x", "y")
Z = ("zh", "zl")
HIGH = lax.Precision.HIGHEST
F32 = jnp.float32


def exchange(parts, axis):
    shape = parts.shape
    got = lax.all_to_all(parts.reshape(-1, shape[2]), axis, 0, 0, tiled=True)
    return got.reshape(shape)


def swap(value):
    return lax.ppermute(value, "core", [(0, 1), (1, 0)])


def call(body, outs, scratch, *operands):
    def kernel(*refs):
        body([lax.axis_index(n) for n in ("zl", "x", "core", "zh", "y")], *refs)

    vmem = pl.BlockSpec(memory_space=pltpu.VMEM)
    return pl.pallas_call(
        kernel,
        out_shape=[jax.ShapeDtypeStruct(s, F32) for s in outs],
        in_specs=[vmem] * len(operands),
        out_specs=[vmem] * len(outs),
        scratch_shapes=[pltpu.VMEM(s, F32) for s in scratch],
        compiler_params=pltpu.CompilerParams(vmem_limit_bytes=40 * 1024 * 1024),
    )(*operands)


def lanes(rows=16):
    return lax.broadcasted_iota(jnp.int32, (rows, 128), 1)


def split(value):
    top = value.astype(jnp.bfloat16)
    return top, (value - top.astype(F32)).astype(jnp.bfloat16)


def product(left, right, dims):
    (lt, lb), (rt, rb) = left, right
    dot = functools.partial(
        lax.dot_general, dimension_numbers=(dims, ((), ())), preferred_element_type=F32
    )
    return dot(lt, rt) + (dot(lt, rb) + dot(lb, rt))


def fill_slot(ref, p, value):
    ref[p, 16:24, 0:128] = value[0:8]
    ref[p, 16:24, 128:256] = value[8:16]


def slot(ref, p):
    v = ref[p, 16:24, :]
    return jnp.concatenate([v[:, 0:128], v[:, 128:256]], axis=0)


def send_block(block, out_ref, x):
    for p in range(16):
        out_ref[p, 0:16, :] = block[0:16]
        fill_slot(out_ref, p, jnp.where(x == p // 4, block[16:32, 0:128], block[16:32, 128:256]))


def slip_of(block, place, zl, zh):
    a = block[16:32, 0:128]
    b = block[16:32, 128:256]
    if zh:
        a = pltpu.roll(a, 128 - 32 * zh, 1)
    if not zl:
        b = pltpu.roll(b, 32, 1)
    at = lanes()
    second = (at // 32) % 2 == 1
    ab = jnp.where(at < 32, a, jnp.where(second, b, 0.0))
    c = block[2 * place : 2 * place + 2, :]
    return c, ab


def first_pack(index, own_ref, other_ref, out_ref, done_ref, pad):
    even = index[2] == 0
    own, other = own_ref[0:32, 0:128], other_ref[0:32, 0:128]
    low, high = jnp.where(even, own, other), jnp.where(even, other, own)
    pad[...] = jnp.zeros((128, 128), F32)
    pad[0:16, :] = low[0:16]
    pad[16:32, :] = high[0:16]
    ab = pad[...].T[0:16, :] + pltpu.roll(low[16:32], 32, 1) + pltpu.roll(high[16:32], 96, 1)
    for p in range(8):
        out_ref[p, 0:8, :] = jnp.zeros((8, 128), F32)
        out_ref[p, 0:2, :] = own_ref[32:34, 0:128]
        out_ref[p, 2:4, :] = own_ref[32:34, 128:256]
        out_ref[p, 8:24, :] = ab
    done_ref[...] = ab


def block_from_slips(index, got_ref, block_ref, out_ref):
    zl, zh = index[0], index[3]
    for p in range(8):
        block_ref[2 * p : 2 * p + 2, 0:128] = got_ref[p, 0:2, :]
        block_ref[2 * p : 2 * p + 2, 128:256] = got_ref[p, 2:4, :]
    at = lanes()
    a = jnp.zeros((16, 128), F32)
    for q in range(4):
        v = jnp.where(at < 32, got_ref[2 * q + zl, 8:24, :], 0.0)
        a = a + (pltpu.roll(v, 32 * q, 1) if q else v)
    second = (at // 32) % 2 == 1
    low = jnp.where(second, got_ref[2 * zh, 8:24, :], 0.0)
    high = jnp.where(second, got_ref[2 * zh + 1, 8:24, :], 0.0)
    block_ref[16:32, 0:128] = a
    block_ref[16:32, 128:256] = pltpu.roll(low, 96, 1) + high
    send_block(block_ref[...], out_ref, index[1])


def gradients(
    index, got_ref, block_ref, kept_ref, came_ref, out_ref, own_ref, turn, khatri, terms, first
):
    x, core, y = index[1], index[2], index[4]
    order = [i + 16 * core if i < 12 else i + 4 - 16 * core for i in range(24)]
    for q in range(4):
        v = jnp.where(y == q, block_ref[16:32, 0:128], slot(got_ref, x * 4 + q))
        turn[16 * q : 16 * q + 16, :] = v
        turn[64 + 16 * q : 80 + 16 * q, :] = pltpu.roll(v, 96, 1)
    turned = turn[...].T
    first[:, 0:128] = turned[0:32]
    first[:, 128:256] = turned[64:96]
    a = [first[pl.ds(i, 1), :] for i in order]
    for q in range(4):
        v = jnp.where(x == q, block_ref[16:32, 128:256], slot(got_ref, q * 4 + y))
        turn[32 * q : 32 * q + 16, :] = v
        turn[32 * q + 16 : 32 * q + 32, :] = pltpu.roll(v, 64, 1)
    turned = turn[...].T
    b = jnp.concatenate([turned[0:32], turned[32:64]], axis=1)
    for i in range(24):
        khatri[32 * i : 32 * i + 32, :] = a[i] * b
    c = got_ref[:, 0:16, :].reshape(256, 256)
    c, turned_c = split(c), split(c.T)
    parts = split(khatri[...])
    model = product(parts, turned_c, ((1,), (0,)))
    target = jnp.concatenate([kept_ref[...], came_ref[...]], axis=0)
    deriv = split(jax.nn.sigmoid(model) - target)
    terms[...] = product(deriv, c, ((1,), (0,)))
    grad_c = product(deriv, parts, ((0,), (0,)))
    grad_b = jnp.zeros((32, 256), F32)
    turn[...] = jnp.zeros((128, 128), F32)
    for i in range(24):
        term = terms[32 * i : 32 * i + 32, :]
        grad_b = grad_b + term * a[i]
        row = jnp.sum(term * b, axis=0, keepdims=True)
        turn[pl.ds(order[i], 1), :] = row[:, 0:128]
        turn[pl.ds(order[i] + 64, 1), :] = row[:, 128:256]
    turned = turn[...].T
    pieces_a = [
        turned[16 * q : 16 * q + 16] + pltpu.roll(turned[64 + 16 * q : 80 + 16 * q], 32, 1)
        for q in range(4)
    ]
    turn[...] = jnp.zeros((128, 128), F32)
    turn[0:32, :] = grad_b[:, 0:128]
    turn[32:64, :] = grad_b[:, 128:256]
    turned = turn[...].T
    pieces_b = [
        turned[32 * q : 32 * q + 16] + pltpu.roll(turned[32 * q + 16 : 32 * q + 32], 64, 1)
        for q in range(4)
    ]
    out_ref[:, 0:16, :] = grad_c.reshape(16, 16, 256)
    for p in range(16):
        fill_slot(out_ref, p, jnp.where(x == p // 4, pieces_a[p % 4], pieces_b[p // 4]))
    own_a, own_b = pieces_a[0], pieces_b[0]
    for q in range(1, 4):
        own_a = jnp.where(y == q, pieces_a[q], own_a)
        own_b = jnp.where(x == q, pieces_b[q], own_b)
    own_ref[:, 0:128] = own_a
    own_ref[:, 128:256] = own_b


def sum_xy(index, got_ref, own_ref):
    x, y = index[1], index[4]
    c = jnp.sum(got_ref[:, 0:16, :], axis=0)
    a, b = own_ref[:, 0:128], own_ref[:, 128:256]
    for q in range(4):
        a = a + jnp.where(y == q, 0.0, slot(got_ref, x * 4 + q))
        b = b + jnp.where(x == q, 0.0, slot(got_ref, q * 4 + y))
    return c, a, b


def middle_pack(index, got_ref, own_ref, out_ref, sum_ref):
    c, a, b = sum_xy(index, got_ref, own_ref)
    for p in range(8):
        out_ref[p, 0:16, :] = c
        fill_slot(out_ref, p, jnp.where(index[0] == p % 2, a, b))
    sum_ref[:, 0:128] = a
    sum_ref[:, 128:256] = b


def middle_sum(index, got_ref, own_ref, c_ref, ab_ref):
    zl, zh = index[0], index[3]
    c_ref[...] = jnp.sum(got_ref[:, 0:16, :], axis=0)
    a = own_ref[:, 0:128]
    for q in range(4):
        a = a + jnp.where(zh == q, 0.0, slot(got_ref, 2 * q + zl))
    ab_ref[:, 0:128] = a
    ab_ref[:, 128:256] = own_ref[:, 128:256] + slot(got_ref, 2 * zh + 1 - zl)


def middle_update(rates, index, block_ref, c_ref, ab_ref, other_ref, slip_ref, block_out, out_ref, new):
    rate_a, rate_b, rate_c = rates
    ab = ab_ref[...] + other_ref[...]
    new[0:16, :] = block_ref[0:16, :] - rate_c * c_ref[...]
    new[16:32, 0:128] = block_ref[16:32, 0:128] - rate_a * ab[:, 0:128]
    new[16:32, 128:256] = block_ref[16:32, 128:256] - rate_b * ab[:, 128:256]
    block = new[...]
    block_out[...] = block
    send_block(block, out_ref, index[1])
    own = index[3] * 2 + index[0]
    c = jnp.zeros((2, 256), F32)
    ab = jnp.zeros((16, 128), F32)
    for p in range(8):
        c_p, ab_p = slip_of(block, p, p % 2, p // 2)
        c = jnp.where(own == p, c_p, c)
        ab = jnp.where(own == p, ab_p, ab)
    slip_ref[0:8, :] = jnp.zeros((8, 128), F32)
    slip_ref[0:2, :] = c[:, 0:128]
    slip_ref[2:4, :] = c[:, 128:256]
    slip_ref[8:24, :] = ab


def last_pack(index, got_ref, own_ref, out_ref, new):
    c, a, b = sum_xy(index, got_ref, own_ref)
    new[0:16, :] = c
    new[16:32, 0:128] = a
    new[16:32, 128:256] = b
    block = new[...]
    for p in range(8):
        c_p, ab_p = slip_of(block, p, p % 2, p // 2)
        out_ref[p, 0:8, :] = jnp.zeros((8, 128), F32)
        out_ref[p, 0:2, :] = c_p[:, 0:128]
        out_ref[p, 2:4, :] = c_p[:, 128:256]
        out_ref[p, 8:24, :] = ab_p


def last_sum(index, got_ref, slip_ref):
    zl, zh = index[0], index[3]
    c = got_ref[0, 0:8, :]
    for p in range(1, 8):
        c = c + got_ref[p, 0:8, :]
    a = got_ref[zl, 8:24, :]
    for q in range(1, 4):
        a = a + got_ref[2 * q + zl, 8:24, :]
    b = got_ref[2 * zh, 8:24, :] + got_ref[2 * zh + 1, 8:24, :]
    slip_ref[0:8, :] = c
    slip_ref[8:24, :] = jnp.where(lanes() < 32, a, b)


def last_update(rates, index, old_ref, grad_ref, other_ref, a_ref, bt_ref, c_ref, pad):
    rate_a, rate_b, rate_c = rates
    core = index[2]
    c = old_ref[0:8, :] - rate_c * grad_ref[0:8, :]
    c_ref[:, 0:128] = c[0:2, :]
    c_ref[:, 128:256] = c[2:4, :]
    rate = jnp.where(lanes() < 32, rate_a, rate_b)
    ab = old_ref[8:24, :] - rate * (grad_ref[8:24, :] + other_ref[8:24, :])
    b = jnp.where(core == 0, pltpu.roll(ab, 96, 1), pltpu.roll(ab, 32, 1))
    bt_ref[...] = b[:, 0:32]
    pad[...] = jnp.zeros((128, 128), F32)
    pad[0:16, :] = jnp.where(core == 0, ab, pltpu.roll(ab, 112, 1))
    turned = pad[...].T
    a_ref[...] = turned[0:12, 0:16]


def arrange(index, after_ref, own_ref, other_ref, kept_ref, came_ref):
    del after_ref
    spot = lax.broadcasted_iota(jnp.int32, (512, 256), 1)
    xs, ys = spot // 64, (spot // 16) % 4
    zhs, zls, us = (spot // 4) % 4, (spot // 2) % 2, spot % 2
    source = zls * 256 + xs * 64 + index[2] * 32 + zhs * 8 + ys * 2 + us
    here = lax.broadcasted_iota(jnp.int32, (512, 256), 0)
    pick = jnp.where(here == source, 1.0, 0.0).astype(jnp.bfloat16)
    for from_ref, to_ref in ((own_ref, kept_ref), (other_ref, came_ref)):
        rest = from_ref[...]
        total = jnp.zeros((384, 256), F32)
        for _ in range(3):
            part = rest.astype(jnp.bfloat16)
            rest = rest - part.astype(F32)
            total = total + jnp.dot(part, pick, preferred_element_type=F32)
        to_ref[...] = total


def per_device(tensor, first_factor, second_factor, third_factor):
    n_i, n_j, depth = tensor.shape
    size_i, size_j = n_i * 16, n_j * 16
    rates = tuple(4.0 / float(n) ** 0.5 for n in (size_j * depth, size_i * depth, size_i * size_j))
    wide = (16, 24, 256)
    square, pair = (128, 128), (16, 256)

    flat = tensor.reshape(-1, depth)
    arguments = (first_factor, 16), (second_factor.T, 16), (third_factor, 8)
    shards = jnp.concatenate(
        [jnp.pad(v, ((0, n - v.shape[0]), (0, 256 - v.shape[1]))) for v, n in arguments]
    )
    shards_other = swap(shards)
    flat, shards_other = lax.optimization_barrier((flat, shards_other))
    flat_other = swap(flat)
    send, done = call(
        first_pack, [(8, 24, 128), (16, 128)], [square], shards, shards_other
    )
    targets = call(arrange, [(384, 256), (384, 256)], [], done, flat, flat_other)
    got, targets = lax.optimization_barrier((exchange(send, Z), targets))
    block, send = call(block_from_slips, [(32, 256), wide], [], got)
    step = functools.partial(
        call, gradients, [wide, pair], [square, (768, 256), (768, 256), (32, 256)]
    )

    send, own = step(exchange(send, XY), block, *targets)
    send, own = call(middle_pack, [(8, 24, 256), pair], [], exchange(send, XY), own)
    grad_c, grad_ab = call(middle_sum, [pair, pair], [], exchange(send, Z), own)
    slip, block, send = call(
        functools.partial(middle_update, rates),
        [(24, 128), (32, 256), wide],
        [(32, 256)],
        block,
        grad_c,
        grad_ab,
        swap(grad_ab),
    )
    send, own = step(exchange(send, XY), block, *targets)
    (send,) = call(last_pack, [(8, 24, 128)], [(32, 256)], exchange(send, XY), own)
    (grad,) = call(last_sum, [(24, 128)], [], exchange(send, Z))
    new_a, new_bt, new_c = call(
        functools.partial(last_update, rates),
        [(n_i, 16), (16, n_j), third_factor.shape],
        [square],
        slip,
        grad,
        swap(grad),
    )
    return (new_a, new_bt.T, new_c)


def solution(mesh):
    fine = Mesh(mesh.devices.reshape(2, 4, 2, 4, 4), ("zl", "x", "core", "zh", "y"))
    rows, cols = ("zl", "x", "core"), ("zh", "y")
    in_specs = (P(rows, cols, None), P(rows, cols), P(cols, rows), P(rows + cols, None))
    out_specs = (P(rows, cols), P(cols, rows), P(rows + cols, None))
    return jax.shard_map(
        per_device, mesh=fine, in_specs=in_specs, out_specs=out_specs, check_vma=False
    )
```

```python
import functools

import jax
import jax.numpy as jnp
from jax import lax
from jax.experimental import pallas as pl
from jax.experimental.pallas import tpu as pltpu
from jax.sharding import Mesh, PartitionSpec as P

XY = ("x", "y")
Z = ("zl", "zh")
HIGH = lax.Precision.HIGHEST
F32 = jnp.float32


def exchange(parts, axis):
    shape = parts.shape
    got = lax.all_to_all(parts.reshape(-1, shape[2]), axis, 0, 0, tiled=True)
    return got.reshape(shape)


def swap(value):
    return lax.ppermute(value, "core", [(0, 1), (1, 0)])


def call(body, outs, scratch, *operands):
    def kernel(*refs):
        body([lax.axis_index(n) for n in ("zl", "x", "core", "zh", "y")], *refs)

    vmem = pl.BlockSpec(memory_space=pltpu.VMEM)
    return pl.pallas_call(
        kernel,
        out_shape=[jax.ShapeDtypeStruct(s, F32) for s in outs],
        in_specs=[vmem] * len(operands),
        out_specs=[vmem] * len(outs),
        scratch_shapes=[pltpu.VMEM(s, F32) for s in scratch],
        compiler_params=pltpu.CompilerParams(vmem_limit_bytes=40 * 1024 * 1024),
    )(*operands)


def lanes(rows=16):
    return lax.broadcasted_iota(jnp.int32, (rows, 128), 1)


def split(value):
    top = value.astype(jnp.bfloat16)
    return top, (value - top.astype(F32)).astype(jnp.bfloat16)


def product(left, right, dims):
    (lt, lb), (rt, rb) = left, right
    dot = functools.partial(
        lax.dot_general, dimension_numbers=(dims, ((), ())), preferred_element_type=F32
    )
    return dot(lt, rt) + (dot(lt, rb) + dot(lb, rt))


def fill_slot(ref, p, value):
    ref[p, 16:24, 0:128] = value[0:8]
    ref[p, 16:24, 128:256] = value[8:16]


def slot(ref, p):
    v = ref[p, 16:24, :]
    return jnp.concatenate([v[:, 0:128], v[:, 128:256]], axis=0)


def send_block(block, out_ref, x):
    for p in range(16):
        out_ref[p, 0:16, :] = block[0:16]
        fill_slot(out_ref, p, jnp.where(x == p // 4, block[16:32, 0:128], block[16:32, 128:256]))


def slip_of(block, place, zl, zh):
    a = block[16:32, 0:128]
    b = block[16:32, 128:256]
    if zh:
        a = pltpu.roll(a, 128 - 32 * zh, 1)
    if not zl:
        b = pltpu.roll(b, 32, 1)
    at = lanes()
    second = (at // 32) % 2 == 1
    ab = jnp.where(at < 32, a, jnp.where(second, b, 0.0))
    c = block[2 * place : 2 * place + 2, :]
    return c, ab


def first_pack(index, own_ref, other_ref, out_ref, done_ref, pad):
    even = index[2] == 0
    own, other = own_ref[0:32, 0:128], other_ref[0:32, 0:128]
    low, high = jnp.where(even, own, other), jnp.where(even, other, own)
    pad[...] = jnp.zeros((128, 128), F32)
    pad[0:16, :] = low[0:16]
    pad[16:32, :] = high[0:16]
    ab = pad[...].T[0:16, :] + pltpu.roll(low[16:32], 32, 1) + pltpu.roll(high[16:32], 96, 1)
    for p in range(8):
        out_ref[p, 0:8, :] = jnp.zeros((8, 128), F32)
        out_ref[p, 0:2, :] = own_ref[32:34, 0:128]
        out_ref[p, 2:4, :] = own_ref[32:34, 128:256]
        out_ref[p, 8:24, :] = ab
    done_ref[...] = ab


def block_from_slips(index, got_ref, block_ref, out_ref):
    zl, zh = index[0], index[3]
    for p in range(8):
        block_ref[2 * p : 2 * p + 2, 0:128] = got_ref[p, 0:2, :]
        block_ref[2 * p : 2 * p + 2, 128:256] = got_ref[p, 2:4, :]
    at = lanes()
    a = jnp.zeros((16, 128), F32)
    for q in range(4):
        v = jnp.where(at < 32, got_ref[zl * 4 + q, 8:24, :], 0.0)
        a = a + (pltpu.roll(v, 32 * q, 1) if q else v)
    second = (at // 32) % 2 == 1
    low = jnp.where(second, got_ref[zh, 8:24, :], 0.0)
    high = jnp.where(second, got_ref[4 + zh, 8:24, :], 0.0)
    block_ref[16:32, 0:128] = a
    block_ref[16:32, 128:256] = pltpu.roll(low, 96, 1) + high
    send_block(block_ref[...], out_ref, index[1])


def gradients(
    index, got_ref, block_ref, kept_ref, came_ref, out_ref, own_ref, turn, khatri, terms, first
):
    x, core, y = index[1], index[2], index[4]
    order = [i + 16 * core if i < 12 else i + 4 - 16 * core for i in range(24)]
    for q in range(4):
        v = jnp.where(y == q, block_ref[16:32, 0:128], slot(got_ref, x * 4 + q))
        turn[16 * q : 16 * q + 16, :] = v
        turn[64 + 16 * q : 80 + 16 * q, :] = pltpu.roll(v, 96, 1)
    turned = turn[...].T
    first[:, 0:128] = turned[0:32]
    first[:, 128:256] = turned[64:96]
    a = [first[pl.ds(i, 1), :] for i in order]
    for q in range(4):
        v = jnp.where(x == q, block_ref[16:32, 128:256], slot(got_ref, q * 4 + y))
        turn[32 * q : 32 * q + 16, :] = v
        turn[32 * q + 16 : 32 * q + 32, :] = pltpu.roll(v, 64, 1)
    turned = turn[...].T
    b = jnp.concatenate([turned[0:32], turned[32:64]], axis=1)
    for i in range(24):
        khatri[32 * i : 32 * i + 32, :] = a[i] * b
    c = got_ref[:, 0:16, :].reshape(256, 256)
    c, turned_c = split(c), split(c.T)
    parts = split(khatri[...])
    model = product(parts, turned_c, ((1,), (0,)))
    target = jnp.concatenate([kept_ref[...], came_ref[...]], axis=0)
    deriv = split(jax.nn.sigmoid(model) - target)
    terms[...] = product(deriv, c, ((1,), (0,)))
    grad_c = product(deriv, parts, ((0,), (0,)))
    grad_b = jnp.zeros((32, 256), F32)
    turn[...] = jnp.zeros((128, 128), F32)
    for i in range(24):
        term = terms[32 * i : 32 * i + 32, :]
        grad_b = grad_b + term * a[i]
        row = jnp.sum(term * b, axis=0, keepdims=True)
        turn[pl.ds(order[i], 1), :] = row[:, 0:128]
        turn[pl.ds(order[i] + 64, 1), :] = row[:, 128:256]
    turned = turn[...].T
    pieces_a = [
        turned[16 * q : 16 * q + 16] + pltpu.roll(turned[64 + 16 * q : 80 + 16 * q], 32, 1)
        for q in range(4)
    ]
    turn[...] = jnp.zeros((128, 128), F32)
    turn[0:32, :] = grad_b[:, 0:128]
    turn[32:64, :] = grad_b[:, 128:256]
    turned = turn[...].T
    pieces_b = [
        turned[32 * q : 32 * q + 16] + pltpu.roll(turned[32 * q + 16 : 32 * q + 32], 64, 1)
        for q in range(4)
    ]
    out_ref[:, 0:16, :] = grad_c.reshape(16, 16, 256)
    for p in range(16):
        fill_slot(out_ref, p, jnp.where(x == p // 4, pieces_a[p % 4], pieces_b[p // 4]))
    own_a, own_b = pieces_a[0], pieces_b[0]
    for q in range(1, 4):
        own_a = jnp.where(y == q, pieces_a[q], own_a)
        own_b = jnp.where(x == q, pieces_b[q], own_b)
    own_ref[:, 0:128] = own_a
    own_ref[:, 128:256] = own_b


def sum_xy(index, got_ref, own_ref):
    x, y = index[1], index[4]
    c = jnp.sum(got_ref[:, 0:16, :], axis=0)
    a, b = own_ref[:, 0:128], own_ref[:, 128:256]
    for q in range(4):
        a = a + jnp.where(y == q, 0.0, slot(got_ref, x * 4 + q))
        b = b + jnp.where(x == q, 0.0, slot(got_ref, q * 4 + y))
    return c, a, b


def middle_total(index, got_ref, own_ref, c_ref, ab_ref):
    c_ref[...], ab_ref[:, 0:128], ab_ref[:, 128:256] = sum_xy(index, got_ref, own_ref)


def middle_pack(index, c_ref, ab_ref, other_ref, out_ref, sum_ref):
    ab = ab_ref[...] + other_ref[...]
    sum_ref[...] = ab
    for p in range(8):
        out_ref[p, 0:16, :] = c_ref[...]
        fill_slot(out_ref, p, jnp.where(index[0] == p // 4, ab[:, 0:128], ab[:, 128:256]))


def middle_update(rates, index, got_ref, own_ref, block_ref, slip_ref, block_out, out_ref, new):
    zl, zh = index[0], index[3]
    rate_a, rate_b, rate_c = rates
    c = jnp.sum(got_ref[:, 0:16, :], axis=0)
    a = own_ref[:, 0:128]
    for q in range(4):
        a = a + jnp.where(zh == q, 0.0, slot(got_ref, zl * 4 + q))
    b = own_ref[:, 128:256] + slot(got_ref, (1 - zl) * 4 + zh)
    new[0:16, :] = block_ref[0:16, :] - rate_c * c
    new[16:32, 0:128] = block_ref[16:32, 0:128] - rate_a * a
    new[16:32, 128:256] = block_ref[16:32, 128:256] - rate_b * b
    block = new[...]
    block_out[...] = block
    send_block(block, out_ref, index[1])
    own = index[0] * 4 + index[3]
    c = jnp.zeros((2, 256), F32)
    ab = jnp.zeros((16, 128), F32)
    for p in range(8):
        c_p, ab_p = slip_of(block, p, p // 4, p % 4)
        c = jnp.where(own == p, c_p, c)
        ab = jnp.where(own == p, ab_p, ab)
    slip_ref[0:8, :] = jnp.zeros((8, 128), F32)
    slip_ref[0:2, :] = c[:, 0:128]
    slip_ref[2:4, :] = c[:, 128:256]
    slip_ref[8:24, :] = ab


def last_pack(index, got_ref, own_ref, out_ref, new):
    c, a, b = sum_xy(index, got_ref, own_ref)
    new[0:16, :] = c
    new[16:32, 0:128] = a
    new[16:32, 128:256] = b
    block = new[...]
    for p in range(8):
        c_p, ab_p = slip_of(block, p, p // 4, p % 4)
        out_ref[p, 0:8, :] = jnp.zeros((8, 128), F32)
        out_ref[p, 0:2, :] = c_p[:, 0:128]
        out_ref[p, 2:4, :] = c_p[:, 128:256]
        out_ref[p, 8:24, :] = ab_p


def last_sum(index, got_ref, slip_ref):
    zl, zh = index[0], index[3]
    c = got_ref[0, 0:8, :]
    for p in range(1, 8):
        c = c + got_ref[p, 0:8, :]
    a = got_ref[zl * 4, 8:24, :]
    for q in range(1, 4):
        a = a + got_ref[zl * 4 + q, 8:24, :]
    b = got_ref[zh, 8:24, :] + got_ref[4 + zh, 8:24, :]
    slip_ref[0:8, :] = c
    slip_ref[8:24, :] = jnp.where(lanes() < 32, a, b)


def last_update(rates, index, old_ref, grad_ref, other_ref, a_ref, bt_ref, c_ref, pad):
    rate_a, rate_b, rate_c = rates
    core = index[2]
    c = old_ref[0:8, :] - rate_c * grad_ref[0:8, :]
    c_ref[:, 0:128] = c[0:2, :]
    c_ref[:, 128:256] = c[2:4, :]
    rate = jnp.where(lanes() < 32, rate_a, rate_b)
    ab = old_ref[8:24, :] - rate * (grad_ref[8:24, :] + other_ref[8:24, :])
    b = jnp.where(core == 0, pltpu.roll(ab, 96, 1), pltpu.roll(ab, 32, 1))
    bt_ref[...] = b[:, 0:32]
    pad[...] = jnp.zeros((128, 128), F32)
    pad[0:16, :] = jnp.where(core == 0, ab, pltpu.roll(ab, 112, 1))
    turned = pad[...].T
    a_ref[...] = turned[0:12, 0:16]


def arrange(index, after_ref, own_ref, other_ref, kept_ref, came_ref):
    del after_ref
    spot = lax.broadcasted_iota(jnp.int32, (512, 256), 1)
    xs, ys = spot // 64, (spot // 16) % 4
    zls, zhs, us = (spot // 8) % 2, (spot // 2) % 4, spot % 2
    source = zls * 256 + xs * 64 + index[2] * 32 + zhs * 8 + ys * 2 + us
    here = lax.broadcasted_iota(jnp.int32, (512, 256), 0)
    pick = jnp.where(here == source, 1.0, 0.0).astype(jnp.bfloat16)
    for from_ref, to_ref in ((own_ref, kept_ref), (other_ref, came_ref)):
        rest = from_ref[...]
        total = jnp.zeros((384, 256), F32)
        for _ in range(3):
            part = rest.astype(jnp.bfloat16)
            rest = rest - part.astype(F32)
            total = total + jnp.dot(part, pick, preferred_element_type=F32)
        to_ref[...] = total


def per_device(tensor, first_factor, second_factor, third_factor):
    n_i, n_j, depth = tensor.shape
    size_i, size_j = n_i * 16, n_j * 16
    rates = tuple(4.0 / float(n) ** 0.5 for n in (size_j * depth, size_i * depth, size_i * size_j))
    wide = (16, 24, 256)
    square, pair = (128, 128), (16, 256)

    flat = tensor.reshape(-1, depth)
    arguments = (first_factor, 16), (second_factor.T, 16), (third_factor, 8)
    shards = jnp.concatenate(
        [jnp.pad(v, ((0, n - v.shape[0]), (0, 256 - v.shape[1]))) for v, n in arguments]
    )
    shards_other = swap(shards)
    flat, shards_other = lax.optimization_barrier((flat, shards_other))
    flat_other = swap(flat)
    send, done = call(
        first_pack, [(8, 24, 128), (16, 128)], [square], shards, shards_other
    )
    targets = call(arrange, [(384, 256), (384, 256)], [], done, flat, flat_other)
    got, targets = lax.optimization_barrier((exchange(send, Z), targets))
    block, send = call(block_from_slips, [(32, 256), wide], [], got)
    step = functools.partial(
        call, gradients, [wide, pair], [square, (768, 256), (768, 256), (32, 256)]
    )

    send, own = step(exchange(send, XY), block, *targets)
    total_c, total_ab = call(middle_total, [pair, pair], [], exchange(send, XY), own)
    send, own = call(
        middle_pack, [(8, 24, 256), pair], [], total_c, total_ab, swap(total_ab)
    )
    slip, block, send = call(
        functools.partial(middle_update, rates),
        [(24, 128), (32, 256), wide],
        [(32, 256)],
        exchange(send, Z),
        own,
        block,
    )
    send, own = step(exchange(send, XY), block, *targets)
    (send,) = call(last_pack, [(8, 24, 128)], [(32, 256)], exchange(send, XY), own)
    (grad,) = call(last_sum, [(24, 128)], [], exchange(send, Z))
    new_a, new_bt, new_c = call(
        functools.partial(last_update, rates),
        [(n_i, 16), (16, n_j), third_factor.shape],
        [square],
        slip,
        grad,
        swap(grad),
    )
    return (new_a, new_bt.T, new_c)


def solution(mesh):
    fine = Mesh(mesh.devices.reshape(2, 4, 2, 4, 4), ("zl", "x", "core", "zh", "y"))
    rows, cols = ("zl", "x", "core"), ("zh", "y")
    in_specs = (P(rows, cols, None), P(rows, cols), P(cols, rows), P(rows + cols, None))
    out_specs = (P(rows, cols), P(cols, rows), P(rows + cols, None))
    return jax.shard_map(
        per_device, mesh=fine, in_specs=in_specs, out_specs=out_specs, check_vma=False
    )
```

```python
import functools

import jax
import jax.numpy as jnp
from jax import lax
from jax.experimental import pallas as pl
from jax.experimental.pallas import tpu as pltpu
from jax.sharding import Mesh, PartitionSpec as P

XY = ("x", "y")
Z = ("zl", "zh")
HIGH = lax.Precision.HIGHEST
F32 = jnp.float32


def exchange(parts, axis):
    shape = parts.shape
    got = lax.all_to_all(parts.reshape(-1, shape[2]), axis, 0, 0, tiled=True)
    return got.reshape(shape)


def swap(value):
    return lax.ppermute(value, "core", [(0, 1), (1, 0)])


def call(body, outs, scratch, *operands):
    def kernel(*refs):
        body([lax.axis_index(n) for n in ("zl", "x", "core", "zh", "y")], *refs)

    vmem = pl.BlockSpec(memory_space=pltpu.VMEM)
    return pl.pallas_call(
        kernel,
        out_shape=[jax.ShapeDtypeStruct(s, F32) for s in outs],
        in_specs=[vmem] * len(operands),
        out_specs=[vmem] * len(outs),
        scratch_shapes=[pltpu.VMEM(s, F32) for s in scratch],
        compiler_params=pltpu.CompilerParams(vmem_limit_bytes=40 * 1024 * 1024),
    )(*operands)


def lanes(rows=16):
    return lax.broadcasted_iota(jnp.int32, (rows, 128), 1)


def split(value):
    top = value.astype(jnp.bfloat16)
    return top, (value - top.astype(F32)).astype(jnp.bfloat16)


def product(left, right, dims):
    (lt, lb), (rt, rb) = left, right
    dot = functools.partial(
        lax.dot_general, dimension_numbers=(dims, ((), ())), preferred_element_type=F32
    )
    return dot(lt, rt) + (dot(lt, rb) + dot(lb, rt))


def fill_slot(ref, p, value):
    ref[p, 16:24, 0:128] = value[0:8]
    ref[p, 16:24, 128:256] = value[8:16]


def slot(ref, p):
    v = ref[p, 16:24, :]
    return jnp.concatenate([v[:, 0:128], v[:, 128:256]], axis=0)


def send_block(block, out_ref, x):
    for p in range(16):
        out_ref[p, 0:16, :] = block[0:16]
        fill_slot(out_ref, p, jnp.where(x == p // 4, block[16:32, 0:128], block[16:32, 128:256]))


def slip_of(block, place, zl, zh):
    a = block[16:32, 0:128]
    b = block[16:32, 128:256]
    if zh:
        a = pltpu.roll(a, 128 - 32 * zh, 1)
    if not zl:
        b = pltpu.roll(b, 32, 1)
    at = lanes()
    second = (at // 32) % 2 == 1
    ab = jnp.where(at < 32, a, jnp.where(second, b, 0.0))
    c = block[2 * place : 2 * place + 2, :]
    return c, ab


def first_pack(index, own_ref, other_ref, out_ref, pad):
    even = index[2] == 0
    own, other = own_ref[0:32, 0:128], other_ref[0:32, 0:128]
    low, high = jnp.where(even, own, other), jnp.where(even, other, own)
    pad[...] = jnp.zeros((128, 128), F32)
    pad[0:16, :] = low[0:16]
    pad[16:32, :] = high[0:16]
    ab = pad[...].T[0:16, :] + pltpu.roll(low[16:32], 32, 1) + pltpu.roll(high[16:32], 96, 1)
    for p in range(8):
        out_ref[p, 0:8, :] = jnp.zeros((8, 128), F32)
        out_ref[p, 0:2, :] = own_ref[32:34, 0:128]
        out_ref[p, 2:4, :] = own_ref[32:34, 128:256]
        out_ref[p, 8:24, :] = ab


def block_from_slips(index, got_ref, block_ref, out_ref):
    zl, zh = index[0], index[3]
    for p in range(8):
        block_ref[2 * p : 2 * p + 2, 0:128] = got_ref[p, 0:2, :]
        block_ref[2 * p : 2 * p + 2, 128:256] = got_ref[p, 2:4, :]
    at = lanes()
    a = jnp.zeros((16, 128), F32)
    for q in range(4):
        v = jnp.where(at < 32, got_ref[zl * 4 + q, 8:24, :], 0.0)
        a = a + (pltpu.roll(v, 32 * q, 1) if q else v)
    second = (at // 32) % 2 == 1
    low = jnp.where(second, got_ref[zh, 8:24, :], 0.0)
    high = jnp.where(second, got_ref[4 + zh, 8:24, :], 0.0)
    block_ref[16:32, 0:128] = a
    block_ref[16:32, 128:256] = pltpu.roll(low, 96, 1) + high
    send_block(block_ref[...], out_ref, index[1])


def gradients(
    index, got_ref, block_ref, kept_ref, came_ref, out_ref, own_ref, turn, khatri, terms, first
):
    x, core, y = index[1], index[2], index[4]
    order = [i + 16 * core if i < 12 else i + 4 - 16 * core for i in range(24)]
    for q in range(4):
        v = jnp.where(y == q, block_ref[16:32, 0:128], slot(got_ref, x * 4 + q))
        turn[16 * q : 16 * q + 16, :] = v
        turn[64 + 16 * q : 80 + 16 * q, :] = pltpu.roll(v, 96, 1)
    turned = turn[...].T
    first[:, 0:128] = turned[0:32]
    first[:, 128:256] = turned[64:96]
    a = [first[pl.ds(i, 1), :] for i in order]
    for q in range(4):
        v = jnp.where(x == q, block_ref[16:32, 128:256], slot(got_ref, q * 4 + y))
        turn[32 * q : 32 * q + 16, :] = v
        turn[32 * q + 16 : 32 * q + 32, :] = pltpu.roll(v, 64, 1)
    turned = turn[...].T
    b = jnp.concatenate([turned[0:32], turned[32:64]], axis=1)
    for i in range(24):
        khatri[32 * i : 32 * i + 32, :] = a[i] * b
    c = got_ref[:, 0:16, :].reshape(256, 256)
    c, turned_c = split(c), split(c.T)
    parts = split(khatri[...])
    model = product(parts, turned_c, ((1,), (0,)))
    target = jnp.concatenate([kept_ref[...], came_ref[...]], axis=0)
    deriv = split(jax.nn.sigmoid(model) - target)
    terms[...] = product(deriv, c, ((1,), (0,)))
    grad_c = product(deriv, parts, ((0,), (0,)))
    grad_b = jnp.zeros((32, 256), F32)
    turn[...] = jnp.zeros((128, 128), F32)
    for i in range(24):
        term = terms[32 * i : 32 * i + 32, :]
        grad_b = grad_b + term * a[i]
        row = jnp.sum(term * b, axis=0, keepdims=True)
        turn[pl.ds(order[i], 1), :] = row[:, 0:128]
        turn[pl.ds(order[i] + 64, 1), :] = row[:, 128:256]
    turned = turn[...].T
    pieces_a = [
        turned[16 * q : 16 * q + 16] + pltpu.roll(turned[64 + 16 * q : 80 + 16 * q], 32, 1)
        for q in range(4)
    ]
    turn[...] = jnp.zeros((128, 128), F32)
    turn[0:32, :] = grad_b[:, 0:128]
    turn[32:64, :] = grad_b[:, 128:256]
    turned = turn[...].T
    pieces_b = [
        turned[32 * q : 32 * q + 16] + pltpu.roll(turned[32 * q + 16 : 32 * q + 32], 64, 1)
        for q in range(4)
    ]
    out_ref[:, 0:16, :] = grad_c.reshape(16, 16, 256)
    for p in range(16):
        fill_slot(out_ref, p, jnp.where(x == p // 4, pieces_a[p % 4], pieces_b[p // 4]))
    own_a, own_b = pieces_a[0], pieces_b[0]
    for q in range(1, 4):
        own_a = jnp.where(y == q, pieces_a[q], own_a)
        own_b = jnp.where(x == q, pieces_b[q], own_b)
    own_ref[:, 0:128] = own_a
    own_ref[:, 128:256] = own_b


def sum_xy(index, got_ref, own_ref):
    x, y = index[1], index[4]
    c = jnp.sum(got_ref[:, 0:16, :], axis=0)
    a, b = own_ref[:, 0:128], own_ref[:, 128:256]
    for q in range(4):
        a = a + jnp.where(y == q, 0.0, slot(got_ref, x * 4 + q))
        b = b + jnp.where(x == q, 0.0, slot(got_ref, q * 4 + y))
    return c, a, b


def middle_pack(index, got_ref, own_ref, out_ref, sum_ref):
    c, a, b = sum_xy(index, got_ref, own_ref)
    for p in range(8):
        out_ref[p, 0:16, :] = c
        fill_slot(out_ref, p, jnp.where(index[0] == p // 4, a, b))
    sum_ref[:, 0:128] = a
    sum_ref[:, 128:256] = b


def middle_sum(index, got_ref, own_ref, c_ref, ab_ref):
    zl, zh = index[0], index[3]
    c_ref[...] = jnp.sum(got_ref[:, 0:16, :], axis=0)
    a = own_ref[:, 0:128]
    for q in range(4):
        a = a + jnp.where(zh == q, 0.0, slot(got_ref, zl * 4 + q))
    ab_ref[:, 0:128] = a
    ab_ref[:, 128:256] = own_ref[:, 128:256] + slot(got_ref, (1 - zl) * 4 + zh)


def middle_update(rates, index, block_ref, c_ref, ab_ref, other_ref, slip_ref, block_out, out_ref, new):
    rate_a, rate_b, rate_c = rates
    ab = ab_ref[...] + other_ref[...]
    new[0:16, :] = block_ref[0:16, :] - rate_c * c_ref[...]
    new[16:32, 0:128] = block_ref[16:32, 0:128] - rate_a * ab[:, 0:128]
    new[16:32, 128:256] = block_ref[16:32, 128:256] - rate_b * ab[:, 128:256]
    block = new[...]
    block_out[...] = block
    send_block(block, out_ref, index[1])
    own = index[0] * 4 + index[3]
    c = jnp.zeros((2, 256), F32)
    ab = jnp.zeros((16, 128), F32)
    for p in range(8):
        c_p, ab_p = slip_of(block, p, p // 4, p % 4)
        c = jnp.where(own == p, c_p, c)
        ab = jnp.where(own == p, ab_p, ab)
    slip_ref[0:8, :] = jnp.zeros((8, 128), F32)
    slip_ref[0:2, :] = c[:, 0:128]
    slip_ref[2:4, :] = c[:, 128:256]
    slip_ref[8:24, :] = ab


def last_pack(index, got_ref, own_ref, out_ref, new):
    c, a, b = sum_xy(index, got_ref, own_ref)
    new[0:16, :] = c
    new[16:32, 0:128] = a
    new[16:32, 128:256] = b
    block = new[...]
    for p in range(8):
        c_p, ab_p = slip_of(block, p, p // 4, p % 4)
        out_ref[p, 0:8, :] = jnp.zeros((8, 128), F32)
        out_ref[p, 0:2, :] = c_p[:, 0:128]
        out_ref[p, 2:4, :] = c_p[:, 128:256]
        out_ref[p, 8:24, :] = ab_p


def last_sum(index, got_ref, slip_ref):
    zl, zh = index[0], index[3]
    c = got_ref[0, 0:8, :]
    for p in range(1, 8):
        c = c + got_ref[p, 0:8, :]
    a = got_ref[zl * 4, 8:24, :]
    for q in range(1, 4):
        a = a + got_ref[zl * 4 + q, 8:24, :]
    b = got_ref[zh, 8:24, :] + got_ref[4 + zh, 8:24, :]
    slip_ref[0:8, :] = c
    slip_ref[8:24, :] = jnp.where(lanes() < 32, a, b)


def last_update(rates, index, old_ref, grad_ref, other_ref, a_ref, bt_ref, c_ref, pad):
    rate_a, rate_b, rate_c = rates
    core = index[2]
    c = old_ref[0:8, :] - rate_c * grad_ref[0:8, :]
    c_ref[:, 0:128] = c[0:2, :]
    c_ref[:, 128:256] = c[2:4, :]
    rate = jnp.where(lanes() < 32, rate_a, rate_b)
    ab = old_ref[8:24, :] - rate * (grad_ref[8:24, :] + other_ref[8:24, :])
    b = jnp.where(core == 0, pltpu.roll(ab, 96, 1), pltpu.roll(ab, 32, 1))
    bt_ref[...] = b[:, 0:32]
    pad[...] = jnp.zeros((128, 128), F32)
    pad[0:16, :] = jnp.where(core == 0, ab, pltpu.roll(ab, 112, 1))
    turned = pad[...].T
    a_ref[...] = turned[0:12, 0:16]


def arrange(flat_ref, kept_ref, sent_ref):
    spot = lax.broadcasted_iota(jnp.int32, (512, 256), 1)
    xs, ys = spot // 64, (spot // 16) % 4
    zls, zhs, us = (spot // 8) % 2, (spot // 2) % 4, spot % 2
    source = zls * 256 + xs * 64 + zhs * 8 + ys * 2 + us
    gap = lax.broadcasted_iota(jnp.int32, (512, 256), 0) - source
    core = lax.axis_index("core")
    own, other = core * 32, 32 - core * 32
    picks = [jnp.where(gap == n, 1.0, 0.0).astype(jnp.bfloat16) for n in (own, other)]
    totals = [jnp.zeros((128, 256), F32)] * 2
    rest = flat_ref[...]
    for _ in range(3):
        part = rest.astype(jnp.bfloat16)
        rest = rest - part.astype(F32)
        totals = [
            t + jnp.dot(part, pick, preferred_element_type=F32) for t, pick in zip(totals, picks)
        ]
    kept_ref[...], sent_ref[...] = totals


def per_device(tensor, first_factor, second_factor, third_factor):
    n_i, n_j, depth = tensor.shape
    size_i, size_j = n_i * 16, n_j * 16
    rates = tuple(4.0 / float(n) ** 0.5 for n in (size_j * depth, size_i * depth, size_i * size_j))
    wide = (16, 24, 256)
    square, pair = (128, 128), (16, 256)

    flat = tensor.reshape(-1, depth)
    arguments = (first_factor, 16), (second_factor.T, 16), (third_factor, 8)
    shards = jnp.concatenate(
        [jnp.pad(v, ((0, n - v.shape[0]), (0, 256 - v.shape[1]))) for v, n in arguments]
    )
    kept, sent = pl.pallas_call(
        arrange,
        grid=(3,),
        in_specs=[pl.BlockSpec((128, depth), lambda i: (i, 0))],
        out_specs=[pl.BlockSpec((128, depth // 2), lambda i: (i, 0))] * 2,
        out_shape=[jax.ShapeDtypeStruct((384, depth // 2), F32)] * 2,
        compiler_params=pltpu.CompilerParams(vmem_limit_bytes=62_800_000),
    )(flat)
    sent, shards_other = lax.optimization_barrier((sent, swap(shards)))
    came = swap(sent)
    (send,) = call(first_pack, [(8, 24, 128)], [square], shards, shards_other)
    got, came = lax.optimization_barrier((exchange(send, Z), came))
    targets = kept, came
    block, send = call(block_from_slips, [(32, 256), wide], [], got)
    step = functools.partial(
        call, gradients, [wide, pair], [square, (768, 256), (768, 256), (32, 256)]
    )

    send, own = step(exchange(send, XY), block, *targets)
    send, own = call(middle_pack, [(8, 24, 256), pair], [], exchange(send, XY), own)
    grad_c, grad_ab = call(middle_sum, [pair, pair], [], exchange(send, Z), own)
    slip, block, send = call(
        functools.partial(middle_update, rates),
        [(24, 128), (32, 256), wide],
        [(32, 256)],
        block,
        grad_c,
        grad_ab,
        swap(grad_ab),
    )
    send, own = step(exchange(send, XY), block, *targets)
    (send,) = call(last_pack, [(8, 24, 128)], [(32, 256)], exchange(send, XY), own)
    (grad,) = call(last_sum, [(24, 128)], [], exchange(send, Z))
    new_a, new_bt, new_c = call(
        functools.partial(last_update, rates),
        [(n_i, 16), (16, n_j), third_factor.shape],
        [square],
        slip,
        grad,
        swap(grad),
    )
    return (new_a, new_bt.T, new_c)


def solution(mesh):
    fine = Mesh(mesh.devices.reshape(2, 4, 2, 4, 4), ("zl", "x", "core", "zh", "y"))
    rows, cols = ("zl", "x", "core"), ("zh", "y")
    in_specs = (P(rows, cols, None), P(rows, cols), P(cols, rows), P(rows + cols, None))
    out_specs = (P(rows, cols), P(cols, rows), P(rows + cols, None))
    return jax.shard_map(
        per_device, mesh=fine, in_specs=in_specs, out_specs=out_specs, check_vma=False
    )
```

```python
import functools

import jax
import jax.numpy as jnp
from jax import lax
from jax.experimental import pallas as pl
from jax.experimental.pallas import tpu as pltpu
from jax.sharding import Mesh, PartitionSpec as P

XY = ("x", "y")
Z = ("zl", "zh")
HIGH = lax.Precision.HIGHEST
F32 = jnp.float32


def exchange(parts, axis):
    shape = parts.shape
    got = lax.all_to_all(parts.reshape(-1, shape[2]), axis, 0, 0, tiled=True)
    return got.reshape(shape)


def swap(value):
    return lax.ppermute(value, "core", [(0, 1), (1, 0)])


def call(body, outs, scratch, *operands):
    def kernel(*refs):
        body([lax.axis_index(n) for n in ("zl", "x", "core", "zh", "y")], *refs)

    vmem = pl.BlockSpec(memory_space=pltpu.VMEM)
    return pl.pallas_call(
        kernel,
        out_shape=[jax.ShapeDtypeStruct(s, F32) for s in outs],
        in_specs=[vmem] * len(operands),
        out_specs=[vmem] * len(outs),
        scratch_shapes=[pltpu.VMEM(s, F32) for s in scratch],
        compiler_params=pltpu.CompilerParams(vmem_limit_bytes=40 * 1024 * 1024),
    )(*operands)


def lanes(rows=16):
    return lax.broadcasted_iota(jnp.int32, (rows, 128), 1)


def split(value):
    top = value.astype(jnp.bfloat16)
    return top, (value - top.astype(F32)).astype(jnp.bfloat16)


def product(left, right, dims):
    (lt, lb), (rt, rb) = left, right
    dot = functools.partial(
        lax.dot_general, dimension_numbers=(dims, ((), ())), preferred_element_type=F32
    )
    return dot(lt, rt) + (dot(lt, rb) + dot(lb, rt))


def fill_slot(ref, p, value):
    ref[p, 16:24, 0:128] = value[0:8]
    ref[p, 16:24, 128:256] = value[8:16]


def slot(ref, p):
    v = ref[p, 16:24, :]
    return jnp.concatenate([v[:, 0:128], v[:, 128:256]], axis=0)


def send_block(block, out_ref, x):
    for p in range(16):
        out_ref[p, 0:16, :] = block[0:16]
        fill_slot(out_ref, p, jnp.where(x == p // 4, block[16:32, 0:128], block[16:32, 128:256]))


def slip_of(block, place, zl, zh):
    a = block[16:32, 0:128]
    b = block[16:32, 128:256]
    if zh:
        a = pltpu.roll(a, 128 - 32 * zh, 1)
    if not zl:
        b = pltpu.roll(b, 32, 1)
    at = lanes()
    second = (at // 32) % 2 == 1
    ab = jnp.where(at < 32, a, jnp.where(second, b, 0.0))
    c = block[2 * place : 2 * place + 2, :]
    return c, ab


def first_pack(index, own_ref, other_ref, out_ref, pad):
    even = index[2] == 0
    own, other = own_ref[0:32, 0:128], other_ref[0:32, 0:128]
    low, high = jnp.where(even, own, other), jnp.where(even, other, own)
    pad[...] = jnp.zeros((128, 128), F32)
    pad[0:16, :] = low[0:16]
    pad[16:32, :] = high[0:16]
    ab = pad[...].T[0:16, :] + pltpu.roll(low[16:32], 32, 1) + pltpu.roll(high[16:32], 96, 1)
    for p in range(8):
        out_ref[p, 0:8, :] = jnp.zeros((8, 128), F32)
        out_ref[p, 0:2, :] = own_ref[32:34, 0:128]
        out_ref[p, 2:4, :] = own_ref[32:34, 128:256]
        out_ref[p, 8:24, :] = ab


def block_from_slips(index, got_ref, block_ref, out_ref):
    zl, zh = index[0], index[3]
    for p in range(8):
        block_ref[2 * p : 2 * p + 2, 0:128] = got_ref[p, 0:2, :]
        block_ref[2 * p : 2 * p + 2, 128:256] = got_ref[p, 2:4, :]
    at = lanes()
    a = jnp.zeros((16, 128), F32)
    for q in range(4):
        v = jnp.where(at < 32, got_ref[zl * 4 + q, 8:24, :], 0.0)
        a = a + (pltpu.roll(v, 32 * q, 1) if q else v)
    second = (at // 32) % 2 == 1
    low = jnp.where(second, got_ref[zh, 8:24, :], 0.0)
    high = jnp.where(second, got_ref[4 + zh, 8:24, :], 0.0)
    block_ref[16:32, 0:128] = a
    block_ref[16:32, 128:256] = pltpu.roll(low, 96, 1) + high
    send_block(block_ref[...], out_ref, index[1])


def gradients(
    index, got_ref, block_ref, kept_ref, came_ref, out_ref, own_ref, turn, khatri, terms, first
):
    x, core, y = index[1], index[2], index[4]
    order = [i + 16 * core if i < 12 else i + 4 - 16 * core for i in range(24)]
    for q in range(4):
        v = jnp.where(y == q, block_ref[16:32, 0:128], slot(got_ref, x * 4 + q))
        turn[16 * q : 16 * q + 16, :] = v
        turn[64 + 16 * q : 80 + 16 * q, :] = pltpu.roll(v, 96, 1)
    turned = turn[...].T
    first[:, 0:128] = turned[0:32]
    first[:, 128:256] = turned[64:96]
    a = [first[pl.ds(i, 1), :] for i in order]
    for q in range(4):
        v = jnp.where(x == q, block_ref[16:32, 128:256], slot(got_ref, q * 4 + y))
        turn[32 * q : 32 * q + 16, :] = v
        turn[32 * q + 16 : 32 * q + 32, :] = pltpu.roll(v, 64, 1)
    turned = turn[...].T
    b = jnp.concatenate([turned[0:32], turned[32:64]], axis=1)
    for i in range(24):
        khatri[32 * i : 32 * i + 32, :] = a[i] * b
    c = got_ref[:, 0:16, :].reshape(256, 256)
    c, turned_c = split(c), split(c.T)
    parts = split(khatri[...])
    model = product(parts, turned_c, ((1,), (0,)))
    target = jnp.concatenate([kept_ref[...], came_ref[...]], axis=0)
    deriv = split(jax.nn.sigmoid(model) - target)
    terms[...] = product(deriv, c, ((1,), (0,)))
    grad_c = product(deriv, parts, ((0,), (0,)))
    grad_b = jnp.zeros((32, 256), F32)
    turn[...] = jnp.zeros((128, 128), F32)
    for i in range(24):
        term = terms[32 * i : 32 * i + 32, :]
        grad_b = grad_b + term * a[i]
        row = jnp.sum(term * b, axis=0, keepdims=True)
        turn[pl.ds(order[i], 1), :] = row[:, 0:128]
        turn[pl.ds(order[i] + 64, 1), :] = row[:, 128:256]
    turned = turn[...].T
    pieces_a = [
        turned[16 * q : 16 * q + 16] + pltpu.roll(turned[64 + 16 * q : 80 + 16 * q], 32, 1)
        for q in range(4)
    ]
    turn[...] = jnp.zeros((128, 128), F32)
    turn[0:32, :] = grad_b[:, 0:128]
    turn[32:64, :] = grad_b[:, 128:256]
    turned = turn[...].T
    pieces_b = [
        turned[32 * q : 32 * q + 16] + pltpu.roll(turned[32 * q + 16 : 32 * q + 32], 64, 1)
        for q in range(4)
    ]
    out_ref[:, 0:16, :] = grad_c.reshape(16, 16, 256)
    for p in range(16):
        fill_slot(out_ref, p, jnp.where(x == p // 4, pieces_a[p % 4], pieces_b[p // 4]))
    own_a, own_b = pieces_a[0], pieces_b[0]
    for q in range(1, 4):
        own_a = jnp.where(y == q, pieces_a[q], own_a)
        own_b = jnp.where(x == q, pieces_b[q], own_b)
    own_ref[:, 0:128] = own_a
    own_ref[:, 128:256] = own_b


def sum_xy(index, got_ref, own_ref):
    x, y = index[1], index[4]
    c = jnp.sum(got_ref[:, 0:16, :], axis=0)
    a, b = own_ref[:, 0:128], own_ref[:, 128:256]
    for q in range(4):
        a = a + jnp.where(y == q, 0.0, slot(got_ref, x * 4 + q))
        b = b + jnp.where(x == q, 0.0, slot(got_ref, q * 4 + y))
    return c, a, b


def middle_pack(index, got_ref, own_ref, out_ref, sum_ref):
    c, a, b = sum_xy(index, got_ref, own_ref)
    for p in range(8):
        out_ref[p, 0:16, :] = c
        fill_slot(out_ref, p, jnp.where(index[0] == p // 4, a, b))
    sum_ref[:, 0:128] = a
    sum_ref[:, 128:256] = b


def middle_sum(index, got_ref, own_ref, c_ref, ab_ref):
    zl, zh = index[0], index[3]
    c_ref[...] = jnp.sum(got_ref[:, 0:16, :], axis=0)
    a = own_ref[:, 0:128]
    for q in range(4):
        a = a + jnp.where(zh == q, 0.0, slot(got_ref, zl * 4 + q))
    ab_ref[:, 0:128] = a
    ab_ref[:, 128:256] = own_ref[:, 128:256] + slot(got_ref, (1 - zl) * 4 + zh)


def middle_update(rates, index, block_ref, c_ref, ab_ref, other_ref, slip_ref, block_out, out_ref, new):
    rate_a, rate_b, rate_c = rates
    ab = ab_ref[...] + other_ref[...]
    new[0:16, :] = block_ref[0:16, :] - rate_c * c_ref[...]
    new[16:32, 0:128] = block_ref[16:32, 0:128] - rate_a * ab[:, 0:128]
    new[16:32, 128:256] = block_ref[16:32, 128:256] - rate_b * ab[:, 128:256]
    block = new[...]
    block_out[...] = block
    send_block(block, out_ref, index[1])
    own = index[0] * 4 + index[3]
    c = jnp.zeros((2, 256), F32)
    ab = jnp.zeros((16, 128), F32)
    for p in range(8):
        c_p, ab_p = slip_of(block, p, p // 4, p % 4)
        c = jnp.where(own == p, c_p, c)
        ab = jnp.where(own == p, ab_p, ab)
    slip_ref[0:8, :] = jnp.zeros((8, 128), F32)
    slip_ref[0:2, :] = c[:, 0:128]
    slip_ref[2:4, :] = c[:, 128:256]
    slip_ref[8:24, :] = ab


def last_pack(index, got_ref, own_ref, out_ref, new):
    c, a, b = sum_xy(index, got_ref, own_ref)
    new[0:16, :] = c
    new[16:32, 0:128] = a
    new[16:32, 128:256] = b
    block = new[...]
    for p in range(8):
        c_p, ab_p = slip_of(block, p, p // 4, p % 4)
        out_ref[p, 0:8, :] = jnp.zeros((8, 128), F32)
        out_ref[p, 0:2, :] = c_p[:, 0:128]
        out_ref[p, 2:4, :] = c_p[:, 128:256]
        out_ref[p, 8:24, :] = ab_p


def last_sum(index, got_ref, slip_ref):
    zl, zh = index[0], index[3]
    c = got_ref[0, 0:8, :]
    for p in range(1, 8):
        c = c + got_ref[p, 0:8, :]
    a = got_ref[zl * 4, 8:24, :]
    for q in range(1, 4):
        a = a + got_ref[zl * 4 + q, 8:24, :]
    b = got_ref[zh, 8:24, :] + got_ref[4 + zh, 8:24, :]
    slip_ref[0:8, :] = c
    slip_ref[8:24, :] = jnp.where(lanes() < 32, a, b)


def last_update(rates, index, old_ref, grad_ref, other_ref, a_ref, bt_ref, c_ref, pad):
    rate_a, rate_b, rate_c = rates
    core = index[2]
    c = old_ref[0:8, :] - rate_c * grad_ref[0:8, :]
    c_ref[:, 0:128] = c[0:2, :]
    c_ref[:, 128:256] = c[2:4, :]
    rate = jnp.where(lanes() < 32, rate_a, rate_b)
    ab = old_ref[8:24, :] - rate * (grad_ref[8:24, :] + other_ref[8:24, :])
    b = jnp.where(core == 0, pltpu.roll(ab, 96, 1), pltpu.roll(ab, 32, 1))
    bt_ref[...] = b[:, 0:32]
    pad[...] = jnp.zeros((128, 128), F32)
    pad[0:16, :] = jnp.where(core == 0, ab, pltpu.roll(ab, 112, 1))
    turned = pad[...].T
    a_ref[...] = turned[0:12, 0:16]


def arrange(index, after_ref, own_ref, other_ref, kept_ref, came_ref):
    del after_ref
    spot = lax.broadcasted_iota(jnp.int32, (512, 256), 1)
    xs, ys = spot // 64, (spot // 16) % 4
    zls, zhs, us = (spot // 8) % 2, (spot // 2) % 4, spot % 2
    source = zls * 256 + xs * 64 + index[2] * 32 + zhs * 8 + ys * 2 + us
    here = lax.broadcasted_iota(jnp.int32, (512, 256), 0)
    pick = jnp.where(here == source, 1.0, 0.0).astype(jnp.bfloat16)
    for from_ref, to_ref in ((own_ref, kept_ref), (other_ref, came_ref)):
        rest = from_ref[...]
        total = jnp.zeros((384, 256), F32)
        for _ in range(3):
            part = rest.astype(jnp.bfloat16)
            rest = rest - part.astype(F32)
            total = total + jnp.dot(part, pick, preferred_element_type=F32)
        to_ref[...] = total


def per_device(tensor, first_factor, second_factor, third_factor):
    n_i, n_j, depth = tensor.shape
    size_i, size_j = n_i * 16, n_j * 16
    rates = tuple(4.0 / float(n) ** 0.5 for n in (size_j * depth, size_i * depth, size_i * size_j))
    wide = (16, 24, 256)
    square, pair = (128, 128), (16, 256)

    flat = tensor.reshape(-1, depth)
    arguments = (first_factor, 16), (second_factor.T, 16), (third_factor, 8)
    shards = jnp.concatenate(
        [jnp.pad(v, ((0, n - v.shape[0]), (0, 256 - v.shape[1]))) for v, n in arguments]
    )
    shards_other = swap(shards)
    flat, shards_other = lax.optimization_barrier((flat, shards_other))
    flat_other = swap(flat)
    (send,) = call(first_pack, [(8, 24, 128)], [square], shards, shards_other)
    block, send = call(block_from_slips, [(32, 256), wide], [], exchange(send, Z))
    targets = call(arrange, [(384, 256), (384, 256)], [], block, flat, flat_other)
    step = functools.partial(
        call, gradients, [wide, pair], [square, (768, 256), (768, 256), (32, 256)]
    )

    send, own = step(exchange(send, XY), block, *targets)
    send, own = call(middle_pack, [(8, 24, 256), pair], [], exchange(send, XY), own)
    grad_c, grad_ab = call(middle_sum, [pair, pair], [], exchange(send, Z), own)
    slip, block, send = call(
        functools.partial(middle_update, rates),
        [(24, 128), (32, 256), wide],
        [(32, 256)],
        block,
        grad_c,
        grad_ab,
        swap(grad_ab),
    )
    send, own = step(exchange(send, XY), block, *targets)
    (send,) = call(last_pack, [(8, 24, 128)], [(32, 256)], exchange(send, XY), own)
    (grad,) = call(last_sum, [(24, 128)], [], exchange(send, Z))
    new_a, new_bt, new_c = call(
        functools.partial(last_update, rates),
        [(n_i, 16), (16, n_j), third_factor.shape],
        [square],
        slip,
        grad,
        swap(grad),
    )
    return (new_a, new_bt.T, new_c)


def solution(mesh):
    fine = Mesh(mesh.devices.reshape(2, 4, 2, 4, 4), ("zl", "x", "core", "zh", "y"))
    rows, cols = ("zl", "x", "core"), ("zh", "y")
    in_specs = (P(rows, cols, None), P(rows, cols), P(cols, rows), P(rows + cols, None))
    out_specs = (P(rows, cols), P(cols, rows), P(rows + cols, None))
    return jax.shard_map(
        per_device, mesh=fine, in_specs=in_specs, out_specs=out_specs, check_vma=False
    )
```
